128 devices in a mesh: dp: 4 (over x), outer: 16 (over z, y), inner: 2 (over core).
Axes of the slice: x: 4, y: 4, z: 4, core: 2. Of those that a mesh axis runs over, the one named last changes fastest.
Arguments:
- queries: bfloat16 [4, 4096, 1024], P('dp', ('outer', 'inner')), may hold values from -6 to 6
- keys: bfloat16 [4, 4096, 2, 1024], P('dp', ('outer', 'inner')), may hold values from -6 to 6
- values: bfloat16 [4, 4096, 2, 1024], P('dp', ('outer', 'inner')), may hold values from -6 to 6
- betas: float32 [4, 8, 2, 4096], P('dp', None, None, ('outer', 'inner')), may hold values from 0.3 to 1.6
- grad_out: bfloat16 [4, 4096, 1024], P('dp', ('outer', 'inner')), may hold values from -16 to 16
- gain: float32 [1024], replicated, may hold values from 0.1 to 1.9
Outputs:
- grad_queries: bfloat16 [4, 4096, 1024], P('dp', ('outer', 'inner'))
- grad_keys: bfloat16 [4, 4096, 2, 1024], P('dp', ('outer', 'inner'))
- grad_values: bfloat16 [4, 4096, 2, 1024], P('dp', ('outer', 'inner'))
- gain_grad: float32 [1024], replicated
The draws below stay inside these ranges and needn't reach their ends.
All inputs are finite; a program needn't handle non-finite values.
Results may differ from the reference program's by a relative error of at most 0.001.
Values sent between devices are 32-bit elements; how exact they have to be, the bound alone decides.
A program may use at most 128 MiB of HBM per device.

```python
import math
import jax
import jax.numpy as jnp
from jax import lax

HEADS = 8
HEAD_DIM = 128
TOK_DEV = 128
STRETCH = 64
BATCH = 4
SEQ = 4096
N_OUTER = 16
N_INNER = 2


def draw_keys(key, part):
    seeds = [jax.random.fold_in(key, 3 + offset) for offset in range(5)]
    share = 0.5
    gradual_forgetting = jax.random.bernoulli(seeds[0], share, (BATCH, 1, 1, HEADS, 1))
    baseline_amplitude = jax.random.bernoulli(seeds[1], 0.25, (BATCH, 1, 1, HEADS, HEAD_DIM))
    beginning_shifts = jax.random.randint(seeds[2], (BATCH, 1, 1, HEADS, 3), 0, SEQ)
    position_list = lax.broadcasted_iota(jnp.int32, (1, SEQ, 1, 1, 1), 1)
    cluster_length = jnp.any((position_list >= beginning_shifts) & (position_list < beginning_shifts + 48), axis=-1, keepdims=True)
    dispersion_extent = jnp.exp(jax.random.uniform(seeds[3], (BATCH, 1, 1, HEADS, HEAD_DIM), minval=-0.7, maxval=0.7))
    tiny_perturbation = 8.0 / math.sqrt(2.0 * SEQ)
    multiplier_value = jnp.where(gradual_forgetting, jnp.where(baseline_amplitude & jnp.logical_not(cluster_length), tiny_perturbation, 1.0), dispersion_extent)
    shape = (BATCH, SEQ, 2, HEADS, HEAD_DIM)
    noise = jax.random.normal(seeds[4], shape)
    field = jnp.clip(noise * multiplier_value, -6.0, 6.0)
    return field.reshape(BATCH, SEQ, 2, HEADS * HEAD_DIM).astype(jnp.bfloat16)


def draw_grad_out(key, part):
    seeds = [jax.random.fold_in(key, 11 + offset) for offset in range(3)]
    shape = (BATCH, SEQ, HEADS * HEAD_DIM)
    position_list = (lax.broadcasted_iota(jnp.int32, (BATCH, SEQ, 1), 0) * SEQ + lax.broadcasted_iota(jnp.int32, (BATCH, SEQ, 1), 1)).astype(jnp.float32)
    ramp = 1.0 + 2.0 * position_list / (BATCH * SEQ)
    field = jax.random.normal(seeds[0], shape)
    return jnp.clip(field * ramp, -16.0, 16.0).astype(jnp.bfloat16)


def block_scale(stream_key, dims, cuts, least, largest):
    def one(dim, parts):
        heights = jax.random.uniform(jax.random.fold_in(jax.random.fold_in(stream_key, 6), dim), (parts,), jnp.float32, least / len(cuts), largest / len(cuts))
        return jnp.repeat(jnp.exp(heights), dims[dim] // parts).reshape((-1,) + (1,) * (len(dims) - dim - 1))

    level = one(*cuts[0])
    for cut in cuts[1:]:
        level = level * one(*cut)
    return level


def bell_draw(own_key, extent, spread, limit, split=(), held_as=jnp.bfloat16):
    entries = spread * jax.random.normal(own_key, extent, jnp.float32)
    if split:
        entries = entries * block_scale(own_key, extent, split, -0.22, 0.18)
    return jnp.clip(entries, -limit, limit).astype(held_as)


def setup_inputs(seed: int = 0) -> dict:
    splits = jax.random.split(jax.random.key(seed), 7)
    queries = bell_draw(splits[0], (BATCH, SEQ, HEADS * HEAD_DIM), 1.0, 6.0, ((0, 4), (1, 32)))
    keys = draw_keys(jax.random.fold_in(splits[6], 71), 0)
    values = bell_draw(splits[2], (BATCH, SEQ, 2, HEADS * HEAD_DIM), 1.0, 6.0, ((0, 4), (1, 32)))
    betas = jnp.clip(0.3 + 1.3 * jax.random.uniform(splits[3], (BATCH, HEADS, 2, SEQ), jnp.float32) ** block_scale(splits[3], (BATCH, HEADS, 2, SEQ), ((0, 4), (3, 32)), -0.2, 0.2), 0.3, 1.6)
    grad_out = draw_grad_out(jax.random.fold_in(splits[6], 71), 0)
    gain = jnp.clip(1.0 + 0.18 * jax.random.normal(splits[5], (HEADS * HEAD_DIM,), jnp.float32), 0.1, 1.9)
    return {"queries": queries, "keys": keys, "values": values, "betas": betas, "grad_out": grad_out, "gain": gain}


EXACT = lax.Precision.HIGHEST

def product(left, right):
    return jnp.dot(left, right, precision=EXACT)

def unit_rows(raw):
    return raw * lax.rsqrt(lax.optimization_barrier(jnp.sum(raw * raw, axis=-1, keepdims=True)) + 1e-06)

def block_step(state, pieces):
    query_blk, key_blk, value_blk, rate_blk = pieces
    span = query_blk.shape[0]
    refl = key_blk.shape[0]
    token_ids = lax.broadcasted_iota(jnp.int32, (span, refl), 0)
    refl_ids = lax.broadcasted_iota(jnp.int32, (span, refl), 1)
    read_mask = (refl_ids <= 2 * token_ids + 1).astype(jnp.float32)
    row_ids = lax.broadcasted_iota(jnp.int32, (refl, refl), 0)
    col_ids = lax.broadcasted_iota(jnp.int32, (refl, refl), 1)
    strict = (col_ids < row_ids).astype(jnp.float32)
    lower_mat = jnp.eye(refl, dtype=jnp.float32) + rate_blk[:, None] * product(key_blk, key_blk.T) * strict
    target = rate_blk[:, None] * (value_blk - product(key_blk, state.T))
    update = jax.scipy.linalg.solve_triangular(lower_mat, target, lower=True)
    scores = product(query_blk, key_blk.T) * read_mask
    output = product(query_blk, state.T) + product(scores, update)
    return (state + product(update.T, key_blk), output)

def segment_step(state, pieces):
    return lax.scan(jax.checkpoint(block_step), state, pieces)

def head_output(query_n, key_n, value_f, rate_f):
    segments = N_OUTER * N_INNER
    per_seg = TOK_DEV // STRETCH
    pieces = (query_n.reshape(segments, per_seg, STRETCH, HEAD_DIM), key_n.reshape(segments, per_seg, 2 * STRETCH, HEAD_DIM), value_f.reshape(segments, per_seg, 2 * STRETCH, HEAD_DIM), rate_f.reshape(segments, per_seg, 2 * STRETCH))
    start = jnp.zeros((HEAD_DIM, HEAD_DIM), jnp.float32)
    final_state, outputs = lax.scan(jax.checkpoint(segment_step), start, pieces)
    return outputs.reshape(SEQ, HEAD_DIM)

def pair_grads(index, queries, keys, values, betas, grad_out, gain):
    batch_id = (index // HEADS).astype(jnp.int32)
    head_id = (index % HEADS).astype(jnp.int32)
    zero_id = jnp.zeros((), jnp.int32)
    column = (head_id * HEAD_DIM).astype(jnp.int32)
    query_h = lax.dynamic_slice(queries, (batch_id, zero_id, column), (1, SEQ, HEAD_DIM))[0].astype(jnp.float32)
    key_h = lax.dynamic_slice(keys, (batch_id, zero_id, zero_id, column), (1, SEQ, 2, HEAD_DIM))[0].astype(jnp.float32)
    value_h = lax.dynamic_slice(values, (batch_id, zero_id, zero_id, column), (1, SEQ, 2, HEAD_DIM))[0].astype(jnp.float32)
    rate_h = lax.dynamic_slice(betas, (batch_id, head_id, zero_id, zero_id), (1, 1, 2, SEQ))[0, 0]
    cotan_h = lax.dynamic_slice(grad_out, (batch_id, zero_id, column), (1, SEQ, HEAD_DIM))[0].astype(jnp.float32)
    gain_h = lax.dynamic_slice(gain, (column,), (HEAD_DIM,))
    rate_f = rate_h.T.reshape(2 * SEQ)

    def forward(query_raw, key_raw, value_raw, gain_raw):
        query_n = unit_rows(query_raw)
        key_n = unit_rows(key_raw).reshape(2 * SEQ, HEAD_DIM)
        output = head_output(query_n, key_n, value_raw.reshape(2 * SEQ, HEAD_DIM), rate_f)
        scale_inv = lax.rsqrt(lax.optimization_barrier(jnp.mean(output * output, axis=-1, keepdims=True)) + 1e-05)
        return output * scale_inv * gain_raw[None, :]
    result, pullback = jax.vjp(forward, query_h, key_h, value_h, gain_h)
    return pullback(cotan_h)

def reference(queries, keys, values, betas, grad_out, gain):
    indices = jnp.arange(BATCH * HEADS, dtype=jnp.int32)
    grad_q, grad_k, grad_v, grad_g = lax.map(lambda index: pair_grads(index, queries, keys, values, betas, grad_out, gain), indices)
    grad_q = grad_q.reshape(BATCH, HEADS, SEQ, HEAD_DIM).transpose(0, 2, 1, 3).reshape(BATCH, SEQ, HEADS * HEAD_DIM)
    grad_k = grad_k.reshape(BATCH, HEADS, SEQ, 2, HEAD_DIM).transpose(0, 2, 3, 1, 4).reshape(BATCH, SEQ, 2, HEADS * HEAD_DIM)
    grad_v = grad_v.reshape(BATCH, HEADS, SEQ, 2, HEAD_DIM).transpose(0, 2, 3, 1, 4).reshape(BATCH, SEQ, 2, HEADS * HEAD_DIM)
    grad_g = lax.optimization_barrier(jnp.sum(grad_g.reshape(BATCH, HEADS, HEAD_DIM), axis=0)).reshape(HEADS * HEAD_DIM)
    factor = 1.0 / jnp.sqrt(jnp.float32(BATCH * SEQ))
    return (grad_q.astype(jnp.bfloat16), grad_k.astype(jnp.bfloat16), grad_v.astype(jnp.bfloat16), grad_g * factor)
```

```python
import functools
import math

import jax
import jax.numpy as jnp
from jax import lax
from jax.experimental import pallas as pl
from jax.experimental.pallas import tpu as pltpu
from jax.sharding import PartitionSpec as P

HEADS = 8
DIM = 128
HALF = 64
GROUP = 2
EPS_KEY = 1e-06
EPS_OUT = 1e-05
F32 = jnp.float32
BF16 = jnp.bfloat16
MESH = pl.DeviceIdType.MESH
VMEM = pl.BlockSpec(memory_space=pltpu.VMEM)
LIMIT = 48 * 1024 * 1024


def split(x):
    high = x.astype(BF16)
    return high, (x - high.astype(F32)).astype(BF16)


def raw_dot(left, right, dims):
    return lax.dot_general(left, right, (dims, ((), ())), preferred_element_type=F32)


def folded(wide):
    half = wide.shape[1] // 2
    return wide[:, :half] + wide[:, half:]


def nn(a, b):
    lhs = jnp.concatenate(a, axis=1)
    rhs = jnp.concatenate(b, axis=1)
    return folded(raw_dot(lhs, jnp.concatenate([rhs, rhs], axis=0), ((1,), (0,))))


def nt(a, b):
    lhs = jnp.concatenate(a, axis=1)
    rhs = jnp.concatenate(b, axis=0)
    return folded(raw_dot(lhs, jnp.concatenate([rhs, rhs], axis=1), ((1,), (1,))))


def tn(a, b):
    lhs = jnp.concatenate(a, axis=0)
    rhs = jnp.concatenate(b, axis=1)
    return folded(raw_dot(lhs, jnp.concatenate([rhs, rhs], axis=0), ((0,), (0,))))


def stacked(*pairs):
    return tuple(jnp.concatenate(part, axis=0) for part in zip(*pairs))


def beside(*pairs):
    return tuple(jnp.concatenate(part, axis=1) for part in zip(*pairs))


def inv_norm(x):
    return lax.rsqrt(jnp.sum(x * x, axis=1, keepdims=True) + EPS_KEY)


def places():
    row = lax.broadcasted_iota(jnp.int32, (DIM, DIM), 0)
    col = lax.broadcasted_iota(jnp.int32, (DIM, DIM), 1)

    def order(n):
        return jnp.where(n < HALF, 2 * n, 2 * n - (DIM - 1))

    return row, col, order(row), order(col)


def read_mask(col):
    token = lax.broadcasted_iota(jnp.int32, (HALF, DIM), 0)
    return jnp.where(col[:HALF] < HALF, col[:HALF], col[:HALF] - HALF) <= token


def rows_of(first, second, block, head):
    at = slice(block * HALF, (block + 1) * HALF)
    cols = slice(head * DIM, (head + 1) * DIM)
    return jnp.concatenate([first[at, cols], second[at, cols]], axis=0)


def tokens_of(ref, block, head):
    return ref[block * HALF : (block + 1) * HALF, head * DIM : (head + 1) * DIM]


def maps_kernel(q, k0, k1, v0, v1, rate, t_dev, o_dev, q_dev, y_dev, w_out, u_out, g_out, z_out, t_out, o_out, qe_out):
    row, col, row_at, col_at = places()
    eye = row == col
    strict = col_at < row_at
    reads = read_mask(col)
    many = [(h, b) for h in range(GROUP) for b in range(2)]
    count = len(many)
    key, val, query, ratecol, raterow = [], [], [], [], []
    for h, b in many:
        kr = rows_of(k0, k1, b, h).astype(F32)
        key.append(kr * inv_norm(kr))
        val.append(rows_of(v0, v1, b, h))
        qr = tokens_of(q, b, h).astype(F32)
        query.append(qr * inv_norm(qr))
        r = rate[h, b : b + 1, :]
        raterow.append(r)
        ratecol.append(jnp.sum(jnp.where(eye, r, 0.0), axis=1, keepdims=True))
    keys = [split(x) for x in key]
    both = [nt(stacked(keys[i], split(query[i])), keys[i]) for i in range(count)]
    lower = [split(jnp.where(strict, ratecol[i] * both[i][:DIM], 0.0)) for i in range(count)]
    scores = [split(jnp.where(reads, both[i][DIM:], 0.0)) for i in range(count)]

    def level(s):
        shift = s.bit_length() - 1
        rb, cb = row_at >> shift, col_at >> shift
        return ((rb >> 1) == (cb >> 1)) & ((rb & 1) == 1) & ((cb & 1) == 0)

    def masked(pair, mask):
        return tuple(jnp.where(mask, x.astype(F32), 0.0).astype(BF16) for x in pair)

    one = jnp.where(eye, 1.0, 0.0)
    first = level(1)
    inverse = [one - jnp.where(first, ratecol[i] * both[i][:DIM], 0.0) for i in range(count)]
    s = 2
    while s < DIM:
        mask = level(s)
        halves = [split(x) for x in inverse]
        inner = [split(nn(masked(lower[i], mask), halves[i])) for i in range(count)]
        inverse = [inverse[i] - nn(halves[i], inner[i]) for i in range(count)]
        s *= 2
    scaled = [split(inverse[i] * raterow[i]) for i in range(count)]
    zero = jnp.zeros((DIM, DIM), BF16)
    pack = [beside(keys[i], (val[i], zero)) for i in range(count)]
    solved = [nn(scaled[i], pack[i]) for i in range(count)]
    z = [nn(scores[i], scaled[i]) for i in range(count)]
    gmat = [tn(scaled[i], keys[i]) for i in range(count)]
    zr = [nn(split(z[i]), pack[i]) for i in range(count)]
    move = [tn(split(solved[i]), keys[i]) for i in range(count)]
    trans = [one - move[i][:DIM] for i in range(count)]
    offs = [move[i][DIM:] for i in range(count)]
    qe = [query[i] - zr[i][:, :DIM] for i in range(count)]
    y = [zr[i][:, DIM:] for i in range(count)]
    for i, (h, b) in enumerate(many):
        w_out[h, b] = solved[i][:, :DIM]
        u_out[h, b] = solved[i][:, DIM:]
        g_out[h, b] = gmat[i]
        z_out[h, b] = z[i]
        t_out[h, b] = trans[i]
    for h in range(GROUP):
        a, b = 2 * h, 2 * h + 1
        ta, tb = split(trans[a]), split(trans[b])
        oa, qb = split(offs[a]), split(qe[b])
        through = nn(stacked(ta, oa), tb)
        t_dev[h] = through[:DIM]
        o_dev[h] = through[DIM:] + offs[b]
        back = nt(qb, stacked(ta, oa))
        q_dev[h] = jnp.concatenate([qe[a], back[:, :DIM]], axis=0)
        y_dev[h] = jnp.concatenate([y[a], y[b] + back[:, DIM:]], axis=0)
        o_out[h] = offs[a]
        qe_out[h] = qe[b]


def shape(*dims, dtype=F32):
    return jax.ShapeDtypeStruct(dims, dtype)


def head_spec(*rest):
    return pl.BlockSpec((GROUP, *rest), lambda i: (i,) + (0,) * len(rest))


def wide_spec(offset=0):
    return pl.BlockSpec((DIM, GROUP * DIM), lambda i: (0, i + offset))


def state_maps(q, k, v, rate):
    steps = HEADS // GROUP
    square, pair, thin = (DIM, DIM), (2, DIM, DIM), (2, HALF, DIM)
    outs = [square, square, square, square, pair, pair, pair, thin, pair, square, (HALF, DIM)]
    return pl.pallas_call(
        maps_kernel,
        grid=(steps,),
        in_specs=[wide_spec(), wide_spec(), wide_spec(steps), wide_spec(), wide_spec(steps), head_spec(2, DIM)],
        out_specs=[head_spec(*s) for s in outs],
        out_shape=[shape(HEADS, *s) for s in outs],
        compiler_params=pltpu.CompilerParams(vmem_limit_bytes=LIMIT),
    )(q, k, k, v, v, rate)


def place():
    return 2 * lax.axis_index("outer") + lax.axis_index("inner")


def device(d):
    return {"outer": lax.div(d, 2), "inner": lax.rem(d, 2)}


def greet(n, others):
    barrier = pltpu.get_barrier_semaphore()
    me = place()

    def tell(i, c):
        pl.semaphore_signal(barrier, inc=1, device_id=device(lax.rem(me + i, n)), device_id_type=MESH)
        return c

    lax.fori_loop(1, n, tell, 0)
    for peer in others:
        pl.semaphore_signal(barrier, inc=1, device_id=peer, device_id_type=MESH)
    pl.semaphore_wait(barrier, n - 1 + len(others))


def to(src, dst, send, recv, target):
    return pltpu.make_async_remote_copy(
        src_ref=src, dst_ref=dst, send_sem=send, recv_sem=recv, device_id=target, device_id_type=MESH
    )


def forward_kernel(n, t_dev, o_dev, t_all, state, o_all, s_all, st, rt, so, ro, ss, rs):
    me = place()
    greet(n, ())

    def put(i, c):
        d = lax.rem(me + i, n)
        to(t_dev.at[lax.div(d, 4)], t_all.at[me], st.at[d], rt.at[me], device(d)).start()
        to(o_dev.at[d], o_all.at[me], so.at[d], ro.at[me], device(d)).start()
        return c

    lax.fori_loop(1, n, put, 0)
    t_all[me] = t_dev[lax.div(me, 4)]
    o_all[me] = o_dev[me]

    def step(p, now):
        @pl.when(p != me)
        def _():
            to(t_dev.at[0], t_all.at[p], st.at[p], rt.at[p], device(p)).wait_recv()
            to(o_dev.at[0], o_all.at[p], so.at[p], ro.at[p], device(p)).wait_recv()

        s_all[p] = now

        @pl.when(p != me)
        def _():
            to(s_all.at[p], state.at[me], ss.at[p], rs.at[me], device(p)).start()

        return nn(split(now), split(t_all[p])) + o_all[p]

    lax.fori_loop(0, n, step, jnp.zeros((DIM // 4, DIM), F32))
    state[me] = s_all[me]

    def finish(i, c):
        d = lax.rem(me + i, n)
        to(s_all.at[d], state.at[d], ss.at[d], rs.at[d], device(d)).wait()
        to(t_dev.at[0], t_all.at[d], st.at[d], rt.at[d], device(d)).wait_send()
        to(o_dev.at[0], o_all.at[d], so.at[d], ro.at[d], device(d)).wait_send()
        return c

    lax.fori_loop(1, n, finish, 0)


def dma(n):
    return pltpu.SemaphoreType.DMA((n,))


def forward_scan(t_dev, o_dev, n):
    return pl.pallas_call(
        functools.partial(forward_kernel, n),
        in_specs=[VMEM, VMEM],
        out_specs=[VMEM, VMEM],
        out_shape=[shape(n, DIM, DIM), shape(n, DIM // 4, DIM)],
        scratch_shapes=[pltpu.VMEM((n, DIM // 4, DIM), F32), pltpu.VMEM((n, DIM // 4, DIM), F32)] + [dma(n)] * 6,
        compiler_params=pltpu.CompilerParams(collective_id=0, has_side_effects=True, vmem_limit_bytes=LIMIT),
    )(t_dev, o_dev)


def middle_kernel(q_dev, y_dev, state, cotan, gain, d_out, source):
    for h in range(GROUP):
        cols = slice(h * DIM, (h + 1) * DIM)
        cot = cotan[:, cols].astype(F32)
        qd = split(q_dev[h])
        out = nt(qd, split(state[h])) + y_dev[h]
        scale = lax.rsqrt(jnp.mean(out * out, axis=1, keepdims=True) + EPS_OUT)
        normed = out * scale
        scaled = cot * gain[h]
        grad = scale * (scaled - normed * jnp.mean(normed * scaled, axis=1, keepdims=True))
        d_out[h] = grad
        src = tn(split(grad), qd)
        part = jnp.sum(cot * normed, axis=0, keepdims=True)
        for quarter in range(4):
            source[h, quarter, 0:32] = src[quarter * 32 : quarter * 32 + 32]
            source[h, quarter, 32:40] = jnp.broadcast_to(part, (8, DIM))


def middle(q_dev, y_dev, state, cotan, gain):
    square = head_spec(DIM, DIM)
    return pl.pallas_call(
        middle_kernel,
        grid=(HEADS // GROUP,),
        in_specs=[square, square, square, wide_spec(), head_spec(1, DIM)],
        out_specs=[square, head_spec(4, 40, DIM)],
        out_shape=[shape(HEADS, DIM, DIM), shape(HEADS, 4, 40, DIM)],
        compiler_params=pltpu.CompilerParams(vmem_limit_bytes=LIMIT),
    )(q_dev, y_dev, state, cotan, gain)


def backward_kernel(n, ways, source, t_all, adjoint, total, got, a_all, g_all, sx, rx, sa, ra, sd, rd, sg, rg):
    me = place()
    dp = lax.axis_index("dp")
    peers = [{"dp": lax.rem(dp + i, ways)} for i in range(1, ways)]
    greet(n, peers)

    def put(i, c):
        d = lax.rem(me - i + n, n)
        to(source.at[d], got.at[me], sx.at[d], rx.at[me], device(d)).start()
        return c

    lax.fori_loop(1, n, put, 0)
    got[me] = source[me]

    def step(i, carry):
        now, gains = carry
        p = n - 1 - i

        @pl.when(p != me)
        def _():
            to(source.at[0], got.at[p], sx.at[p], rx.at[p], device(p)).wait_recv()

        a_all[p] = now

        @pl.when(p != me)
        def _():
            to(a_all.at[p], adjoint.at[me], sa.at[p], ra.at[me], device(p)).start()

        return nt(split(now), split(t_all[p])) + got[p, 0:32], gains + got[p, 32:40]

    _, gains = lax.fori_loop(0, n, step, (jnp.zeros((DIM // 4, DIM), F32), jnp.zeros((8, DIM), F32)))
    adjoint[me] = a_all[me]
    g_all[dp] = gains
    for i in range(1, ways):
        other = lax.rem(dp + i, ways)
        to(g_all.at[dp], g_all.at[dp], sd.at[other], rd.at[dp], {"dp": other}).start()
    for i in range(1, ways):
        other = lax.rem(dp + i, ways)
        to(g_all.at[other], g_all.at[other], sd.at[other], rd.at[other], {"dp": other}).wait()
    summed = g_all[0]
    for i in range(1, ways):
        summed = summed + g_all[i]
    head = lax.div(me, 4)

    @pl.when(lax.rem(me, 4) == 0)
    def _():
        total[head] = summed

        def give(i, c):
            d = lax.rem(me + i, n)
            to(total.at[head], total.at[head], sg.at[d], rg.at[head], device(d)).start()
            return c

        lax.fori_loop(1, n, give, 0)

        def gone(i, c):
            d = lax.rem(me + i, n)
            to(total.at[head], total.at[head], sg.at[d], rg.at[head], device(d)).wait_send()
            return c

        lax.fori_loop(1, n, gone, 0)

    for h in range(HEADS):

        @pl.when(me != 4 * h)
        def _(h=h):
            to(total.at[h], total.at[h], sg.at[h], rg.at[h], device(4 * h)).wait_recv()

    def finish(i, c):
        d = lax.rem(me + i, n)
        to(a_all.at[d], adjoint.at[d], sa.at[d], ra.at[d], device(d)).wait()
        to(source.at[d], got.at[d], sx.at[d], rx.at[d], device(d)).wait_send()
        return c

    lax.fori_loop(1, n, finish, 0)


def backward_scan(source, t_all, n, ways):
    return pl.pallas_call(
        functools.partial(backward_kernel, n, ways),
        in_specs=[VMEM, VMEM],
        out_specs=[VMEM, VMEM],
        out_shape=[shape(n, DIM // 4, DIM), shape(HEADS, 8, DIM)],
        scratch_shapes=[
            pltpu.VMEM((n, 40, DIM), F32),
            pltpu.VMEM((n, DIM // 4, DIM), F32),
            pltpu.VMEM((ways, 8, DIM), F32),
        ]
        + [dma(n)] * 4
        + [dma(ways)] * 2
        + [dma(n), dma(HEADS)],
        compiler_params=pltpu.CompilerParams(collective_id=1, has_side_effects=True, vmem_limit_bytes=LIMIT),
    )(source, t_all)


def unit_back(unit, inv, grad):
    return inv * (grad - unit * jnp.sum(unit * grad, axis=1, keepdims=True))


def final_kernel(
    q, k0, k1, state, adjoint, grad, w_in, u_in, g_in, z_in, t_in, o_in, qe_in, gq_out, gk0, gk1, gv0, gv1
):
    row, col, row_at, col_at = places()
    strict = col_at < row_at
    reads = read_mask(col)
    many = [(h, b) for h in range(GROUP) for b in range(2)]
    count = len(many)
    key, kinv, query, qinv, states, adjoints, do = [], [], [], [], [], [], []
    for h in range(GROUP):
        ta, tb = split(t_in[h, 0]), split(t_in[h, 1])
        s0, a1 = split(state[h]), split(adjoint[h])
        do0, do1 = split(grad[h, :HALF]), split(grad[h, HALF:])
        s1 = split(nn(s0, ta) + o_in[h])
        a0 = split(nt(a1, tb) + tn(do1, split(qe_in[h])))
        states += [s0, s1]
        adjoints += [a0, a1]
        do += [do0, do1]
        for b in range(2):
            kr = rows_of(k0, k1, b, h).astype(F32)
            kinv.append(inv_norm(kr))
            key.append(kr * kinv[-1])
            qr = tokens_of(q, b, h).astype(F32)
            qinv.append(inv_norm(qr))
            query.append(qr * qinv[-1])
    keys = [split(x) for x in key]
    update = [split(u_in[many[i]] - nt(split(w_in[many[i]]), states[i])) for i in range(count)]
    target = [tn(split(z_in[many[i]]), do[i]) + nt(split(g_in[many[i]]), adjoints[i]) for i in range(count)]
    less = [split(-x) for x in target]
    pair = [stacked(do[i], less[i]) for i in range(count)]
    inner = [nt(pair[i], update[i]) for i in range(count)]
    d_scores = [split(jnp.where(reads, inner[i][:HALF], 0.0)) for i in range(count)]
    d_gram = [jnp.where(strict, inner[i][HALF:], 0.0) for i in range(count)]
    d_gram = [split(x + x.T) for x in d_gram]
    by_state = [nn(pair[i], states[i]) for i in range(count)]
    by_key = [nn(stacked(d_scores[i], d_gram[i]), keys[i]) for i in range(count)]
    by_adj = [nn(update[i], adjoints[i]) for i in range(count)]
    by_query = [tn(d_scores[i], split(query[i])) for i in range(count)]
    for i, (h, b) in enumerate(many):
        both = by_state[i] + by_key[i]
        gq = unit_back(query[i], qinv[i], both[:HALF]).astype(BF16)
        gk = unit_back(key[i], kinv[i], both[HALF:] + by_adj[i] + by_query[i]).astype(BF16)
        gv = target[i].astype(BF16)
        at = slice(b * HALF, (b + 1) * HALF)
        cols = slice(h * DIM, (h + 1) * DIM)
        gq_out[at, cols] = gq
        gk0[at, cols] = gk[:HALF]
        gk1[at, cols] = gk[HALF:]
        gv0[at, cols] = gv[:HALF]
        gv1[at, cols] = gv[HALF:]


def final(q, k, state, adjoint, grad, w_in, u_in, g_in, z_in, t_in, o_in, qe_in):
    steps = HEADS // GROUP
    square, pair, thin = head_spec(DIM, DIM), head_spec(2, DIM, DIM), head_spec(2, HALF, DIM)
    return pl.pallas_call(
        final_kernel,
        grid=(steps,),
        in_specs=[wide_spec(), wide_spec(), wide_spec(steps), square, square, square]
        + [pair, pair, pair, thin, pair, square, head_spec(HALF, DIM)],
        out_specs=[wide_spec()] * 5,
        out_shape=[shape(DIM, HEADS * DIM, dtype=BF16)] * 5,
        compiler_params=pltpu.CompilerParams(vmem_limit_bytes=LIMIT),
    )(q, k, k, state, adjoint, grad, w_in, u_in, g_in, z_in, t_in, o_in, qe_in)


def on_device(queries, keys, values, betas, grad_out, gain):
    n = lax.axis_size("outer") * lax.axis_size("inner")
    ways = lax.axis_size("dp")
    q = queries[0]
    k = keys[0].reshape(DIM, 2 * HEADS * DIM)
    v = values[0].reshape(DIM, 2 * HEADS * DIM)
    rate = betas[0].reshape(HEADS, 2, 2, HALF).transpose(0, 2, 1, 3).reshape(HEADS, 2, DIM)
    t_dev, o_dev, q_dev, y_dev, w, u, g, z, t_blk, o_blk, qe = state_maps(q, k, v, rate)
    t_all, state = forward_scan(t_dev, o_dev.reshape(n, DIM // 4, DIM), n)
    state = state.reshape(HEADS, DIM, DIM)
    grad, source = middle(q_dev, y_dev, state, grad_out[0], gain.reshape(HEADS, 1, DIM))
    adjoint, total = backward_scan(source.reshape(n, 40, DIM), t_all, n, ways)
    adjoint = adjoint.reshape(HEADS, DIM, DIM)
    gq, gk0, gk1, gv0, gv1 = final(q, k, state, adjoint, grad, w, u, g, z, t_blk, o_blk, qe)
    grad_k = jnp.stack([gk0, gk1], axis=1)[None]
    grad_v = jnp.stack([gv0, gv1], axis=1)[None]
    gain_grad = total[:, 0, :].reshape(HEADS * DIM) * (1.0 / math.sqrt(DIM * n * ways))
    return gq[None], grad_k, grad_v, gain_grad


def solution(mesh):
    seq = ("outer", "inner")
    return jax.shard_map(
        on_device,
        mesh=mesh,
        in_specs=(
            P("dp", seq, None),
            P("dp", seq, None, None),
            P("dp", seq, None, None),
            P("dp", None, None, seq),
            P("dp", seq, None),
            P(),
        ),
        out_specs=(P("dp", seq, None), P("dp", seq, None, None), P("dp", seq, None, None), P()),
        check_vma=False,
    )
```

```python
import functools
import math

import jax
import jax.numpy as jnp
from jax import lax
from jax.experimental import pallas as pl
from jax.experimental.pallas import tpu as pltpu
from jax.sharding import PartitionSpec as P

HEADS = 8
DIM = 128
HALF = 64
GROUP = 2
RUN = 4
EPS_KEY = 1e-06
EPS_OUT = 1e-05
F32 = jnp.float32
BF16 = jnp.bfloat16
MESH = pl.DeviceIdType.MESH
VMEM = pl.BlockSpec(memory_space=pltpu.VMEM)
LIMIT = 48 * 1024 * 1024


def split(x):
    high = x.astype(BF16)
    return high, (x - high.astype(F32)).astype(BF16)


def raw_dot(left, right, dims):
    return lax.dot_general(left, right, (dims, ((), ())), preferred_element_type=F32)


def folded(wide):
    half = wide.shape[1] // 2
    return wide[:, :half] + wide[:, half:]


def nn(a, b):
    lhs = jnp.concatenate(a, axis=1)
    rhs = jnp.concatenate(b, axis=1)
    return folded(raw_dot(lhs, jnp.concatenate([rhs, rhs], axis=0), ((1,), (0,))))


def nt(a, b):
    lhs = jnp.concatenate(a, axis=1)
    rhs = jnp.concatenate(b, axis=0)
    return folded(raw_dot(lhs, jnp.concatenate([rhs, rhs], axis=1), ((1,), (1,))))


def tn(a, b):
    lhs = jnp.concatenate(a, axis=0)
    rhs = jnp.concatenate(b, axis=1)
    return folded(raw_dot(lhs, jnp.concatenate([rhs, rhs], axis=0), ((0,), (0,))))


def nn_sum(*terms):
    lhs = jnp.concatenate([x for a, _ in terms for x in a], axis=1)
    rhs = []
    for _, b in terms:
        rhs += [jnp.concatenate(b, axis=1)] * 2
    return folded(raw_dot(lhs, jnp.concatenate(rhs, axis=0), ((1,), (0,))))


def stacked(*pairs):
    return tuple(jnp.concatenate(part, axis=0) for part in zip(*pairs))


def beside(*pairs):
    return tuple(jnp.concatenate(part, axis=1) for part in zip(*pairs))


def inv_norm(x):
    return lax.rsqrt(jnp.sum(x * x, axis=1, keepdims=True) + EPS_KEY)


def places():
    row = lax.broadcasted_iota(jnp.int32, (DIM, DIM), 0)
    col = lax.broadcasted_iota(jnp.int32, (DIM, DIM), 1)

    def order(n):
        return jnp.where(n < HALF, 2 * n, 2 * n - (DIM - 1))

    return row, col, order(row), order(col)


def read_mask(col):
    token = lax.broadcasted_iota(jnp.int32, (HALF, DIM), 0)
    return jnp.where(col[:HALF] < HALF, col[:HALF], col[:HALF] - HALF) <= token


def put(ref, at, pair):
    ref[(0, *at)] = pair[0]
    ref[(1, *at)] = pair[1]


def get(ref, *at):
    return ref[(0, *at)], ref[(1, *at)]


def joined(pair):
    return pair[0].astype(F32) + pair[1].astype(F32)


def columns(head, part=0):
    return pl.ds(pl.multiple_of((part * HEADS + head) * DIM, DIM), DIM)


def tokens(block):
    return slice(block * HALF, (block + 1) * HALF)


def two_keys(ref, block, head):
    return jnp.concatenate([ref[tokens(block), columns(head, j)] for j in range(2)], axis=0)


def to(src, dst, send, recv, target):
    return pltpu.make_async_remote_copy(
        src_ref=src, dst_ref=dst, send_sem=send, recv_sem=recv, device_id=target, device_id_type=MESH
    )


def device(d):
    return {"outer": lax.div(d, 2), "inner": lax.rem(d, 2)}


def layer_kernel(
    n, ways,
    q, k, v, rate, cotan, gain,
    gq_out, gk_out, gv_out, total,
    t_dev, o_dev, q_dev, y_dev, knp, qnp, kinv, qinv, wp, u, gp, zp, tp, o_blk, qep,
    t_all, o_all, runs, local, s_all, state, dop, source, got, a_all, adjoint, g_all,
    sp, upd, part, hold, src1,
    st, rt, sf, rf, so, ro, ss, rs, sx, rx, sa, ra, sd, rd, sg, rg,
):
    core = lax.axis_index("inner")
    chip = lax.axis_index("outer")
    me = 2 * chip + core
    mine = lax.div(me, 4)
    dp = lax.axis_index("dp")
    chips = n // 2
    sibling = {"inner": 1 - core}
    barrier = pltpu.get_barrier_semaphore()

    def tell(i, c):
        pl.semaphore_signal(barrier, inc=1, device_id=device(lax.rem(me + i, n)), device_id_type=MESH)
        return c

    lax.fori_loop(1, n, tell, 0)
    for i in range(1, ways):
        pl.semaphore_signal(barrier, inc=1, device_id={"dp": lax.rem(dp + i, ways)}, device_id_type=MESH)
    pl.semaphore_wait(barrier, n + ways - 2)

    row, col, row_at, col_at = places()
    eye = row == col
    strict = col_at < row_at
    reads = read_mask(col)
    many = [(h, b) for h in range(GROUP) for b in range(2)]
    count = len(many)
    one = jnp.where(eye, 1.0, 0.0)
    steps = HEADS // GROUP

    def level(s):
        shift = s.bit_length() - 1
        rb, cb = row_at >> shift, col_at >> shift
        return ((rb >> 1) == (cb >> 1)) & ((rb & 1) == 1) & ((cb & 1) == 0)

    def masked(pair, mask):
        return tuple(jnp.where(mask, x.astype(F32), 0.0).astype(BF16) for x in pair)

    def send_maps(h):
        for e in range(2):
            d = 4 * h + 2 * e + core

            @pl.when(d != me)
            def _():
                to(t_dev.at[h], t_all.at[me], st.at[d], rt.at[me], device(d)).start()

        for j in range(4):
            d = 4 * h + j

            @pl.when(d != me)
            def _():
                to(o_dev.at[d], o_all.at[me], so.at[d], ro.at[me], device(d)).start()

    def maps(step, c):
        heads = [step * GROUP + h for h in range(GROUP)]
        keys, vals, query, queries, ratecol, raterow = [], [], [], [], [], []
        for h, b in many:
            kr = two_keys(k, b, heads[h]).astype(F32)
            inv = inv_norm(kr)
            kinv[heads[h], b] = inv
            keys.append(split(kr * inv))
            put(knp, (heads[h], b), keys[-1])
            vals.append(two_keys(v, b, heads[h]))
            qr = q[tokens(b), columns(heads[h])].astype(F32)
            inv = inv_norm(qr)
            qinv[heads[h], b] = inv
            query.append(qr * inv)
            queries.append(split(query[-1]))
            put(qnp, (heads[h], b), queries[-1])
            r = rate[heads[h], b : b + 1, :]
            raterow.append(r)
            ratecol.append(jnp.sum(jnp.where(eye, r, 0.0), axis=1, keepdims=True))
        both = [nt(stacked(keys[i], queries[i]), keys[i]) for i in range(count)]
        lower = [jnp.where(strict, ratecol[i] * both[i][:DIM], 0.0) for i in range(count)]
        scores = [split(jnp.where(reads, both[i][DIM:], 0.0)) for i in range(count)]
        first = level(1)
        inverse = [one - jnp.where(first, lower[i], 0.0) for i in range(count)]
        lower = [split(x) for x in lower]
        s = 2
        while s < DIM:
            mask = level(s)
            halves = [split(x) for x in inverse]
            inner = [split(nn(masked(lower[i], mask), halves[i])) for i in range(count)]
            inverse = [inverse[i] - nn(halves[i], inner[i]) for i in range(count)]
            s *= 2
        scaled = [split(inverse[i] * raterow[i]) for i in range(count)]
        zero = jnp.zeros((DIM, DIM), BF16)
        pack = [beside(keys[i], (vals[i], zero)) for i in range(count)]
        solved = [nn(scaled[i], pack[i]) for i in range(count)]
        z = [split(nn(scores[i], scaled[i])) for i in range(count)]
        gmat = [split(tn(scaled[i], keys[i])) for i in range(count)]
        solved_p = [split(x) for x in solved]
        move = [tn(solved_p[i], keys[i]) for i in range(count)]
        trans = [one - move[i][:DIM] for i in range(count)]
        offs = [move[i][DIM:] for i in range(count)]
        trans_p = [split(x) for x in trans]
        offs_p = [split(x) for x in offs]
        for h in range(GROUP):
            a, b = 2 * h, 2 * h + 1
            through = nn(stacked(trans_p[a], offs_p[a]), trans_p[b])
            t_dev[heads[h]] = through[:DIM]
            o_now = through[DIM:] + offs[b]
            for j in range(4):
                o_dev[4 * heads[h] + j] = o_now[j * 32 : j * 32 + 32]
            send_maps(heads[h])
        zr = [nn(z[i], pack[i]) for i in range(count)]
        qe = [query[i] - zr[i][:, :DIM] for i in range(count)]
        y = [zr[i][:, DIM:] for i in range(count)]
        for i, (h, b) in enumerate(many):
            put(wp, (heads[h], b), tuple(x[:, :DIM] for x in solved_p[i]))
            u[heads[h], b] = solved[i][:, DIM:]
            put(gp, (heads[h], b), gmat[i])
            put(zp, (heads[h], b), z[i])
            put(tp, (heads[h], b), trans_p[i])
        for h in range(GROUP):
            a, b = 2 * h, 2 * h + 1
            later = split(qe[b])
            back = nt(later, stacked(trans_p[a], offs_p[a]))
            put(q_dev, (heads[h], slice(0, HALF)), split(qe[a]))
            put(q_dev, (heads[h], slice(HALF, DIM)), split(back[:, :DIM]))
            y_dev[heads[h], :HALF] = y[a]
            y_dev[heads[h], HALF:] = y[b] + back[:, DIM:]
            o_blk[heads[h]] = offs[a]
            put(qep, (heads[h],), later)
        return c

    lax.fori_loop(0, steps, maps, 0)

    t_all[me] = t_dev[mine]
    o_all[me] = o_dev[me]

    def hand_over(i, c):
        p = 2 * lax.rem(chip - i + chips, chips) + core

        @pl.when(p != me)
        def _():
            to(t_dev.at[0], t_all.at[p], st.at[p], rt.at[p], device(p)).wait_recv()

        to(t_all.at[p], t_all.at[p], sf.at[p], rf.at[p], sibling).start()
        return c

    lax.fori_loop(0, chips, hand_over, 0)

    def handed(i, c):
        p = 2 * lax.rem(chip - i + chips, chips) + 1 - core
        to(t_all.at[p], t_all.at[p], sf.at[p], rf.at[p], sibling).wait_recv()
        return c

    lax.fori_loop(0, chips, handed, 0)

    def offset_here(i, c):
        p = lax.rem(me - i + n, n)
        to(o_dev.at[0], o_all.at[p], so.at[p], ro.at[p], device(p)).wait_recv()
        return c

    lax.fori_loop(1, n, offset_here, 0)

    groups = n // RUN
    wide = 4

    def products(i, c):
        base = [(i * wide + g) * RUN for g in range(wide)]
        trans = [split(t_all[p]) for p in base]
        offs = [o_all[p] for p in base]
        for g in range(wide):
            put(runs, (base[g],), trans[g])
            local[base[g]] = offs[g]
        trans = [stacked(trans[g], split(offs[g])) for g in range(wide)]
        for j in range(1, RUN):
            new = [nn(trans[g], split(t_all[base[g] + j])) for g in range(wide)]
            for g in range(wide):
                offs[g] = new[g][DIM:] + o_all[base[g] + j]
                local[base[g] + j] = offs[g]
                trans[g] = split(jnp.concatenate([new[g][:DIM], offs[g]], axis=0))
                put(runs, (base[g] + j,), tuple(x[:DIM] for x in trans[g]))
        return c

    lax.fori_loop(0, groups // wide, products, 0)

    def tell_state(p, now):
        s_all[p] = now

        @pl.when(p != me)
        def _():
            to(s_all.at[p], state.at[me], ss.at[p], rs.at[me], device(p)).start()

    def walk(g, now):
        base = g * RUN
        tell_state(base, now)
        halves = split(now)
        new = [nn(halves, get(runs, base + j)) + local[base + j] for j in range(RUN)]
        for j in range(RUN - 1):
            tell_state(base + j + 1, new[j])
        return new[RUN - 1]

    lax.fori_loop(0, groups, walk, jnp.zeros((DIM // 4, DIM), F32))
    state[me] = s_all[me]

    def suffixes(i, c):
        base = [(i * wide + g) * RUN for g in range(wide)]
        last = [split(t_all[p + RUN - 1]) for p in base]
        for g in range(wide):
            put(runs, (base[g] + RUN - 2,), last[g])
        for j in range(RUN - 2, 0, -1):
            last = [split(nn(split(t_all[base[g] + j]), last[g])) for g in range(wide)]
            for g in range(wide):
                put(runs, (base[g] + j - 1,), last[g])
        return c

    lax.fori_loop(0, groups // wide, suffixes, 0)

    def whole(ref, h):
        return ref[pl.ds(4 * h, 4)].reshape(DIM, DIM)

    def middle(step, c):
        heads = [step * GROUP + h for h in range(GROUP)]
        for h in heads:
            for j in range(4):
                d = 4 * h + j

                @pl.when(d != me)
                def _():
                    to(s_all.at[d], state.at[d], ss.at[d], rs.at[d], device(d)).wait_recv()

        qd = [get(q_dev, h) for h in heads]
        outs = [nt(qd[i], split(whole(state, h))) + y_dev[h] for i, h in enumerate(heads)]
        for i, h in enumerate(heads):
            out = outs[i]
            cot = cotan[:, columns(h)].astype(F32)
            scale = lax.rsqrt(jnp.mean(out * out, axis=1, keepdims=True) + EPS_OUT)
            normed = out * scale
            scaled = cot * gain[h]
            grad = scale * (scaled - normed * jnp.mean(normed * scaled, axis=1, keepdims=True))
            halves = split(grad)
            put(dop, (h,), halves)
            src = tn(halves, qd[i])
            gains = jnp.broadcast_to(jnp.sum(cot * normed, axis=0, keepdims=True), (8, DIM))
            for j in range(4):
                d = 4 * h + j
                source[d, 0:32] = src[j * 32 : j * 32 + 32]
                source[d, 32:40] = gains

                @pl.when(d != me)
                def _():
                    to(source.at[d], got.at[me], sx.at[d], rx.at[me], device(d)).start()

        return c

    lax.fori_loop(0, steps, middle, 0)
    got[me] = source[me]

    def by_states(step, c):
        heads = [step * GROUP + h for h in range(GROUP)]
        states, do = [], []
        for h in heads:
            s0 = split(whole(state, h))
            s1 = split(nn(s0, get(tp, h, 0)) + o_blk[h])
            do0, do1 = get(dop, h, slice(0, HALF)), get(dop, h, slice(HALF, DIM))
            states += [s0, s1]
            do += [do0, do1]
            src1[h] = tn(do1, get(qep, h))
        update = [split(u[heads[h], b] - nt(get(wp, heads[h], b), states[i])) for i, (h, b) in enumerate(many)]
        d_scores = [split(jnp.where(reads, nt(do[i], update[i]), 0.0)) for i in range(count)]
        for i, (h, b) in enumerate(many):
            at = (heads[h], b)
            put(sp, at, states[i])
            put(upd, at, update[i])
            hold[at] = tn(get(zp, *at), do[i])
            qn = get(qnp, *at)
            part[at] = tn(d_scores[i], qn)
            grad = nn_sum((do[i], states[i]), (d_scores[i], get(knp, *at)))
            unit = joined(qn)
            grad = qinv[at] * (grad - unit * jnp.sum(unit * grad, axis=1, keepdims=True))
            gq_out[tokens(b), columns(heads[h])] = grad.astype(BF16)
        return c

    lax.fori_loop(0, steps, by_states, 0)

    def source_here(i, gains):
        p = n - 1 - i

        @pl.when(p != me)
        def _():
            to(source.at[0], got.at[p], sx.at[p], rx.at[p], device(p)).wait_recv()

        return gains + got[p, 32:40]

    gains = lax.fori_loop(0, n, source_here, jnp.zeros((8, DIM), F32))
    g_all[dp] = gains
    for i in range(1, ways):
        other = lax.rem(dp + i, ways)
        to(g_all.at[dp], g_all.at[dp], sd.at[other], rd.at[dp], {"dp": other}).start()

    def locals_back(i, c):
        base = [(i * wide + g) * RUN for g in range(wide)]
        now = [got[p + RUN - 1, 0:32] for p in base]
        for g in range(wide):
            local[base[g] + RUN - 1] = now[g]
        for j in range(RUN - 1, 0, -1):
            new = [nt(split(now[g]), split(t_all[base[g] + j - 1])) for g in range(wide)]
            now = [new[g] + got[base[g] + j - 1, 0:32] for g in range(wide)]
            for g in range(wide):
                local[base[g] + j - 1] = now[g]
        return c

    lax.fori_loop(0, groups // wide, locals_back, 0)

    def tell_adjoint(p, now):
        a_all[p] = now

        @pl.when(p != me)
        def _():
            to(a_all.at[p], adjoint.at[me], sa.at[p], ra.at[me], device(p)).start()

    def walk_back(i, now):
        base = (groups - 1 - i) * RUN
        tell_adjoint(base + RUN - 1, now)
        halves = split(now)
        new = [nt(halves, get(runs, base + j)) for j in range(RUN)]
        for j in range(RUN - 2, -1, -1):
            tell_adjoint(base + j, new[j] + local[base + j + 1])
        return new[RUN - 1] + local[base]

    lax.fori_loop(0, groups, walk_back, jnp.zeros((DIM // 4, DIM), F32))
    adjoint[me] = a_all[me]

    for i in range(1, ways):
        other = lax.rem(dp + i, ways)
        to(g_all.at[other], g_all.at[other], sd.at[other], rd.at[other], {"dp": other}).wait()

    @pl.when(lax.rem(me, 4) == 0)
    def _():
        summed = g_all[0]
        for i in range(1, ways):
            summed = summed + g_all[i]
        total[mine] = summed

        def give(i, c):
            d = lax.rem(me + i, n)
            to(total.at[mine], total.at[mine], sg.at[d], rg.at[mine], device(d)).start()
            return c

        lax.fori_loop(1, n, give, 0)

    def final(step, c):
        heads = [step * GROUP + h for h in range(GROUP)]
        for h in heads:
            for j in range(4):
                d = 4 * h + j

                @pl.when(d != me)
                def _():
                    to(a_all.at[d], adjoint.at[d], sa.at[d], ra.at[d], device(d)).wait_recv()

        adjoints = []
        for h in heads:
            a1 = split(whole(adjoint, h))
            adjoints += [split(nt(a1, get(tp, h, 1)) + src1[h]), a1]
        places_of = [(heads[h], b) for h, b in many]
        target = [hold[at] + nt(get(gp, *at), adjoints[i]) for i, at in enumerate(places_of)]
        less = [split(-x) for x in target]
        update = [get(upd, *at) for at in places_of]
        d_gram = [jnp.where(strict, nt(less[i], update[i]), 0.0) for i in range(count)]
        d_gram = [split(x + x.T) for x in d_gram]
        for i, (h, b) in enumerate(many):
            at = places_of[i]
            kn = get(knp, *at)
            grad = part[at] + nn_sum((less[i], get(sp, *at)), (d_gram[i], kn), (update[i], adjoints[i]))
            unit = joined(kn)
            grad = kinv[at] * (grad - unit * jnp.sum(unit * grad, axis=1, keepdims=True))
            for j in range(2):
                gk_out[tokens(b), columns(heads[h], j)] = grad[tokens(j)].astype(BF16)
                gv_out[tokens(b), columns(heads[h], j)] = target[i][tokens(j)].astype(BF16)
        return c

    lax.fori_loop(0, steps, final, 0)

    @pl.when(lax.rem(me, 4) == 0)
    def _():
        def gone(i, c):
            d = lax.rem(me + i, n)
            to(total.at[mine], total.at[mine], sg.at[d], rg.at[mine], device(d)).wait_send()
            return c

        lax.fori_loop(1, n, gone, 0)

    def finish(i, c):
        d = lax.rem(me + i, n)
        to(o_dev.at[0], o_all.at[d], so.at[d], ro.at[d], device(d)).wait_send()
        to(s_all.at[d], state.at[d], ss.at[d], rs.at[d], device(d)).wait_send()
        to(source.at[d], got.at[d], sx.at[d], rx.at[d], device(d)).wait_send()
        to(a_all.at[d], adjoint.at[d], sa.at[d], ra.at[d], device(d)).wait_send()
        return c

    lax.fori_loop(1, n, finish, 0)

    def finish_maps(i, c):
        d = 2 * lax.rem(chip + i, chips) + core

        @pl.when(d != me)
        def _():
            to(t_dev.at[0], t_all.at[d], st.at[d], rt.at[d], device(d)).wait_send()

        to(t_all.at[d], t_all.at[d], sf.at[d], rf.at[d], sibling).wait_send()
        return c

    lax.fori_loop(0, chips, finish_maps, 0)

    for h in range(HEADS):

        @pl.when(me != 4 * h)
        def _(h=h):
            to(total.at[h], total.at[h], sg.at[h], rg.at[h], device(4 * h)).wait_recv()


def shape(*dims, dtype=F32):
    return jax.ShapeDtypeStruct(dims, dtype)


def layer(q, k, v, rate, cotan, gain, n, ways):
    def full(*dims):
        return pltpu.VMEM(dims, F32)

    def pair(*dims):
        return pltpu.VMEM((2, *dims), BF16)

    def dma(size):
        return pltpu.SemaphoreType.DMA((size,))

    square = (HEADS, DIM, DIM)
    blocks = (HEADS, 2, DIM, DIM)
    thin = (HEADS, 2, HALF, DIM)
    quarter = (n, DIM // 4, DIM)
    scratch = [
        full(*square), full(*quarter), pair(*square), full(*square),
        pair(*blocks), pair(*thin), full(HEADS, 2, DIM, 1), full(HEADS, 2, HALF, 1),
        pair(*blocks), full(*blocks), pair(*blocks), pair(*thin), pair(*blocks), full(*square), pair(HEADS, HALF, DIM),
        full(n, DIM, DIM), full(*quarter), pair(n, DIM, DIM), full(*quarter), full(*quarter), full(*quarter),
        pair(*square), full(n, 40, DIM), full(n, 40, DIM), full(*quarter), full(*quarter), full(ways, 8, DIM),
        pair(*blocks), pair(*blocks), full(*blocks), full(*blocks), full(*square),
    ]
    sems = [dma(n)] * 12 + [dma(ways)] * 2 + [dma(n), dma(HEADS)]
    wide = HEADS * DIM
    return pl.pallas_call(
        functools.partial(layer_kernel, n, ways),
        in_specs=[VMEM] * 6,
        out_specs=[VMEM] * 4,
        out_shape=[
            shape(DIM, wide, dtype=BF16),
            shape(DIM, 2 * wide, dtype=BF16),
            shape(DIM, 2 * wide, dtype=BF16),
            shape(HEADS, 8, DIM),
        ],
        scratch_shapes=scratch + sems,
        compiler_params=pltpu.CompilerParams(collective_id=0, has_side_effects=True, vmem_limit_bytes=LIMIT),
    )(q, k, v, rate, cotan, gain)


def on_device(queries, keys, values, betas, grad_out, gain):
    n = lax.axis_size("outer") * lax.axis_size("inner")
    ways = lax.axis_size("dp")
    k = keys[0].reshape(DIM, 2 * HEADS * DIM)
    v = values[0].reshape(DIM, 2 * HEADS * DIM)
    rate = betas[0].reshape(HEADS, 2, 2, HALF).transpose(0, 2, 1, 3).reshape(HEADS, 2, DIM)
    gq, gk, gv, total = layer(queries[0], k, v, rate, grad_out[0], gain.reshape(HEADS, 1, DIM), n, ways)
    grad_k = gk.reshape(1, DIM, 2, HEADS * DIM)
    grad_v = gv.reshape(1, DIM, 2, HEADS * DIM)
    gain_grad = total[:, 0, :].reshape(HEADS * DIM) * (1.0 / math.sqrt(DIM * n * ways))
    return gq[None], grad_k, grad_v, gain_grad


def solution(mesh):
    seq = ("outer", "inner")
    return jax.shard_map(
        on_device,
        mesh=mesh,
        in_specs=(
            P("dp", seq, None),
            P("dp", seq, None, None),
            P("dp", seq, None, None),
            P("dp", None, None, seq),
            P("dp", seq, None),
            P(),
        ),
        out_specs=(P("dp", seq, None), P("dp", seq, None, None), P("dp", seq, None, None), P()),
        check_vma=False,
    )
```

```python
import functools
import math

import jax
import jax.numpy as jnp
from jax import lax
from jax.experimental import pallas as pl
from jax.experimental.pallas import tpu as pltpu
from jax.sharding import PartitionSpec as P

HEADS = 8
DIM = 128
HALF = 64
GROUP = 2
RUN = 4
EPS_KEY = 1e-06
EPS_OUT = 1e-05
F32 = jnp.float32
BF16 = jnp.bfloat16
MESH = pl.DeviceIdType.MESH
VMEM = pl.BlockSpec(memory_space=pltpu.VMEM)
LIMIT = 48 * 1024 * 1024


def split(x):
    high = x.astype(BF16)
    return high, (x - high.astype(F32)).astype(BF16)


def raw_dot(left, right, dims):
    return lax.dot_general(left, right, (dims, ((), ())), preferred_element_type=F32)


def folded(wide):
    half = wide.shape[1] // 2
    return wide[:, :half] + wide[:, half:]


def nn(a, b):
    lhs = jnp.concatenate(a, axis=1)
    rhs = jnp.concatenate(b, axis=1)
    return folded(raw_dot(lhs, jnp.concatenate([rhs, rhs], axis=0), ((1,), (0,))))


def nt(a, b):
    lhs = jnp.concatenate(a, axis=1)
    rhs = jnp.concatenate(b, axis=0)
    return folded(raw_dot(lhs, jnp.concatenate([rhs, rhs], axis=1), ((1,), (1,))))


def tn(a, b):
    lhs = jnp.concatenate(a, axis=0)
    rhs = jnp.concatenate(b, axis=1)
    return folded(raw_dot(lhs, jnp.concatenate([rhs, rhs], axis=0), ((0,), (0,))))


def nn_sum(*terms):
    lhs = jnp.concatenate([x for a, _ in terms for x in a], axis=1)
    rhs = []
    for _, b in terms:
        rhs += [jnp.concatenate(b, axis=1)] * 2
    return folded(raw_dot(lhs, jnp.concatenate(rhs, axis=0), ((1,), (0,))))


def stacked(*pairs):
    return tuple(jnp.concatenate(part, axis=0) for part in zip(*pairs))


def beside(*pairs):
    return tuple(jnp.concatenate(part, axis=1) for part in zip(*pairs))


def inv_norm(x):
    return lax.rsqrt(jnp.sum(x * x, axis=1, keepdims=True) + EPS_KEY)


def places():
    row = lax.broadcasted_iota(jnp.int32, (DIM, DIM), 0)
    col = lax.broadcasted_iota(jnp.int32, (DIM, DIM), 1)

    def order(n):
        return jnp.where(n < HALF, 2 * n, 2 * n - (DIM - 1))

    return row, col, order(row), order(col)


def read_mask(col):
    token = lax.broadcasted_iota(jnp.int32, (HALF, DIM), 0)
    return jnp.where(col[:HALF] < HALF, col[:HALF], col[:HALF] - HALF) <= token


def put(ref, at, pair):
    ref[(0, *at)] = pair[0]
    ref[(1, *at)] = pair[1]


def get(ref, *at):
    return ref[(0, *at)], ref[(1, *at)]


def joined(pair):
    return pair[0].astype(F32) + pair[1].astype(F32)


def columns(head, part=0):
    return pl.ds(pl.multiple_of((part * HEADS + head) * DIM, DIM), DIM)


def tokens(block):
    return slice(block * HALF, (block + 1) * HALF)


def two_keys(ref, block, head):
    return jnp.concatenate([ref[tokens(block), columns(head, j)] for j in range(2)], axis=0)


def to(src, dst, send, recv, target):
    return pltpu.make_async_remote_copy(
        src_ref=src, dst_ref=dst, send_sem=send, recv_sem=recv, device_id=target, device_id_type=MESH
    )


def layer_kernel(
    n, ways,
    q, k, v, rate, cotan, gain,
    gq_out, gk_out, gv_out, total,
    m_dev, m_sib, q_dev, q_grp, y_dev, knp, qnp, kinv, qinv, wp, u, gp, zp, tp, o_blk, qep,
    m_out, m_all, t_all, runs, local, s_all, state, dop, src_two, src_got, src_own, src_next, source, got, a_all, adjoint, g_all,
    sp, upd, part, hold, src1,
    sw, rw, st, rt, sf, rf, ss, rs, shs, rhs, sy, ry, so, ro, sx, rx, sa, ra, sha, rha, sd, rd, sg, rg,
):
    core = lax.axis_index("inner")
    chip = lax.axis_index("outer")
    chips = n // 2
    mine = lax.div(chip, 2)
    dp = lax.axis_index("dp")
    sibling = {"inner": 1 - core}
    steps = HEADS // GROUP
    quarter = DIM // 4

    def there(x):
        return {"outer": x}

    barrier = pltpu.get_barrier_semaphore()

    def tell(i, c):
        pl.semaphore_signal(barrier, inc=1, device_id=there(lax.rem(chip + i, chips)), device_id_type=MESH)
        return c

    lax.fori_loop(1, chips, tell, 0)
    pl.semaphore_signal(barrier, inc=1, device_id=sibling, device_id_type=MESH)
    for i in range(1, ways):
        pl.semaphore_signal(barrier, inc=1, device_id={"dp": lax.rem(dp + i, ways)}, device_id_type=MESH)

    row, col, row_at, col_at = places()
    eye = row == col
    strict = col_at < row_at
    reads = read_mask(col)
    many = [(h, b) for h in range(GROUP) for b in range(2)]
    count = len(many)
    one = jnp.where(eye, 1.0, 0.0)

    def level(s):
        shift = s.bit_length() - 1
        rb, cb = row_at >> shift, col_at >> shift
        return ((rb >> 1) == (cb >> 1)) & ((rb & 1) == 1) & ((cb & 1) == 0)

    def masked(pair, mask):
        return tuple(jnp.where(mask, x.astype(F32), 0.0).astype(BF16) for x in pair)

    def turn(step):
        first = lax.rem(step + chip, steps) * GROUP
        return [first + h for h in range(GROUP)]

    def swap(h):
        return to(m_dev.at[h], m_sib.at[h], sw.at[h], rw.at[h], sibling)

    def chip_maps(step):
        heads = turn(step)
        half = pl.ds(pl.multiple_of(core * HALF, HALF), HALF)
        lead = core == 0
        for h in heads:
            swap(h).wait_recv()
        rows, later, offs = [], [], []
        for h in heads:
            begin = [jnp.where(lead, m_dev[h, j, half], m_sib[h, j, half]) for j in range(2)]
            rows.append(split(jnp.concatenate(begin, axis=0)))
            later.append(split(jnp.where(lead, m_sib[h, 0], m_dev[h, 0])))
            offs.append(jnp.where(lead, m_sib[h, 1, half], m_dev[h, 1, half]))
        made = [nn(rows[i], later[i]) for i in range(GROUP)]
        for i, h in enumerate(heads):
            off = made[i][HALF:] + offs[i]
            for e in range(2):
                x = 2 * h + e
                m_out[x, :HALF] = made[i][:HALF]
                m_out[x, HALF:] = off[e * quarter : (e + 1) * quarter]

                @pl.when(x != chip)
                def _():
                    to(m_out.at[x], m_all.at[chip], st.at[x], rt.at[chip], there(x)).start()

        @pl.when(core == 1)
        def _():
            before = [stacked(split(m_sib[h, 0]), split(m_sib[h, 1])) for h in heads]
            back = [nt(get(q_dev, h), before[i]) for i, h in enumerate(heads)]
            for i, h in enumerate(heads):
                put(q_grp, (h,), split(back[i][:, :DIM]))
                y_dev[h] = y_dev[h] + back[i][:, DIM:]

    def maps(step, c):
        heads = turn(step)
        keys, vals, query, queries, ratecol, raterow = [], [], [], [], [], []
        for h, b in many:
            kr = two_keys(k, b, heads[h]).astype(F32)
            inv = inv_norm(kr)
            kinv[heads[h], b] = inv
            keys.append(split(kr * inv))
            put(knp, (heads[h], b), keys[-1])
            vals.append(two_keys(v, b, heads[h]))
            qr = q[tokens(b), columns(heads[h])].astype(F32)
            inv = inv_norm(qr)
            qinv[heads[h], b] = inv
            query.append(qr * inv)
            queries.append(split(query[-1]))
            put(qnp, (heads[h], b), queries[-1])
            r = rate[heads[h], b : b + 1, :]
            raterow.append(r)
            ratecol.append(jnp.sum(jnp.where(eye, r, 0.0), axis=1, keepdims=True))
        both = [nt(stacked(keys[i], queries[i]), keys[i]) for i in range(count)]
        lower = [jnp.where(strict, ratecol[i] * both[i][:DIM], 0.0) for i in range(count)]
        scores = [split(jnp.where(reads, both[i][DIM:], 0.0)) for i in range(count)]
        first = level(1)
        inverse = [one - jnp.where(first, lower[i], 0.0) for i in range(count)]
        lower = [split(x) for x in lower]
        s = 2
        while s < DIM:
            mask = level(s)
            halves = [split(x) for x in inverse]
            inner = [split(nn(masked(lower[i], mask), halves[i])) for i in range(count)]
            inverse = [inverse[i] - nn(halves[i], inner[i]) for i in range(count)]
            s *= 2
        scaled = [split(inverse[i] * raterow[i]) for i in range(count)]
        zero = jnp.zeros((DIM, DIM), BF16)
        pack = [beside(keys[i], (vals[i], zero)) for i in range(count)]
        solved = [nn(scaled[i], pack[i]) for i in range(count)]
        z = [split(nn(scores[i], scaled[i])) for i in range(count)]
        gmat = [split(tn(scaled[i], keys[i])) for i in range(count)]
        solved_p = [split(x) for x in solved]
        move = [tn(solved_p[i], keys[i]) for i in range(count)]
        trans = [one - move[i][:DIM] for i in range(count)]
        offs = [move[i][DIM:] for i in range(count)]
        trans_p = [split(x) for x in trans]
        offs_p = [split(x) for x in offs]
        zr = [nn(z[i], pack[i]) for i in range(count)]
        qe = [query[i] - zr[i][:, :DIM] for i in range(count)]
        y = [zr[i][:, DIM:] for i in range(count)]
        for i, (h, b) in enumerate(many):
            put(wp, (heads[h], b), tuple(x[:, :DIM] for x in solved_p[i]))
            u[heads[h], b] = solved[i][:, DIM:]
            put(gp, (heads[h], b), gmat[i])
            put(zp, (heads[h], b), z[i])
            put(tp, (heads[h], b), trans_p[i])
        for h in range(GROUP):
            a, b = 2 * h, 2 * h + 1
            through = nn(stacked(trans_p[a], offs_p[a]), trans_p[b])
            m_dev[heads[h], 0] = through[:DIM]
            m_dev[heads[h], 1] = through[DIM:] + offs[b]
            later = split(qe[b])
            back = nt(later, stacked(trans_p[a], offs_p[a]))
            for ref in (q_dev, q_grp):
                put(ref, (heads[h], slice(0, HALF)), split(qe[a]))
                put(ref, (heads[h], slice(HALF, DIM)), split(back[:, :DIM]))
            y_dev[heads[h], :HALF] = y[a]
            y_dev[heads[h], HALF:] = y[b] + back[:, DIM:]
            o_blk[heads[h]] = offs[a]
            put(qep, (heads[h],), later)

        @pl.when(step == 0)
        def _():
            pl.semaphore_wait(barrier, chips + ways - 1)

        for h in heads:
            swap(h).start()

        @pl.when(step > 0)
        def _():
            chip_maps(step - 1)

        return c

    lax.fori_loop(0, steps, maps, 0)
    chip_maps(steps - 1)
    m_all[chip] = m_out[chip]

    def hand_over(i, c):
        p = lax.rem(chip - i + chips, chips)

        @pl.when(p != chip)
        def _():
            to(m_out.at[0], m_all.at[p], st.at[p], rt.at[p], there(p)).wait_recv()

        t_all[p, core] = m_all[p, :HALF]
        to(t_all.at[p, core], t_all.at[p, core], sf.at[p], rf.at[p], sibling).start()
        return c

    lax.fori_loop(0, chips, hand_over, 0)

    def handed(i, c):
        p = lax.rem(chip - i + chips, chips)
        to(t_all.at[p, core], t_all.at[p, 1 - core], sf.at[p], rf.at[p], sibling).wait_recv()
        return c

    lax.fori_loop(0, chips, handed, 0)

    groups = chips // RUN
    bases = [g * RUN for g in range(groups)]

    def transit(p):
        return split(t_all[p].reshape(DIM, DIM))

    trans = [transit(p) for p in bases]
    offs = [m_all[p, HALF:] for p in bases]
    for g, p in enumerate(bases):
        put(runs, (p,), trans[g])
        local[p] = offs[g]
    trans = [stacked(trans[g], split(offs[g])) for g in range(groups)]
    for j in range(1, RUN):
        new = [nn(trans[g], transit(p + j)) for g, p in enumerate(bases)]
        for g, p in enumerate(bases):
            offs[g] = new[g][DIM:] + m_all[p + j, HALF:]
            local[p + j] = offs[g]
            trans[g] = split(jnp.concatenate([new[g][:DIM], offs[g]], axis=0))
            put(runs, (p + j,), tuple(x[:DIM] for x in trans[g]))

    def tell_state(p, now):
        s_all[p] = now

        @pl.when(p != chip)
        def _():
            to(s_all.at[p], state.at[core, chip], ss.at[p], rs.at[chip], there(p)).start()

    def walk(g, now):
        base = g * RUN
        tell_state(base, now)
        halves = split(now)
        new = [nn(halves, get(runs, base + j)) + local[base + j] for j in range(RUN)]
        for j in range(RUN - 1):
            tell_state(base + j + 1, new[j])
        return new[RUN - 1]

    lax.fori_loop(0, groups, walk, jnp.zeros((quarter, DIM), F32))
    state[core, chip] = s_all[chip]

    last = [transit(p + RUN - 1) for p in bases]
    for g, p in enumerate(bases):
        put(runs, (p + RUN - 2,), last[g])
    for j in range(RUN - 2, 0, -1):
        last = [split(nn(transit(p + j), last[g])) for g, p in enumerate(bases)]
        for g, p in enumerate(bases):
            put(runs, (p + j - 1,), last[g])

    def arrive(ref, sent, send, recv, hand_send, hand_recv):
        def one_head(h, c):
            for e in range(2):
                x = 2 * h + e

                @pl.when(x != chip)
                def _():
                    to(sent.at[x], ref.at[core, x], send.at[x], recv.at[x], there(x)).wait_recv()

            at = pl.ds(2 * h, 2)
            to(ref.at[core, at], ref.at[core, at], hand_send.at[h], hand_recv.at[h], sibling).start()
            return c

        lax.fori_loop(0, HEADS, one_head, 0)

    def handed_head(ref, h, hand_send, hand_recv):
        at = pl.ds(2 * h, 2)
        return to(ref.at[core, at], ref.at[1 - core, at], hand_send.at[h], hand_recv.at[h], sibling)

    def whole(ref, h):
        return jnp.concatenate([ref[c, pl.ds(2 * h, 2)].reshape(HALF, DIM) for c in range(2)], axis=0)

    arrive(state, s_all, ss, rs, shs, rhs)

    def swap_source(h):
        return to(src_two.at[h, 1 - core], src_got.at[h], sy.at[h], ry.at[h], sibling)

    def next_source(h):
        return to(src_own.at[h], src_next.at[h], so.at[h], ro.at[h], sibling)

    def middle(step, c):
        heads = [step * GROUP + h for h in range(GROUP)]
        for h in heads:
            handed_head(state, h, shs, rhs).wait_recv()
        qd = [get(q_grp, h) for h in heads]
        outs = [nt(qd[i], split(whole(state, h))) + y_dev[h] for i, h in enumerate(heads)]
        for i, h in enumerate(heads):
            out = outs[i]
            cot = cotan[:, columns(h)].astype(F32)
            scale = lax.rsqrt(jnp.mean(out * out, axis=1, keepdims=True) + EPS_OUT)
            normed = out * scale
            scaled = cot * gain[h]
            grad = scale * (scaled - normed * jnp.mean(normed * scaled, axis=1, keepdims=True))
            halves = split(grad)
            put(dop, (h,), halves)
            src = tn(halves, qd[i])
            gains = jnp.broadcast_to(jnp.sum(cot * normed, axis=0, keepdims=True), (8, DIM))
            for j in range(2):
                src_two[h, j, :HALF] = src[j * HALF : (j + 1) * HALF]
                src_two[h, j, HALF:] = gains
            swap_source(h).start()
        return c

    lax.fori_loop(0, steps, middle, 0)

    def chip_source(h, c):
        swap_source(h).wait_recv()
        both = src_two[h, core] + src_got[h]
        for e in range(2):
            x = 2 * h + e
            source[x, :quarter] = both[e * quarter : (e + 1) * quarter]
            source[x, quarter:] = both[HALF:]

            @pl.when(x != chip)
            def _():
                to(source.at[x], got.at[chip], sx.at[x], rx.at[chip], there(x)).start()

        return c

    lax.fori_loop(0, HEADS, chip_source, 0)
    got[chip] = source[chip]

    @pl.when(core == 1)
    def _():
        def own(step, c):
            for h in [step * GROUP + h for h in range(GROUP)]:
                src_own[h] = tn(get(dop, h), get(q_dev, h))
                next_source(h).start()
            return c

        lax.fori_loop(0, steps, own, 0)

    def by_states(step, c):
        heads = [step * GROUP + h for h in range(GROUP)]
        states, do = [], []
        for h in heads:
            begin = whole(state, h)
            moved = nn(split(begin), split(m_sib[h, 0])) + m_sib[h, 1]
            s0 = split(jnp.where(core == 0, begin, moved))
            s1 = split(nn(s0, get(tp, h, 0)) + o_blk[h])
            do0, do1 = get(dop, h, slice(0, HALF)), get(dop, h, slice(HALF, DIM))
            states += [s0, s1]
            do += [do0, do1]
            src1[h] = tn(do1, get(qep, h))
        update = [split(u[heads[h], b] - nt(get(wp, heads[h], b), states[i])) for i, (h, b) in enumerate(many)]
        d_scores = [split(jnp.where(reads, nt(do[i], update[i]), 0.0)) for i in range(count)]
        for i, (h, b) in enumerate(many):
            at = (heads[h], b)
            put(sp, at, states[i])
            put(upd, at, update[i])
            hold[at] = tn(get(zp, *at), do[i])
            qn = get(qnp, *at)
            part[at] = tn(d_scores[i], qn)
            grad = nn_sum((do[i], states[i]), (d_scores[i], get(knp, *at)))
            unit = joined(qn)
            grad = qinv[at] * (grad - unit * jnp.sum(unit * grad, axis=1, keepdims=True))
            gq_out[tokens(b), columns(heads[h])] = grad.astype(BF16)
        return c

    lax.fori_loop(0, steps, by_states, 0)

    def source_here(i, gains):
        p = chips - 1 - i

        @pl.when(p != chip)
        def _():
            to(source.at[0], got.at[p], sx.at[p], rx.at[p], there(p)).wait_recv()

        return gains + got[p, quarter:]

    gains = lax.fori_loop(0, chips, source_here, jnp.zeros((8, DIM), F32))
    g_all[dp] = gains
    for i in range(1, ways):
        other = lax.rem(dp + i, ways)
        to(g_all.at[dp], g_all.at[dp], sd.at[other], rd.at[dp], {"dp": other}).start()

    now = [got[p + RUN - 1, :quarter] for p in bases]
    for g, p in enumerate(bases):
        local[p + RUN - 1] = now[g]
    for j in range(RUN - 1, 0, -1):
        new = [nt(split(now[g]), transit(p + j - 1)) for g, p in enumerate(bases)]
        now = [new[g] + got[p + j - 1, :quarter] for g, p in enumerate(bases)]
        for g, p in enumerate(bases):
            local[p + j - 1] = now[g]

    def tell_adjoint(p, now):
        a_all[p] = now

        @pl.when(p != chip)
        def _():
            to(a_all.at[p], adjoint.at[core, chip], sa.at[p], ra.at[chip], there(p)).start()

    def walk_back(i, now):
        base = (groups - 1 - i) * RUN
        tell_adjoint(base + RUN - 1, now)
        halves = split(now)
        new = [nt(halves, get(runs, base + j)) for j in range(RUN)]
        for j in range(RUN - 2, -1, -1):
            tell_adjoint(base + j, new[j] + local[base + j + 1])
        return new[RUN - 1] + local[base]

    lax.fori_loop(0, groups, walk_back, jnp.zeros((quarter, DIM), F32))
    adjoint[core, chip] = a_all[chip]

    for i in range(1, ways):
        other = lax.rem(dp + i, ways)
        to(g_all.at[other], g_all.at[other], sd.at[other], rd.at[other], {"dp": other}).wait()

    @pl.when(lax.rem(chip, 2) == 0)
    def _():
        summed = g_all[0]
        for i in range(1, ways):
            summed = summed + g_all[i]
        total[mine] = summed

        def give(i, c):
            x = lax.rem(chip + i, chips)
            to(total.at[mine], total.at[mine], sg.at[x], rg.at[mine], there(x)).start()
            return c

        lax.fori_loop(1, chips, give, 0)

    @pl.when(core == 0)
    def _():
        def came(h, c):
            next_source(h).wait_recv()
            return c

        lax.fori_loop(0, HEADS, came, 0)

    arrive(adjoint, a_all, sa, ra, sha, rha)

    def final(step, c):
        heads = [step * GROUP + h for h in range(GROUP)]
        for h in heads:
            handed_head(adjoint, h, sha, rha).wait_recv()
        adjoints = []
        for h in heads:
            end = whole(adjoint, h)
            moved = nt(split(end), split(m_sib[h, 0])) + src_next[h]
            a1 = split(jnp.where(core == 0, moved, end))
            adjoints += [split(nt(a1, get(tp, h, 1)) + src1[h]), a1]
        places_of = [(heads[h], b) for h, b in many]
        target = [hold[at] + nt(get(gp, *at), adjoints[i]) for i, at in enumerate(places_of)]
        less = [split(-x) for x in target]
        update = [get(upd, *at) for at in places_of]
        d_gram = [jnp.where(strict, nt(less[i], update[i]), 0.0) for i in range(count)]
        d_gram = [split(x + x.T) for x in d_gram]
        for i, (h, b) in enumerate(many):
            at = places_of[i]
            kn = get(knp, *at)
            grad = part[at] + nn_sum((less[i], get(sp, *at)), (d_gram[i], kn), (update[i], adjoints[i]))
            unit = joined(kn)
            grad = kinv[at] * (grad - unit * jnp.sum(unit * grad, axis=1, keepdims=True))
            for j in range(2):
                gk_out[tokens(b), columns(heads[h], j)] = grad[tokens(j)].astype(BF16)
                gv_out[tokens(b), columns(heads[h], j)] = target[i][tokens(j)].astype(BF16)
        return c

    lax.fori_loop(0, steps, final, 0)

    @pl.when(lax.rem(chip, 2) == 0)
    def _():
        def gone(i, c):
            x = lax.rem(chip + i, chips)
            to(total.at[mine], total.at[mine], sg.at[x], rg.at[mine], there(x)).wait_send()
            return c

        lax.fori_loop(1, chips, gone, 0)

    def finish(i, c):
        x = lax.rem(chip + i, chips)
        to(m_out.at[x], m_all.at[x], st.at[x], rt.at[x], there(x)).wait_send()
        to(s_all.at[x], state.at[core, x], ss.at[x], rs.at[x], there(x)).wait_send()
        to(source.at[x], got.at[x], sx.at[x], rx.at[x], there(x)).wait_send()
        to(a_all.at[x], adjoint.at[core, x], sa.at[x], ra.at[x], there(x)).wait_send()
        return c

    lax.fori_loop(1, chips, finish, 0)

    def finish_hand(p, c):
        to(t_all.at[p, core], t_all.at[p, core], sf.at[p], rf.at[p], sibling).wait_send()
        return c

    lax.fori_loop(0, chips, finish_hand, 0)

    def finish_heads(h, c):
        swap(h).wait_send()
        handed_head(state, h, shs, rhs).wait_send()
        handed_head(adjoint, h, sha, rha).wait_send()
        swap_source(h).wait_send()

        @pl.when(core == 1)
        def _():
            next_source(h).wait_send()

        @pl.when(2 * h != chip)
        def _():
            to(total.at[h], total.at[h], sg.at[h], rg.at[h], there(2 * h)).wait_recv()

        return c

    lax.fori_loop(0, HEADS, finish_heads, 0)


def shape(*dims, dtype=F32):
    return jax.ShapeDtypeStruct(dims, dtype)


def layer(q, k, v, rate, cotan, gain, n, ways):
    def full(*dims):
        return pltpu.VMEM(dims, F32)

    def pair(*dims):
        return pltpu.VMEM((2, *dims), BF16)

    def dma(size):
        return pltpu.SemaphoreType.DMA((size,))

    chips = n // 2
    square = (HEADS, DIM, DIM)
    blocks = (HEADS, 2, DIM, DIM)
    thin = (HEADS, 2, HALF, DIM)
    quarter = (chips, DIM // 4, DIM)
    spread = (2, *quarter)
    noted = (DIM // 4 + 8, DIM)
    scratch = [
        full(*blocks), full(*blocks), pair(*square), pair(*square), full(*square),
        pair(*blocks), pair(*thin), full(HEADS, 2, DIM, 1), full(HEADS, 2, HALF, 1),
        pair(*blocks), full(*blocks), pair(*blocks), pair(*thin), pair(*blocks), full(*square), pair(HEADS, HALF, DIM),
        full(chips, 96, DIM), full(chips, 96, DIM), full(chips, 2, HALF, DIM), pair(chips, DIM, DIM), full(*quarter), full(*quarter),
        full(*spread), pair(*square), full(HEADS, 2, HALF + 8, DIM), full(HEADS, HALF + 8, DIM), full(*square), full(*square),
        full(chips, *noted), full(chips, *noted), full(*quarter), full(*spread), full(ways, 8, DIM),
        pair(*blocks), pair(*blocks), full(*blocks), full(*blocks), full(*square),
    ]
    counts = [HEADS, chips, chips, chips, HEADS, HEADS, HEADS, chips, chips, HEADS, ways]
    sems = [dma(size) for size in counts for _ in range(2)] + [dma(chips), dma(HEADS)]
    wide = HEADS * DIM
    return pl.pallas_call(
        functools.partial(layer_kernel, n, ways),
        in_specs=[VMEM] * 6,
        out_specs=[VMEM] * 4,
        out_shape=[
            shape(DIM, wide, dtype=BF16),
            shape(DIM, 2 * wide, dtype=BF16),
            shape(DIM, 2 * wide, dtype=BF16),
            shape(HEADS, 8, DIM),
        ],
        scratch_shapes=scratch + sems,
        compiler_params=pltpu.CompilerParams(collective_id=0, has_side_effects=True, vmem_limit_bytes=LIMIT),
    )(q, k, v, rate, cotan, gain)


def on_device(queries, keys, values, betas, grad_out, gain):
    n = lax.axis_size("outer") * lax.axis_size("inner")
    ways = lax.axis_size("dp")
    k = keys[0].reshape(DIM, 2 * HEADS * DIM)
    v = values[0].reshape(DIM, 2 * HEADS * DIM)
    rate = betas[0].reshape(HEADS, 2, 2, HALF).transpose(0, 2, 1, 3).reshape(HEADS, 2, DIM)
    gq, gk, gv, total = layer(queries[0], k, v, rate, grad_out[0], gain.reshape(HEADS, 1, DIM), n, ways)
    grad_k = gk.reshape(1, DIM, 2, HEADS * DIM)
    grad_v = gv.reshape(1, DIM, 2, HEADS * DIM)
    gain_grad = total[:, 0, :].reshape(HEADS * DIM) * (1.0 / math.sqrt(DIM * n * ways))
    return gq[None], grad_k, grad_v, gain_grad


def solution(mesh):
    seq = ("outer", "inner")
    return jax.shard_map(
        on_device,
        mesh=mesh,
        in_specs=(
            P("dp", seq, None),
            P("dp", seq, None, None),
            P("dp", seq, None, None),
            P("dp", None, None, seq),
            P("dp", seq, None),
            P(),
        ),
        out_specs=(P("dp", seq, None), P("dp", seq, None, None), P("dp", seq, None, None), P()),
        check_vma=False,
    )
```

```python
import functools
import math

import jax
import jax.numpy as jnp
from jax import lax
from jax.experimental import pallas as pl
from jax.experimental.pallas import tpu as pltpu
from jax.sharding import PartitionSpec as P

HEADS = 8
DIM = 128
HALF = 64
GROUP = 2
RUN = 4
EPS_KEY = 1e-06
EPS_OUT = 1e-05
F32 = jnp.float32
BF16 = jnp.bfloat16
MESH = pl.DeviceIdType.MESH
VMEM = pl.BlockSpec(memory_space=pltpu.VMEM)
LIMIT = 48 * 1024 * 1024


def split(x):
    high = x.astype(BF16)
    return high, (x - high.astype(F32)).astype(BF16)


def raw_dot(left, right, dims):
    return lax.dot_general(left, right, (dims, ((), ())), preferred_element_type=F32)


def folded(wide):
    half = wide.shape[1] // 2
    return wide[:, :half] + wide[:, half:]


def nn(a, b):
    lhs = jnp.concatenate(a, axis=1)
    rhs = jnp.concatenate(b, axis=1)
    return folded(raw_dot(lhs, jnp.concatenate([rhs, rhs], axis=0), ((1,), (0,))))


def nt(a, b):
    lhs = jnp.concatenate(a, axis=1)
    rhs = jnp.concatenate(b, axis=0)
    return folded(raw_dot(lhs, jnp.concatenate([rhs, rhs], axis=1), ((1,), (1,))))


def tn(a, b):
    lhs = jnp.concatenate(a, axis=0)
    rhs = jnp.concatenate(b, axis=1)
    return folded(raw_dot(lhs, jnp.concatenate([rhs, rhs], axis=0), ((0,), (0,))))


def nn_sum(*terms):
    lhs = jnp.concatenate([x for a, _ in terms for x in a], axis=1)
    rhs = []
    for _, b in terms:
        rhs += [jnp.concatenate(b, axis=1)] * 2
    return folded(raw_dot(lhs, jnp.concatenate(rhs, axis=0), ((1,), (0,))))


def stacked(*pairs):
    return tuple(jnp.concatenate(part, axis=0) for part in zip(*pairs))


def beside(*pairs):
    return tuple(jnp.concatenate(part, axis=1) for part in zip(*pairs))


def inv_norm(x):
    return lax.rsqrt(jnp.sum(x * x, axis=1, keepdims=True) + EPS_KEY)


def places():
    row = lax.broadcasted_iota(jnp.int32, (DIM, DIM), 0)
    return row, lax.broadcasted_iota(jnp.int32, (DIM, DIM), 1)


def read_mask(col):
    token = lax.broadcasted_iota(jnp.int32, (HALF, DIM), 0)
    return (col[:HALF] >> 1) <= token


def put(ref, at, pair):
    ref[(0, *at)] = pair[0]
    ref[(1, *at)] = pair[1]


def get(ref, *at):
    return ref[(0, *at)], ref[(1, *at)]


def joined(pair):
    return pair[0].astype(F32) + pair[1].astype(F32)


def columns(head):
    return pl.ds(pl.multiple_of(head * DIM, DIM), DIM)


def tokens(block):
    return slice(block * HALF, (block + 1) * HALF)


def two_keys(ref, block, head):
    return ref[tokens(block), :, columns(head)].reshape(DIM, DIM)


def to(src, dst, send, recv, target):
    return pltpu.make_async_remote_copy(
        src_ref=src, dst_ref=dst, send_sem=send, recv_sem=recv, device_id=target, device_id_type=MESH
    )


def layer_kernel(
    n, ways,
    q, k, v, rate, cotan, gain,
    gq_out, gk_out, gv_out, total,
    m_dev, m_sib, q_dev, q_grp, y_dev, knp, qnp, kinv, qinv, wp, u, gp, zp, tp, o_blk, qep, xbp, scp,
    m_out, m_all, t_all, runs, local, s_all, state, dop, src_two, src_got, src_own, src_next, source, got, a_all, adjoint, g_all,
    sp, upd, part, hold, src1,
    sw, rw, st, rt, sf, rf, ss, rs, shs, rhs, sy, ry, so, ro, sx, rx, sa, ra, sha, rha, sd, rd, sg, rg,
):
    core = lax.axis_index("inner")
    chip = lax.axis_index("outer")
    chips = n // 2
    mine = lax.div(chip, 2)
    dp = lax.axis_index("dp")
    sibling = {"inner": 1 - core}
    steps = HEADS // GROUP
    quarter = DIM // 4

    def there(x):
        return {"outer": x}

    barrier = pltpu.get_barrier_semaphore()

    def tell(i, c):
        pl.semaphore_signal(barrier, inc=1, device_id=there(lax.rem(chip + i, chips)), device_id_type=MESH)
        return c

    lax.fori_loop(1, chips, tell, 0)
    pl.semaphore_signal(barrier, inc=1, device_id=sibling, device_id_type=MESH)
    for i in range(1, ways):
        pl.semaphore_signal(barrier, inc=1, device_id={"dp": lax.rem(dp + i, ways)}, device_id_type=MESH)

    row, col = places()
    eye = row == col
    strict = col < row
    reads = read_mask(col)
    many = [(h, b) for h in range(GROUP) for b in range(2)]
    count = len(many)
    one = jnp.where(eye, 1.0, 0.0)

    def level(s):
        shift = s.bit_length() - 1
        rb, cb = row >> shift, col >> shift
        return ((rb >> 1) == (cb >> 1)) & ((rb & 1) == 1) & ((cb & 1) == 0)

    def masked(pair, mask):
        return tuple(jnp.where(mask, x.astype(F32), 0.0).astype(BF16) for x in pair)

    def turn(step):
        first = lax.rem(step + chip, steps) * GROUP
        return [first + h for h in range(GROUP)]

    def swap(h):
        return to(m_dev.at[h], m_sib.at[h], sw.at[h], rw.at[h], sibling)

    def chip_maps(step):
        heads = turn(step)
        half = pl.ds(pl.multiple_of(core * HALF, HALF), HALF)
        lead = core == 0
        for h in heads:
            swap(h).wait_recv()
        rows, later, offs = [], [], []
        for h in heads:
            begin = [jnp.where(lead, m_dev[h, j, half], m_sib[h, j, half]) for j in range(2)]
            rows.append(split(jnp.concatenate(begin, axis=0)))
            later.append(split(jnp.where(lead, m_sib[h, 0], m_dev[h, 0])))
            offs.append(jnp.where(lead, m_sib[h, 1, half], m_dev[h, 1, half]))
        made = [nn(rows[i], later[i]) for i in range(GROUP)]
        for i, h in enumerate(heads):
            off = made[i][HALF:] + offs[i]
            for e in range(2):
                x = 2 * h + e
                m_out[x, :HALF] = made[i][:HALF]
                m_out[x, HALF:] = off[e * quarter : (e + 1) * quarter]

                @pl.when(x != chip)
                def _():
                    to(m_out.at[x], m_all.at[chip], st.at[x], rt.at[chip], there(x)).start()

    def query_side(step):
        heads = [step * GROUP + h for h in range(GROUP)]
        zero = jnp.zeros((DIM, DIM), BF16)
        scaled = [get(xbp, heads[h], b) for h, b in many]
        keys = [get(knp, heads[h], b) for h, b in many]
        pack = [beside(keys[i], (two_keys(v, b, heads[h]), zero)) for i, (h, b) in enumerate(many)]
        z = [split(nn(get(scp, heads[h], b), scaled[i])) for i, (h, b) in enumerate(many)]
        zr = [nn(z[i], pack[i]) for i in range(count)]
        qe = [joined(get(qnp, heads[h], b)) - zr[i][:, :DIM] for i, (h, b) in enumerate(many)]
        for i, (h, b) in enumerate(many):
            put(gp, (heads[h], b), split(tn(scaled[i], keys[i])))
            put(zp, (heads[h], b), z[i])
        for h in range(GROUP):
            a, b = 2 * h, 2 * h + 1
            later = split(qe[b])
            back = nt(later, stacked(get(tp, heads[h], 0), split(o_blk[heads[h]])))
            for ref in (q_dev, q_grp):
                put(ref, (heads[h], slice(0, HALF)), split(qe[a]))
                put(ref, (heads[h], slice(HALF, DIM)), split(back[:, :DIM]))
            y_dev[heads[h], :HALF] = zr[a][:, DIM:]
            y_dev[heads[h], HALF:] = zr[b][:, DIM:] + back[:, DIM:]
            put(qep, (heads[h],), later)

        @pl.when(core == 1)
        def _():
            before = [stacked(split(m_sib[h, 0]), split(m_sib[h, 1])) for h in heads]
            back = [nt(get(q_dev, h), before[i]) for i, h in enumerate(heads)]
            for i, h in enumerate(heads):
                put(q_grp, (h,), split(back[i][:, :DIM]))
                y_dev[h] = y_dev[h] + back[i][:, DIM:]

    def maps(step, c):
        heads = turn(step)
        keys, vals, queries, ratecol, raterow = [], [], [], [], []
        for h, b in many:
            kr = two_keys(k, b, heads[h]).astype(F32)
            inv = inv_norm(kr)
            kinv[heads[h], b] = inv
            keys.append(split(kr * inv))
            put(knp, (heads[h], b), keys[-1])
            vals.append(two_keys(v, b, heads[h]))
            qr = q[tokens(b), columns(heads[h])].astype(F32)
            inv = inv_norm(qr)
            qinv[heads[h], b] = inv
            queries.append(split(qr * inv))
            put(qnp, (heads[h], b), queries[-1])
            r = rate[heads[h], b : b + 1, :]
            raterow.append(r)
            ratecol.append(jnp.sum(jnp.where(eye, r, 0.0), axis=1, keepdims=True))
        both = [nt(stacked(keys[i], queries[i]), keys[i]) for i in range(count)]
        lower = [jnp.where(strict, ratecol[i] * both[i][:DIM], 0.0) for i in range(count)]
        scores = [split(jnp.where(reads, both[i][DIM:], 0.0)) for i in range(count)]
        first = level(1)
        inverse = [one - jnp.where(first, lower[i], 0.0) for i in range(count)]
        lower = [split(x) for x in lower]
        s = 2
        while s < DIM:
            mask = level(s)
            halves = [split(x) for x in inverse]
            inner = [split(nn(masked(lower[i], mask), halves[i])) for i in range(count)]
            inverse = [inverse[i] - nn(halves[i], inner[i]) for i in range(count)]
            s *= 2
        scaled = [split(inverse[i] * raterow[i]) for i in range(count)]
        zero = jnp.zeros((DIM, DIM), BF16)
        pack = [beside(keys[i], (vals[i], zero)) for i in range(count)]
        solved = [nn(scaled[i], pack[i]) for i in range(count)]
        solved_p = [split(x) for x in solved]
        move = [tn(solved_p[i], keys[i]) for i in range(count)]
        trans = [one - move[i][:DIM] for i in range(count)]
        offs = [move[i][DIM:] for i in range(count)]
        trans_p = [split(x) for x in trans]
        offs_p = [split(x) for x in offs]
        for i, (h, b) in enumerate(many):
            put(wp, (heads[h], b), tuple(x[:, :DIM] for x in solved_p[i]))
            u[heads[h], b] = solved[i][:, DIM:]
            put(xbp, (heads[h], b), scaled[i])
            put(scp, (heads[h], b), scores[i])
            put(tp, (heads[h], b), trans_p[i])
        for h in range(GROUP):
            a, b = 2 * h, 2 * h + 1
            through = nn(stacked(trans_p[a], offs_p[a]), trans_p[b])
            m_dev[heads[h], 0] = through[:DIM]
            m_dev[heads[h], 1] = through[DIM:] + offs[b]
            o_blk[heads[h]] = offs[a]

        @pl.when(step == 0)
        def _():
            pl.semaphore_wait(barrier, chips + ways - 1)

        for h in heads:
            swap(h).start()

        @pl.when(step > 0)
        def _():
            chip_maps(step - 1)

        return c

    lax.fori_loop(0, steps, maps, 0)
    chip_maps(steps - 1)
    m_all[chip] = m_out[chip]

    def deferred(step, c):
        query_side(step)
        return c

    lax.fori_loop(0, steps // 2, deferred, 0)

    def hand_over(i, c):
        p = lax.rem(chip - i + chips, chips)

        @pl.when(p != chip)
        def _():
            to(m_out.at[0], m_all.at[p], st.at[p], rt.at[p], there(p)).wait_recv()

        t_all[p, core] = m_all[p, :HALF]
        to(t_all.at[p, core], t_all.at[p, core], sf.at[p], rf.at[p], sibling).start()
        return c

    lax.fori_loop(0, chips, hand_over, 0)
    lax.fori_loop(steps // 2, steps, deferred, 0)

    def handed(i, c):
        p = lax.rem(chip - i + chips, chips)
        to(t_all.at[p, core], t_all.at[p, 1 - core], sf.at[p], rf.at[p], sibling).wait_recv()
        return c

    lax.fori_loop(0, chips, handed, 0)

    groups = chips // RUN
    bases = [g * RUN for g in range(groups)]

    def transit(p):
        return split(t_all[p].reshape(DIM, DIM))

    trans = [transit(p) for p in bases]
    offs = [m_all[p, HALF:] for p in bases]
    for g, p in enumerate(bases):
        put(runs, (p,), trans[g])
        local[p] = offs[g]
    trans = [stacked(trans[g], split(offs[g])) for g in range(groups)]
    for j in range(1, RUN):
        new = [nn(trans[g], transit(p + j)) for g, p in enumerate(bases)]
        for g, p in enumerate(bases):
            offs[g] = new[g][DIM:] + m_all[p + j, HALF:]
            local[p + j] = offs[g]
            trans[g] = split(jnp.concatenate([new[g][:DIM], offs[g]], axis=0))
            put(runs, (p + j,), tuple(x[:DIM] for x in trans[g]))

    def tell_state(p, now):
        s_all[p] = now

        @pl.when(p != chip)
        def _():
            to(s_all.at[p], state.at[core, chip], ss.at[p], rs.at[chip], there(p)).start()

    def walk(g, now):
        base = g * RUN
        tell_state(base, now)
        halves = split(now)
        new = [nn(halves, get(runs, base + j)) + local[base + j] for j in range(RUN)]
        for j in range(RUN - 1):
            tell_state(base + j + 1, new[j])
        return new[RUN - 1]

    lax.fori_loop(0, groups, walk, jnp.zeros((quarter, DIM), F32))
    state[core, chip] = s_all[chip]

    last = [transit(p + RUN - 1) for p in bases]
    for g, p in enumerate(bases):
        put(runs, (p + RUN - 2,), last[g])
    for j in range(RUN - 2, 0, -1):
        last = [split(nn(transit(p + j), last[g])) for g, p in enumerate(bases)]
        for g, p in enumerate(bases):
            put(runs, (p + j - 1,), last[g])

    def arrive(ref, sent, send, recv, hand_send, hand_recv):
        def one_head(h, c):
            for e in range(2):
                x = 2 * h + e

                @pl.when(x != chip)
                def _():
                    to(sent.at[x], ref.at[core, x], send.at[x], recv.at[x], there(x)).wait_recv()

            at = pl.ds(2 * h, 2)
            to(ref.at[core, at], ref.at[core, at], hand_send.at[h], hand_recv.at[h], sibling).start()
            return c

        lax.fori_loop(0, HEADS, one_head, 0)

    def handed_head(ref, h, hand_send, hand_recv):
        at = pl.ds(2 * h, 2)
        return to(ref.at[core, at], ref.at[1 - core, at], hand_send.at[h], hand_recv.at[h], sibling)

    def whole(ref, h):
        return jnp.concatenate([ref[c, pl.ds(2 * h, 2)].reshape(HALF, DIM) for c in range(2)], axis=0)

    arrive(state, s_all, ss, rs, shs, rhs)

    def swap_source(h):
        return to(src_two.at[h, 1 - core], src_got.at[h], sy.at[h], ry.at[h], sibling)

    def next_source(h):
        return to(src_own.at[h], src_next.at[h], so.at[h], ro.at[h], sibling)

    def chip_source(h):
        swap_source(h).wait_recv()
        both = src_two[h, core] + src_got[h]
        for e in range(2):
            x = 2 * h + e
            source[x, :quarter] = both[e * quarter : (e + 1) * quarter]
            source[x, quarter:] = both[HALF:]

            @pl.when(x != chip)
            def _():
                to(source.at[x], got.at[chip], sx.at[x], rx.at[chip], there(x)).start()

    def middle(step, c):
        heads = [step * GROUP + h for h in range(GROUP)]
        for h in heads:
            handed_head(state, h, shs, rhs).wait_recv()
        qd = [get(q_grp, h) for h in heads]
        outs = [nt(qd[i], split(whole(state, h))) + y_dev[h] for i, h in enumerate(heads)]
        for i, h in enumerate(heads):
            out = outs[i]
            cot = cotan[:, columns(h)].astype(F32)
            scale = lax.rsqrt(jnp.mean(out * out, axis=1, keepdims=True) + EPS_OUT)
            normed = out * scale
            scaled = cot * gain[h]
            grad = scale * (scaled - normed * jnp.mean(normed * scaled, axis=1, keepdims=True))
            halves = split(grad)
            put(dop, (h,), halves)
            src = tn(halves, qd[i])
            gains = jnp.broadcast_to(jnp.sum(cot * normed, axis=0, keepdims=True), (8, DIM))
            for j in range(2):
                src_two[h, j, :HALF] = src[j * HALF : (j + 1) * HALF]
                src_two[h, j, HALF:] = gains
            swap_source(h).start()

        @pl.when(step > 0)
        def _():
            for h in heads:
                chip_source(h - GROUP)

        return c

    lax.fori_loop(0, steps, middle, 0)

    for h in range(HEADS - GROUP, HEADS):
        chip_source(h)
    got[chip] = source[chip]

    @pl.when(core == 1)
    def _():
        def own(step, c):
            for h in [step * GROUP + h for h in range(GROUP)]:
                src_own[h] = tn(get(dop, h), get(q_dev, h))
                next_source(h).start()
            return c

        lax.fori_loop(0, steps, own, 0)

    def by_states(step, c):
        heads = [step * GROUP + h for h in range(GROUP)]
        states, do = [], []
        for h in heads:
            begin = whole(state, h)
            moved = nn(split(begin), split(m_sib[h, 0])) + m_sib[h, 1]
            s0 = split(jnp.where(core == 0, begin, moved))
            s1 = split(nn(s0, get(tp, h, 0)) + o_blk[h])
            do0, do1 = get(dop, h, slice(0, HALF)), get(dop, h, slice(HALF, DIM))
            states += [s0, s1]
            do += [do0, do1]
            src1[h] = tn(do1, get(qep, h))
        update = [split(u[heads[h], b] - nt(get(wp, heads[h], b), states[i])) for i, (h, b) in enumerate(many)]
        d_scores = [split(jnp.where(reads, nt(do[i], update[i]), 0.0)) for i in range(count)]
        for i, (h, b) in enumerate(many):
            at = (heads[h], b)
            put(sp, at, states[i])
            put(upd, at, update[i])
            hold[at] = tn(get(zp, *at), do[i])
            qn = get(qnp, *at)
            part[at] = tn(d_scores[i], qn)
            grad = nn_sum((do[i], states[i]), (d_scores[i], get(knp, *at)))
            unit = joined(qn)
            grad = qinv[at] * (grad - unit * jnp.sum(unit * grad, axis=1, keepdims=True))
            gq_out[tokens(b), columns(heads[h])] = grad.astype(BF16)
        return c

    lax.fori_loop(0, steps, by_states, 0)

    def source_here(i, gains):
        p = chips - 1 - i

        @pl.when(p != chip)
        def _():
            to(source.at[0], got.at[p], sx.at[p], rx.at[p], there(p)).wait_recv()

        return gains + got[p, quarter:]

    gains = lax.fori_loop(0, chips, source_here, jnp.zeros((8, DIM), F32))
    g_all[dp] = gains
    for i in range(1, ways):
        other = lax.rem(dp + i, ways)
        to(g_all.at[dp], g_all.at[dp], sd.at[other], rd.at[dp], {"dp": other}).start()

    now = [got[p + RUN - 1, :quarter] for p in bases]
    for g, p in enumerate(bases):
        local[p + RUN - 1] = now[g]
    for j in range(RUN - 1, 0, -1):
        new = [nt(split(now[g]), transit(p + j - 1)) for g, p in enumerate(bases)]
        now = [new[g] + got[p + j - 1, :quarter] for g, p in enumerate(bases)]
        for g, p in enumerate(bases):
            local[p + j - 1] = now[g]

    def tell_adjoint(p, now):
        a_all[p] = now

        @pl.when(p != chip)
        def _():
            to(a_all.at[p], adjoint.at[core, chip], sa.at[p], ra.at[chip], there(p)).start()

    def walk_back(i, now):
        base = (groups - 1 - i) * RUN
        tell_adjoint(base + RUN - 1, now)
        halves = split(now)
        new = [nt(halves, get(runs, base + j)) for j in range(RUN)]
        for j in range(RUN - 2, -1, -1):
            tell_adjoint(base + j, new[j] + local[base + j + 1])
        return new[RUN - 1] + local[base]

    lax.fori_loop(0, groups, walk_back, jnp.zeros((quarter, DIM), F32))
    adjoint[core, chip] = a_all[chip]

    @pl.when(core == 0)
    def _():
        def came(h, c):
            next_source(h).wait_recv()
            return c

        lax.fori_loop(0, HEADS, came, 0)

    arrive(adjoint, a_all, sa, ra, sha, rha)

    for i in range(1, ways):
        other = lax.rem(dp + i, ways)
        to(g_all.at[other], g_all.at[other], sd.at[other], rd.at[other], {"dp": other}).wait()

    @pl.when(lax.rem(chip, 2) == 0)
    def _():
        summed = g_all[0]
        for i in range(1, ways):
            summed = summed + g_all[i]
        total[mine] = summed

        def give(i, c):
            x = lax.rem(chip + i, chips)
            to(total.at[mine], total.at[mine], sg.at[x], rg.at[mine], there(x)).start()
            return c

        lax.fori_loop(1, chips, give, 0)

    def final(step, c):
        heads = [step * GROUP + h for h in range(GROUP)]
        for h in heads:
            handed_head(adjoint, h, sha, rha).wait_recv()
        adjoints = []
        for h in heads:
            end = whole(adjoint, h)
            moved = nt(split(end), split(m_sib[h, 0])) + src_next[h]
            a1 = split(jnp.where(core == 0, moved, end))
            adjoints += [split(nt(a1, get(tp, h, 1)) + src1[h]), a1]
        places_of = [(heads[h], b) for h, b in many]
        target = [hold[at] + nt(get(gp, *at), adjoints[i]) for i, at in enumerate(places_of)]
        less = [split(-x) for x in target]
        update = [get(upd, *at) for at in places_of]
        d_gram = [jnp.where(strict, nt(less[i], update[i]), 0.0) for i in range(count)]
        d_gram = [split(x + x.T) for x in d_gram]
        for i, (h, b) in enumerate(many):
            at = places_of[i]
            kn = get(knp, *at)
            grad = part[at] + nn_sum((less[i], get(sp, *at)), (d_gram[i], kn), (update[i], adjoints[i]))
            unit = joined(kn)
            grad = kinv[at] * (grad - unit * jnp.sum(unit * grad, axis=1, keepdims=True))
            gk_out[tokens(b), :, columns(heads[h])] = grad.astype(BF16).reshape(HALF, 2, DIM)
            gv_out[tokens(b), :, columns(heads[h])] = target[i].astype(BF16).reshape(HALF, 2, DIM)
        return c

    lax.fori_loop(0, steps, final, 0)

    @pl.when(lax.rem(chip, 2) == 0)
    def _():
        def gone(i, c):
            x = lax.rem(chip + i, chips)
            to(total.at[mine], total.at[mine], sg.at[x], rg.at[mine], there(x)).wait_send()
            return c

        lax.fori_loop(1, chips, gone, 0)

    def finish(i, c):
        x = lax.rem(chip + i, chips)
        to(m_out.at[x], m_all.at[x], st.at[x], rt.at[x], there(x)).wait_send()
        to(s_all.at[x], state.at[core, x], ss.at[x], rs.at[x], there(x)).wait_send()
        to(source.at[x], got.at[x], sx.at[x], rx.at[x], there(x)).wait_send()
        to(a_all.at[x], adjoint.at[core, x], sa.at[x], ra.at[x], there(x)).wait_send()
        return c

    lax.fori_loop(1, chips, finish, 0)

    def finish_hand(p, c):
        to(t_all.at[p, core], t_all.at[p, core], sf.at[p], rf.at[p], sibling).wait_send()
        return c

    lax.fori_loop(0, chips, finish_hand, 0)

    def finish_heads(h, c):
        swap(h).wait_send()
        handed_head(state, h, shs, rhs).wait_send()
        handed_head(adjoint, h, sha, rha).wait_send()
        swap_source(h).wait_send()

        @pl.when(core == 1)
        def _():
            next_source(h).wait_send()

        @pl.when(2 * h != chip)
        def _():
            to(total.at[h], total.at[h], sg.at[h], rg.at[h], there(2 * h)).wait_recv()

        return c

    lax.fori_loop(0, HEADS, finish_heads, 0)


def shape(*dims, dtype=F32):
    return jax.ShapeDtypeStruct(dims, dtype)


def layer(q, k, v, rate, cotan, gain, n, ways):
    def full(*dims):
        return pltpu.VMEM(dims, F32)

    def pair(*dims):
        return pltpu.VMEM((2, *dims), BF16)

    def dma(size):
        return pltpu.SemaphoreType.DMA((size,))

    chips = n // 2
    square = (HEADS, DIM, DIM)
    blocks = (HEADS, 2, DIM, DIM)
    thin = (HEADS, 2, HALF, DIM)
    quarter = (chips, DIM // 4, DIM)
    spread = (2, *quarter)
    noted = (DIM // 4 + 8, DIM)
    scratch = [
        full(*blocks), full(*blocks), pair(*square), pair(*square), full(*square),
        pair(*blocks), pair(*thin), full(HEADS, 2, DIM, 1), full(HEADS, 2, HALF, 1),
        pair(*blocks), full(*blocks), pair(*blocks), pair(*thin), pair(*blocks), full(*square), pair(HEADS, HALF, DIM),
        pair(*blocks), pair(*thin),
        full(chips, 96, DIM), full(chips, 96, DIM), full(chips, 2, HALF, DIM), pair(chips, DIM, DIM), full(*quarter), full(*quarter),
        full(*spread), pair(*square), full(HEADS, 2, HALF + 8, DIM), full(HEADS, HALF + 8, DIM), full(*square), full(*square),
        full(chips, *noted), full(chips, *noted), full(*quarter), full(*spread), full(ways, 8, DIM),
        pair(*blocks), pair(*blocks), full(*blocks), full(*blocks), full(*square),
    ]
    counts = [HEADS, chips, chips, chips, HEADS, HEADS, HEADS, chips, chips, HEADS, ways]
    sems = [dma(size) for size in counts for _ in range(2)] + [dma(chips), dma(HEADS)]
    wide = HEADS * DIM
    return pl.pallas_call(
        functools.partial(layer_kernel, n, ways),
        in_specs=[VMEM] * 6,
        out_specs=[VMEM] * 4,
        out_shape=[
            shape(DIM, wide, dtype=BF16),
            shape(DIM, 2, wide, dtype=BF16),
            shape(DIM, 2, wide, dtype=BF16),
            shape(HEADS, 8, DIM),
        ],
        scratch_shapes=scratch + sems,
        compiler_params=pltpu.CompilerParams(collective_id=0, has_side_effects=True, vmem_limit_bytes=LIMIT),
    )(q, k, v, rate, cotan, gain)


def on_device(queries, keys, values, betas, grad_out, gain):
    n = lax.axis_size("outer") * lax.axis_size("inner")
    ways = lax.axis_size("dp")
    rate = betas[0].transpose(0, 2, 1).reshape(HEADS, 2, DIM)
    gq, gk, gv, total = layer(queries[0], keys[0], values[0], rate, grad_out[0], gain.reshape(HEADS, 1, DIM), n, ways)
    gain_grad = total[:, 0, :].reshape(HEADS * DIM) * (1.0 / math.sqrt(DIM * n * ways))
    return gq[None], gk[None], gv[None], gain_grad


def solution(mesh):
    seq = ("outer", "inner")
    return jax.shard_map(
        on_device,
        mesh=mesh,
        in_specs=(
            P("dp", seq, None),
            P("dp", seq, None, None),
            P("dp", seq, None, None),
            P("dp", None, None, seq),
            P("dp", seq, None),
            P(),
        ),
        out_specs=(P("dp", seq, None), P("dp", seq, None, None), P("dp", seq, None, None), P()),
        check_vma=False,
    )
```

```python
import functools
import math

import jax
import jax.numpy as jnp
from jax import lax
from jax.experimental import pallas as pl
from jax.experimental.pallas import tpu as pltpu
from jax.sharding import PartitionSpec as P

HEADS = 8
DIM = 128
HALF = 64
GROUP = 4
RUN = 4
EPS_KEY = 1e-06
EPS_OUT = 1e-05
F32 = jnp.float32
BF16 = jnp.bfloat16
MESH = pl.DeviceIdType.MESH
VMEM = pl.BlockSpec(memory_space=pltpu.VMEM)
LIMIT = 48 * 1024 * 1024


def split(x):
    high = x.astype(BF16)
    return high, (x - high.astype(F32)).astype(BF16)


def raw_dot(left, right, dims):
    return lax.dot_general(left, right, (dims, ((), ())), preferred_element_type=F32)


def folded(wide):
    half = wide.shape[1] // 2
    return wide[:, :half] + wide[:, half:]


def nn(a, b):
    lhs = jnp.concatenate(a, axis=1)
    rhs = jnp.concatenate(b, axis=1)
    return folded(raw_dot(lhs, jnp.concatenate([rhs, rhs], axis=0), ((1,), (0,))))


def nt(a, b):
    lhs = jnp.concatenate(a, axis=1)
    rhs = jnp.concatenate(b, axis=0)
    return folded(raw_dot(lhs, jnp.concatenate([rhs, rhs], axis=1), ((1,), (1,))))


def tn(a, b):
    lhs = jnp.concatenate(a, axis=0)
    rhs = jnp.concatenate(b, axis=1)
    return folded(raw_dot(lhs, jnp.concatenate([rhs, rhs], axis=0), ((0,), (0,))))


def nn_sum(*terms):
    lhs = jnp.concatenate([x for a, _ in terms for x in a], axis=1)
    rhs = []
    for _, b in terms:
        rhs += [jnp.concatenate(b, axis=1)] * 2
    return folded(raw_dot(lhs, jnp.concatenate(rhs, axis=0), ((1,), (0,))))


def stacked(*pairs):
    return tuple(jnp.concatenate(part, axis=0) for part in zip(*pairs))


def beside(*pairs):
    return tuple(jnp.concatenate(part, axis=1) for part in zip(*pairs))


def inv_norm(x):
    return lax.rsqrt(jnp.sum(x * x, axis=1, keepdims=True) + EPS_KEY)


def places():
    row = lax.broadcasted_iota(jnp.int32, (DIM, DIM), 0)
    return row, lax.broadcasted_iota(jnp.int32, (DIM, DIM), 1)


def read_mask(col):
    token = lax.broadcasted_iota(jnp.int32, (HALF, DIM), 0)
    return (col[:HALF] >> 1) <= token


def put(ref, at, pair):
    ref[(0, *at)] = pair[0]
    ref[(1, *at)] = pair[1]


def get(ref, *at):
    return ref[(0, *at)], ref[(1, *at)]


def joined(pair):
    return pair[0].astype(F32) + pair[1].astype(F32)


def columns(head):
    return pl.ds(pl.multiple_of(head * DIM, DIM), DIM)


def tokens(block):
    return slice(block * HALF, (block + 1) * HALF)


def two_keys(ref, block, head):
    return ref[tokens(block), :, columns(head)].reshape(DIM, DIM)


def to(src, dst, send, recv, target):
    return pltpu.make_async_remote_copy(
        src_ref=src, dst_ref=dst, send_sem=send, recv_sem=recv, device_id=target, device_id_type=MESH
    )


def layer_kernel(
    n, ways,
    q, k, v, rate, cotan, gain,
    gq_out, gk_out, gv_out, total,
    m_dev, m_sib, q_dev, q_grp, y_dev, knp, qnp, kinv, qinv, wp, u, gp, zp, tp, o_blk, qep, xbp, scp,
    m_out, m_all, t_all, runs, local, s_all, state, dop, src_two, src_got, src_own, src_next, source, got, a_all, adjoint, g_all,
    sp, upd, part, hold, src1,
    sw, rw, st, rt, sf, rf, ss, rs, shs, rhs, sy, ry, so, ro, sx, rx, sa, ra, sha, rha, sd, rd, sg, rg,
):
    core = lax.axis_index("inner")
    chip = lax.axis_index("outer")
    chips = n // 2
    mine = lax.div(chip, 2)
    dp = lax.axis_index("dp")
    sibling = {"inner": 1 - core}
    steps = HEADS // GROUP
    quarter = DIM // 4

    def there(x):
        return {"outer": x}

    barrier = pltpu.get_barrier_semaphore()

    def tell(i, c):
        pl.semaphore_signal(barrier, inc=1, device_id=there(lax.rem(chip + i, chips)), device_id_type=MESH)
        return c

    lax.fori_loop(1, chips, tell, 0)
    pl.semaphore_signal(barrier, inc=1, device_id=sibling, device_id_type=MESH)
    for i in range(1, ways):
        pl.semaphore_signal(barrier, inc=1, device_id={"dp": lax.rem(dp + i, ways)}, device_id_type=MESH)

    row, col = places()
    eye = row == col
    strict = col < row
    reads = read_mask(col)
    many = [(h, b) for h in range(GROUP) for b in range(2)]
    count = len(many)
    one = jnp.where(eye, 1.0, 0.0)

    def level(s):
        shift = s.bit_length() - 1
        rb, cb = row >> shift, col >> shift
        return ((rb >> 1) == (cb >> 1)) & ((rb & 1) == 1) & ((cb & 1) == 0)

    def masked(pair, mask):
        return tuple(jnp.where(mask, x.astype(F32), 0.0).astype(BF16) for x in pair)

    def turn(step):
        first = lax.rem(step + chip, steps) * GROUP
        return [first + h for h in range(GROUP)]

    def swap(h):
        return to(m_dev.at[h], m_sib.at[h], sw.at[h], rw.at[h], sibling)

    def chip_maps(step):
        heads = turn(step)
        half = pl.ds(pl.multiple_of(core * HALF, HALF), HALF)
        lead = core == 0
        for h in heads:
            swap(h).wait_recv()
        rows, later, offs = [], [], []
        for h in heads:
            begin = [jnp.where(lead, m_dev[h, j, half], m_sib[h, j, half]) for j in range(2)]
            rows.append(split(jnp.concatenate(begin, axis=0)))
            later.append(split(jnp.where(lead, m_sib[h, 0], m_dev[h, 0])))
            offs.append(jnp.where(lead, m_sib[h, 1, half], m_dev[h, 1, half]))
        made = [nn(rows[i], later[i]) for i in range(GROUP)]
        for i, h in enumerate(heads):
            off = made[i][HALF:] + offs[i]
            for e in range(2):
                x = 2 * h + e
                m_out[x, :HALF] = made[i][:HALF]
                m_out[x, HALF:] = off[e * quarter : (e + 1) * quarter]

                @pl.when(x != chip)
                def _():
                    to(m_out.at[x], m_all.at[chip], st.at[x], rt.at[chip], there(x)).start()

    def query_side(step):
        heads = [step * GROUP + h for h in range(GROUP)]
        zero = jnp.zeros((DIM, DIM), BF16)
        scaled = [get(xbp, heads[h], b) for h, b in many]
        keys = [get(knp, heads[h], b) for h, b in many]
        pack = [beside(keys[i], (two_keys(v, b, heads[h]), zero)) for i, (h, b) in enumerate(many)]
        z = [split(nn(get(scp, heads[h], b), scaled[i])) for i, (h, b) in enumerate(many)]
        zr = [nn(z[i], pack[i]) for i in range(count)]
        qe = [joined(get(qnp, heads[h], b)) - zr[i][:, :DIM] for i, (h, b) in enumerate(many)]
        for i, (h, b) in enumerate(many):
            put(gp, (heads[h], b), split(tn(scaled[i], keys[i])))
            put(zp, (heads[h], b), z[i])
        for h in range(GROUP):
            a, b = 2 * h, 2 * h + 1
            later = split(qe[b])
            back = nt(later, stacked(get(tp, heads[h], 0), split(o_blk[heads[h]])))
            for ref in (q_dev, q_grp):
                put(ref, (heads[h], slice(0, HALF)), split(qe[a]))
                put(ref, (heads[h], slice(HALF, DIM)), split(back[:, :DIM]))
            y_dev[heads[h], :HALF] = zr[a][:, DIM:]
            y_dev[heads[h], HALF:] = zr[b][:, DIM:] + back[:, DIM:]
            put(qep, (heads[h],), later)

        @pl.when(core == 1)
        def _():
            before = [stacked(split(m_sib[h, 0]), split(m_sib[h, 1])) for h in heads]
            back = [nt(get(q_dev, h), before[i]) for i, h in enumerate(heads)]
            for i, h in enumerate(heads):
                put(q_grp, (h,), split(back[i][:, :DIM]))
                y_dev[h] = y_dev[h] + back[i][:, DIM:]

    def maps(step, c):
        heads = turn(step)
        keys, vals, queries, ratecol, raterow = [], [], [], [], []
        for h, b in many:
            kr = two_keys(k, b, heads[h]).astype(F32)
            inv = inv_norm(kr)
            kinv[heads[h], b] = inv
            keys.append(split(kr * inv))
            put(knp, (heads[h], b), keys[-1])
            vals.append(two_keys(v, b, heads[h]))
            qr = q[tokens(b), columns(heads[h])].astype(F32)
            inv = inv_norm(qr)
            qinv[heads[h], b] = inv
            queries.append(split(qr * inv))
            put(qnp, (heads[h], b), queries[-1])
            r = rate[heads[h], b : b + 1, :]
            raterow.append(r)
            ratecol.append(jnp.sum(jnp.where(eye, r, 0.0), axis=1, keepdims=True))
        both = [nt(stacked(keys[i], queries[i]), keys[i]) for i in range(count)]
        lower = [jnp.where(strict, ratecol[i] * both[i][:DIM], 0.0) for i in range(count)]
        scores = [split(jnp.where(reads, both[i][DIM:], 0.0)) for i in range(count)]
        first = level(1)
        inverse = [one - jnp.where(first, lower[i], 0.0) for i in range(count)]
        lower = [split(x) for x in lower]
        s = 2
        while s < DIM:
            mask = level(s)
            halves = [split(x) for x in inverse]
            inner = [split(nn(masked(lower[i], mask), halves[i])) for i in range(count)]
            inverse = [inverse[i] - nn(halves[i], inner[i]) for i in range(count)]
            s *= 2
        scaled = [split(inverse[i] * raterow[i]) for i in range(count)]
        zero = jnp.zeros((DIM, DIM), BF16)
        pack = [beside(keys[i], (vals[i], zero)) for i in range(count)]
        solved = [nn(scaled[i], pack[i]) for i in range(count)]
        solved_p = [split(x) for x in solved]
        move = [tn(solved_p[i], keys[i]) for i in range(count)]
        trans = [one - move[i][:DIM] for i in range(count)]
        offs = [move[i][DIM:] for i in range(count)]
        trans_p = [split(x) for x in trans]
        offs_p = [split(x) for x in offs]
        for i, (h, b) in enumerate(many):
            put(wp, (heads[h], b), tuple(x[:, :DIM] for x in solved_p[i]))
            u[heads[h], b] = solved[i][:, DIM:]
            put(xbp, (heads[h], b), scaled[i])
            put(scp, (heads[h], b), scores[i])
            put(tp, (heads[h], b), trans_p[i])
        for h in range(GROUP):
            a, b = 2 * h, 2 * h + 1
            through = nn(stacked(trans_p[a], offs_p[a]), trans_p[b])
            m_dev[heads[h], 0] = through[:DIM]
            m_dev[heads[h], 1] = through[DIM:] + offs[b]
            o_blk[heads[h]] = offs[a]

        @pl.when(step == 0)
        def _():
            pl.semaphore_wait(barrier, chips + ways - 1)

        for h in heads:
            swap(h).start()

        @pl.when(step > 0)
        def _():
            chip_maps(step - 1)

        return c

    lax.fori_loop(0, steps, maps, 0)
    chip_maps(steps - 1)
    m_all[chip] = m_out[chip]

    def deferred(step, c):
        query_side(step)
        return c

    lax.fori_loop(0, steps // 2, deferred, 0)

    def hand_over(i, c):
        p = lax.rem(chip - i + chips, chips)

        @pl.when(p != chip)
        def _():
            to(m_out.at[0], m_all.at[p], st.at[p], rt.at[p], there(p)).wait_recv()

        t_all[p, core] = m_all[p, :HALF]
        to(t_all.at[p, core], t_all.at[p, core], sf.at[p], rf.at[p], sibling).start()
        return c

    lax.fori_loop(0, chips, hand_over, 0)
    lax.fori_loop(steps // 2, steps, deferred, 0)

    def handed(i, c):
        p = lax.rem(chip - i + chips, chips)
        to(t_all.at[p, core], t_all.at[p, 1 - core], sf.at[p], rf.at[p], sibling).wait_recv()
        return c

    lax.fori_loop(0, chips, handed, 0)

    groups = chips // RUN
    bases = [g * RUN for g in range(groups)]

    def transit(p):
        return split(t_all[p].reshape(DIM, DIM))

    trans = [transit(p) for p in bases]
    offs = [m_all[p, HALF:] for p in bases]
    for g, p in enumerate(bases):
        put(runs, (p,), trans[g])
        local[p] = offs[g]
    trans = [stacked(trans[g], split(offs[g])) for g in range(groups)]
    for j in range(1, RUN):
        new = [nn(trans[g], transit(p + j)) for g, p in enumerate(bases)]
        for g, p in enumerate(bases):
            offs[g] = new[g][DIM:] + m_all[p + j, HALF:]
            local[p + j] = offs[g]
            trans[g] = split(jnp.concatenate([new[g][:DIM], offs[g]], axis=0))
            put(runs, (p + j,), tuple(x[:DIM] for x in trans[g]))

    def tell_state(p, now):
        s_all[p] = now

        @pl.when(p != chip)
        def _():
            to(s_all.at[p], state.at[core, chip], ss.at[p], rs.at[chip], there(p)).start()

    def walk(g, now):
        base = g * RUN
        tell_state(base, now)
        halves = split(now)
        new = [nn(halves, get(runs, base + j)) + local[base + j] for j in range(RUN)]
        for j in range(RUN - 1):
            tell_state(base + j + 1, new[j])
        return new[RUN - 1]

    lax.fori_loop(0, groups, walk, jnp.zeros((quarter, DIM), F32))
    state[core, chip] = s_all[chip]

    last = [transit(p + RUN - 1) for p in bases]
    for g, p in enumerate(bases):
        put(runs, (p + RUN - 2,), last[g])
    for j in range(RUN - 2, 0, -1):
        last = [split(nn(transit(p + j), last[g])) for g, p in enumerate(bases)]
        for g, p in enumerate(bases):
            put(runs, (p + j - 1,), last[g])

    def arrive(ref, sent, send, recv, hand_send, hand_recv):
        def one_head(h, c):
            for e in range(2):
                x = 2 * h + e

                @pl.when(x != chip)
                def _():
                    to(sent.at[x], ref.at[core, x], send.at[x], recv.at[x], there(x)).wait_recv()

            at = pl.ds(2 * h, 2)
            to(ref.at[core, at], ref.at[core, at], hand_send.at[h], hand_recv.at[h], sibling).start()
            return c

        lax.fori_loop(0, HEADS, one_head, 0)

    def handed_head(ref, h, hand_send, hand_recv):
        at = pl.ds(2 * h, 2)
        return to(ref.at[core, at], ref.at[1 - core, at], hand_send.at[h], hand_recv.at[h], sibling)

    def whole(ref, h):
        return jnp.concatenate([ref[c, pl.ds(2 * h, 2)].reshape(HALF, DIM) for c in range(2)], axis=0)

    arrive(state, s_all, ss, rs, shs, rhs)

    def swap_source(h):
        return to(src_two.at[h, 1 - core], src_got.at[h], sy.at[h], ry.at[h], sibling)

    def next_source(h):
        return to(src_own.at[h], src_next.at[h], so.at[h], ro.at[h], sibling)

    def chip_source(h):
        swap_source(h).wait_recv()
        both = src_two[h, core] + src_got[h]
        for e in range(2):
            x = 2 * h + e
            source[x, :quarter] = both[e * quarter : (e + 1) * quarter]
            source[x, quarter:] = both[HALF:]

            @pl.when(x != chip)
            def _():
                to(source.at[x], got.at[chip], sx.at[x], rx.at[chip], there(x)).start()

    def middle(step, c):
        heads = [step * GROUP + h for h in range(GROUP)]
        for h in heads:
            handed_head(state, h, shs, rhs).wait_recv()
        qd = [get(q_grp, h) for h in heads]
        outs = [nt(qd[i], split(whole(state, h))) + y_dev[h] for i, h in enumerate(heads)]
        for i, h in enumerate(heads):
            out = outs[i]
            cot = cotan[:, columns(h)].astype(F32)
            scale = lax.rsqrt(jnp.mean(out * out, axis=1, keepdims=True) + EPS_OUT)
            normed = out * scale
            scaled = cot * gain[h]
            grad = scale * (scaled - normed * jnp.mean(normed * scaled, axis=1, keepdims=True))
            halves = split(grad)
            put(dop, (h,), halves)
            src = tn(halves, qd[i])
            gains = jnp.broadcast_to(jnp.sum(cot * normed, axis=0, keepdims=True), (8, DIM))
            for j in range(2):
                src_two[h, j, :HALF] = src[j * HALF : (j + 1) * HALF]
                src_two[h, j, HALF:] = gains
            swap_source(h).start()

        @pl.when(step > 0)
        def _():
            for h in heads:
                chip_source(h - GROUP)

        return c

    lax.fori_loop(0, steps, middle, 0)

    for h in range(HEADS - GROUP, HEADS):
        chip_source(h)
    got[chip] = source[chip]

    @pl.when(core == 1)
    def _():
        def own(step, c):
            for h in [step * GROUP + h for h in range(GROUP)]:
                src_own[h] = tn(get(dop, h), get(q_dev, h))
                next_source(h).start()
            return c

        lax.fori_loop(0, steps, own, 0)

    def by_states(step, c):
        heads = [step * GROUP + h for h in range(GROUP)]
        states, do = [], []
        for h in heads:
            begin = whole(state, h)
            moved = nn(split(begin), split(m_sib[h, 0])) + m_sib[h, 1]
            s0 = split(jnp.where(core == 0, begin, moved))
            s1 = split(nn(s0, get(tp, h, 0)) + o_blk[h])
            do0, do1 = get(dop, h, slice(0, HALF)), get(dop, h, slice(HALF, DIM))
            states += [s0, s1]
            do += [do0, do1]
            src1[h] = tn(do1, get(qep, h))
        update = [split(u[heads[h], b] - nt(get(wp, heads[h], b), states[i])) for i, (h, b) in enumerate(many)]
        d_scores = [split(jnp.where(reads, nt(do[i], update[i]), 0.0)) for i in range(count)]
        for i, (h, b) in enumerate(many):
            at = (heads[h], b)
            put(sp, at, states[i])
            put(upd, at, update[i])
            hold[at] = tn(get(zp, *at), do[i])
            qn = get(qnp, *at)
            part[at] = tn(d_scores[i], qn)
            grad = nn_sum((do[i], states[i]), (d_scores[i], get(knp, *at)))
            unit = joined(qn)
            grad = qinv[at] * (grad - unit * jnp.sum(unit * grad, axis=1, keepdims=True))
            gq_out[tokens(b), columns(heads[h])] = grad.astype(BF16)
        return c

    lax.fori_loop(0, steps, by_states, 0)

    def source_here(i, gains):
        p = chips - 1 - i

        @pl.when(p != chip)
        def _():
            to(source.at[0], got.at[p], sx.at[p], rx.at[p], there(p)).wait_recv()

        return gains + got[p, quarter:]

    gains = lax.fori_loop(0, chips, source_here, jnp.zeros((8, DIM), F32))
    g_all[dp] = gains
    for i in range(1, ways):
        other = lax.rem(dp + i, ways)
        to(g_all.at[dp], g_all.at[dp], sd.at[other], rd.at[dp], {"dp": other}).start()

    now = [got[p + RUN - 1, :quarter] for p in bases]
    for g, p in enumerate(bases):
        local[p + RUN - 1] = now[g]
    for j in range(RUN - 1, 0, -1):
        new = [nt(split(now[g]), transit(p + j - 1)) for g, p in enumerate(bases)]
        now = [new[g] + got[p + j - 1, :quarter] for g, p in enumerate(bases)]
        for g, p in enumerate(bases):
            local[p + j - 1] = now[g]

    def tell_adjoint(p, now):
        a_all[p] = now

        @pl.when(p != chip)
        def _():
            to(a_all.at[p], adjoint.at[core, chip], sa.at[p], ra.at[chip], there(p)).start()

    def walk_back(i, now):
        base = (groups - 1 - i) * RUN
        tell_adjoint(base + RUN - 1, now)
        halves = split(now)
        new = [nt(halves, get(runs, base + j)) for j in range(RUN)]
        for j in range(RUN - 2, -1, -1):
            tell_adjoint(base + j, new[j] + local[base + j + 1])
        return new[RUN - 1] + local[base]

    lax.fori_loop(0, groups, walk_back, jnp.zeros((quarter, DIM), F32))
    adjoint[core, chip] = a_all[chip]

    @pl.when(core == 0)
    def _():
        def came(h, c):
            next_source(h).wait_recv()
            return c

        lax.fori_loop(0, HEADS, came, 0)

    arrive(adjoint, a_all, sa, ra, sha, rha)

    for i in range(1, ways):
        other = lax.rem(dp + i, ways)
        to(g_all.at[other], g_all.at[other], sd.at[other], rd.at[other], {"dp": other}).wait()

    @pl.when(lax.rem(chip, 2) == 0)
    def _():
        summed = g_all[0]
        for i in range(1, ways):
            summed = summed + g_all[i]
        total[mine] = summed

        def give(i, c):
            x = lax.rem(chip + i, chips)
            to(total.at[mine], total.at[mine], sg.at[x], rg.at[mine], there(x)).start()
            return c

        lax.fori_loop(1, chips, give, 0)

    def final(step, c):
        heads = [step * GROUP + h for h in range(GROUP)]
        for h in heads:
            handed_head(adjoint, h, sha, rha).wait_recv()
        adjoints = []
        for h in heads:
            end = whole(adjoint, h)
            moved = nt(split(end), split(m_sib[h, 0])) + src_next[h]
            a1 = split(jnp.where(core == 0, moved, end))
            adjoints += [split(nt(a1, get(tp, h, 1)) + src1[h]), a1]
        places_of = [(heads[h], b) for h, b in many]
        target = [hold[at] + nt(get(gp, *at), adjoints[i]) for i, at in enumerate(places_of)]
        less = [split(-x) for x in target]
        update = [get(upd, *at) for at in places_of]
        d_gram = [jnp.where(strict, nt(less[i], update[i]), 0.0) for i in range(count)]
        d_gram = [split(x + x.T) for x in d_gram]
        for i, (h, b) in enumerate(many):
            at = places_of[i]
            kn = get(knp, *at)
            grad = part[at] + nn_sum((less[i], get(sp, *at)), (d_gram[i], kn), (update[i], adjoints[i]))
            unit = joined(kn)
            grad = kinv[at] * (grad - unit * jnp.sum(unit * grad, axis=1, keepdims=True))
            gk_out[tokens(b), :, columns(heads[h])] = grad.astype(BF16).reshape(HALF, 2, DIM)
            gv_out[tokens(b), :, columns(heads[h])] = target[i].astype(BF16).reshape(HALF, 2, DIM)
        return c

    lax.fori_loop(0, steps, final, 0)

    @pl.when(lax.rem(chip, 2) == 0)
    def _():
        def gone(i, c):
            x = lax.rem(chip + i, chips)
            to(total.at[mine], total.at[mine], sg.at[x], rg.at[mine], there(x)).wait_send()
            return c

        lax.fori_loop(1, chips, gone, 0)

    def finish(i, c):
        x = lax.rem(chip + i, chips)
        to(m_out.at[x], m_all.at[x], st.at[x], rt.at[x], there(x)).wait_send()
        to(s_all.at[x], state.at[core, x], ss.at[x], rs.at[x], there(x)).wait_send()
        to(source.at[x], got.at[x], sx.at[x], rx.at[x], there(x)).wait_send()
        to(a_all.at[x], adjoint.at[core, x], sa.at[x], ra.at[x], there(x)).wait_send()
        return c

    lax.fori_loop(1, chips, finish, 0)

    def finish_hand(p, c):
        to(t_all.at[p, core], t_all.at[p, core], sf.at[p], rf.at[p], sibling).wait_send()
        return c

    lax.fori_loop(0, chips, finish_hand, 0)

    def finish_heads(h, c):
        swap(h).wait_send()
        handed_head(state, h, shs, rhs).wait_send()
        handed_head(adjoint, h, sha, rha).wait_send()
        swap_source(h).wait_send()

        @pl.when(core == 1)
        def _():
            next_source(h).wait_send()

        @pl.when(2 * h != chip)
        def _():
            to(total.at[h], total.at[h], sg.at[h], rg.at[h], there(2 * h)).wait_recv()

        return c

    lax.fori_loop(0, HEADS, finish_heads, 0)


def shape(*dims, dtype=F32):
    return jax.ShapeDtypeStruct(dims, dtype)


def layer(q, k, v, rate, cotan, gain, n, ways):
    def full(*dims):
        return pltpu.VMEM(dims, F32)

    def pair(*dims):
        return pltpu.VMEM((2, *dims), BF16)

    def dma(size):
        return pltpu.SemaphoreType.DMA((size,))

    chips = n // 2
    square = (HEADS, DIM, DIM)
    blocks = (HEADS, 2, DIM, DIM)
    thin = (HEADS, 2, HALF, DIM)
    quarter = (chips, DIM // 4, DIM)
    spread = (2, *quarter)
    noted = (DIM // 4 + 8, DIM)
    scratch = [
        full(*blocks), full(*blocks), pair(*square), pair(*square), full(*square),
        pair(*blocks), pair(*thin), full(HEADS, 2, DIM, 1), full(HEADS, 2, HALF, 1),
        pair(*blocks), full(*blocks), pair(*blocks), pair(*thin), pair(*blocks), full(*square), pair(HEADS, HALF, DIM),
        pair(*blocks), pair(*thin),
        full(chips, 96, DIM), full(chips, 96, DIM), full(chips, 2, HALF, DIM), pair(chips, DIM, DIM), full(*quarter), full(*quarter),
        full(*spread), pair(*square), full(HEADS, 2, HALF + 8, DIM), full(HEADS, HALF + 8, DIM), full(*square), full(*square),
        full(chips, *noted), full(chips, *noted), full(*quarter), full(*spread), full(ways, 8, DIM),
        pair(*blocks), pair(*blocks), full(*blocks), full(*blocks), full(*square),
    ]
    counts = [HEADS, chips, chips, chips, HEADS, HEADS, HEADS, chips, chips, HEADS, ways]
    sems = [dma(size) for size in counts for _ in range(2)] + [dma(chips), dma(HEADS)]
    wide = HEADS * DIM
    return pl.pallas_call(
        functools.partial(layer_kernel, n, ways),
        in_specs=[VMEM] * 6,
        out_specs=[VMEM] * 4,
        out_shape=[
            shape(DIM, wide, dtype=BF16),
            shape(DIM, 2, wide, dtype=BF16),
            shape(DIM, 2, wide, dtype=BF16),
            shape(HEADS, 8, DIM),
        ],
        scratch_shapes=scratch + sems,
        compiler_params=pltpu.CompilerParams(collective_id=0, has_side_effects=True, vmem_limit_bytes=LIMIT),
    )(q, k, v, rate, cotan, gain)


def on_device(queries, keys, values, betas, grad_out, gain):
    n = lax.axis_size("outer") * lax.axis_size("inner")
    ways = lax.axis_size("dp")
    rate = betas[0].transpose(0, 2, 1).reshape(HEADS, 2, DIM)
    gq, gk, gv, total = layer(queries[0], keys[0], values[0], rate, grad_out[0], gain.reshape(HEADS, 1, DIM), n, ways)
    gain_grad = total[:, 0, :].reshape(HEADS * DIM) * (1.0 / math.sqrt(DIM * n * ways))
    return gq[None], gk[None], gv[None], gain_grad


def solution(mesh):
    seq = ("outer", "inner")
    return jax.shard_map(
        on_device,
        mesh=mesh,
        in_specs=(
            P("dp", seq, None),
            P("dp", seq, None, None),
            P("dp", seq, None, None),
            P("dp", None, None, seq),
            P("dp", seq, None),
            P(),
        ),
        out_specs=(P("dp", seq, None), P("dp", seq, None, None), P("dp", seq, None, None), P()),
        check_vma=False,
    )
```

```python
import functools
import math

import jax
import jax.numpy as jnp
from jax import lax
from jax.experimental import pallas as pl
from jax.experimental.pallas import tpu as pltpu
from jax.sharding import PartitionSpec as P

HEADS = 8
DIM = 128
HALF = 64
GROUP = 4
RUN = 4
EPS_KEY = 1e-06
EPS_OUT = 1e-05
F32 = jnp.float32
BF16 = jnp.bfloat16
MESH = pl.DeviceIdType.MESH
VMEM = pl.BlockSpec(memory_space=pltpu.VMEM)
FAR = pl.BlockSpec(memory_space=pltpu.HBM)
LIMIT = 62 * 1024 * 1024


def split(x):
    high = x.astype(BF16)
    return high, (x - high.astype(F32)).astype(BF16)


def raw_dot(left, right, dims):
    return lax.dot_general(left, right, (dims, ((), ())), preferred_element_type=F32)


def folded(wide):
    half = wide.shape[1] // 2
    return wide[:, :half] + wide[:, half:]


def nn(a, b):
    lhs = jnp.concatenate(a, axis=1)
    rhs = jnp.concatenate(b, axis=1)
    return folded(raw_dot(lhs, jnp.concatenate([rhs, rhs], axis=0), ((1,), (0,))))


def nt(a, b):
    lhs = jnp.concatenate(a, axis=1)
    rhs = jnp.concatenate(b, axis=0)
    return folded(raw_dot(lhs, jnp.concatenate([rhs, rhs], axis=1), ((1,), (1,))))


def tn(a, b):
    lhs = jnp.concatenate(a, axis=0)
    rhs = jnp.concatenate(b, axis=1)
    return folded(raw_dot(lhs, jnp.concatenate([rhs, rhs], axis=0), ((0,), (0,))))


def nn_sum(*terms):
    lhs = jnp.concatenate([x for a, _ in terms for x in a], axis=1)
    rhs = []
    for _, b in terms:
        rhs += [jnp.concatenate(b, axis=1)] * 2
    return folded(raw_dot(lhs, jnp.concatenate(rhs, axis=0), ((1,), (0,))))


def stacked(*pairs):
    return tuple(jnp.concatenate(part, axis=0) for part in zip(*pairs))


def beside(*pairs):
    return tuple(jnp.concatenate(part, axis=1) for part in zip(*pairs))


def inv_norm(x):
    return lax.rsqrt(jnp.sum(x * x, axis=1, keepdims=True) + EPS_KEY)


def places():
    row = lax.broadcasted_iota(jnp.int32, (DIM, DIM), 0)
    return row, lax.broadcasted_iota(jnp.int32, (DIM, DIM), 1)


def read_mask(col):
    token = lax.broadcasted_iota(jnp.int32, (HALF, DIM), 0)
    return (col[:HALF] >> 1) <= token


def put(ref, at, pair):
    ref[(0, *at)] = pair[0]
    ref[(1, *at)] = pair[1]


def get(ref, *at):
    return ref[(0, *at)], ref[(1, *at)]


def joined(pair):
    return pair[0].astype(F32) + pair[1].astype(F32)


def columns(head):
    return pl.ds(pl.multiple_of(head * DIM, DIM), DIM)


def tokens(block):
    return slice(block * HALF, (block + 1) * HALF)


def two_keys(ref, block, head):
    return ref[tokens(block), :, columns(head)].reshape(DIM, DIM)


def to(src, dst, send, recv, target):
    return pltpu.make_async_remote_copy(
        src_ref=src, dst_ref=dst, send_sem=send, recv_sem=recv, device_id=target, device_id_type=MESH
    )


def layer_kernel(
    n, ways,
    q_far, k_far, v_far, rate, cotan_far, gain,
    gq_far, gk_far, gv_far, total,
    q, k, v, cotan, gq_out, gk_out, gv_out,
    m_dev, m_sib, q_dev, q_grp, y_dev, knp, qnp, kinv, qinv, wp, u, gp, zp, tp, o_blk, qep, xbp, scp,
    m_out, m_all, t_all, runs, local, s_all, state, dop, src_two, src_got, src_own, src_next, source, got, a_all, adjoint, g_all,
    sp, upd, part, hold, src1,
    sw, rw, st, rt, sf, rf, ss, rs, shs, rhs, sy, ry, so, ro, sx, rx, sa, ra, sha, rha, sd, rd, sg, rg, fetched, stored,
):
    core = lax.axis_index("inner")
    chip = lax.axis_index("outer")
    chips = n // 2
    mine = lax.div(chip, 2)
    dp = lax.axis_index("dp")
    sibling = {"inner": 1 - core}
    steps = HEADS // GROUP
    quarter = DIM // 4

    def there(x):
        return {"outer": x}

    far = ((k_far, k), (q_far, q), (v_far, v), (cotan_far, cotan))
    fetch = [pltpu.make_async_copy(src, dst, fetched.at[i]) for i, (src, dst) in enumerate(far)]
    for copy in fetch:
        copy.start()
    barrier = pltpu.get_barrier_semaphore()

    def tell(i, c):
        pl.semaphore_signal(barrier, inc=1, device_id=there(lax.rem(chip + i, chips)), device_id_type=MESH)
        return c

    lax.fori_loop(1, chips, tell, 0)
    pl.semaphore_signal(barrier, inc=1, device_id=sibling, device_id_type=MESH)
    for i in range(1, ways):
        pl.semaphore_signal(barrier, inc=1, device_id={"dp": lax.rem(dp + i, ways)}, device_id_type=MESH)

    row, col = places()
    eye = row == col
    strict = col < row
    reads = read_mask(col)
    many = [(h, b) for h in range(GROUP) for b in range(2)]
    count = len(many)
    one = jnp.where(eye, 1.0, 0.0)

    def level(s):
        shift = s.bit_length() - 1
        rb, cb = row >> shift, col >> shift
        return ((rb >> 1) == (cb >> 1)) & ((rb & 1) == 1) & ((cb & 1) == 0)

    def masked(pair, mask):
        return tuple(jnp.where(mask, x.astype(F32), 0.0).astype(BF16) for x in pair)

    def turn(step):
        first = lax.rem(step + chip, steps) * GROUP
        return [first + h for h in range(GROUP)]

    def swap(h):
        return to(m_dev.at[h], m_sib.at[h], sw.at[h], rw.at[h], sibling)

    def chip_maps(step):
        heads = turn(step)
        half = pl.ds(pl.multiple_of(core * HALF, HALF), HALF)
        lead = core == 0
        for h in heads:
            swap(h).wait_recv()
        rows, later, offs = [], [], []
        for h in heads:
            begin = [jnp.where(lead, m_dev[h, j, half], m_sib[h, j, half]) for j in range(2)]
            rows.append(split(jnp.concatenate(begin, axis=0)))
            later.append(split(jnp.where(lead, m_sib[h, 0], m_dev[h, 0])))
            offs.append(jnp.where(lead, m_sib[h, 1, half], m_dev[h, 1, half]))
        made = [nn(rows[i], later[i]) for i in range(GROUP)]
        for i, h in enumerate(heads):
            off = made[i][HALF:] + offs[i]
            for e in range(2):
                x = 2 * h + e
                m_out[x, :HALF] = made[i][:HALF]
                m_out[x, HALF:] = off[e * quarter : (e + 1) * quarter]

                @pl.when(x != chip)
                def _():
                    to(m_out.at[x], m_all.at[chip], st.at[x], rt.at[chip], there(x)).start()

    def query_side(step):
        heads = [step * GROUP + h for h in range(GROUP)]
        zero = jnp.zeros((DIM, DIM), BF16)
        scaled = [get(xbp, heads[h], b) for h, b in many]
        keys = [get(knp, heads[h], b) for h, b in many]
        pack = [beside(keys[i], (two_keys(v, b, heads[h]), zero)) for i, (h, b) in enumerate(many)]
        z = [split(nn(get(scp, heads[h], b), scaled[i])) for i, (h, b) in enumerate(many)]
        zr = [nn(z[i], pack[i]) for i in range(count)]
        qe = [joined(get(qnp, heads[h], b)) - zr[i][:, :DIM] for i, (h, b) in enumerate(many)]
        for i, (h, b) in enumerate(many):
            put(gp, (heads[h], b), split(tn(scaled[i], keys[i])))
            put(zp, (heads[h], b), z[i])
        for h in range(GROUP):
            a, b = 2 * h, 2 * h + 1
            later = split(qe[b])
            back = nt(later, stacked(get(tp, heads[h], 0), split(o_blk[heads[h]])))
            for ref in (q_dev, q_grp):
                put(ref, (heads[h], slice(0, HALF)), split(qe[a]))
                put(ref, (heads[h], slice(HALF, DIM)), split(back[:, :DIM]))
            y_dev[heads[h], :HALF] = zr[a][:, DIM:]
            y_dev[heads[h], HALF:] = zr[b][:, DIM:] + back[:, DIM:]
            put(qep, (heads[h],), later)

        @pl.when(core == 1)
        def _():
            before = [stacked(split(m_sib[h, 0]), split(m_sib[h, 1])) for h in heads]
            back = [nt(get(q_dev, h), before[i]) for i, h in enumerate(heads)]
            for i, h in enumerate(heads):
                put(q_grp, (h,), split(back[i][:, :DIM]))
                y_dev[h] = y_dev[h] + back[i][:, DIM:]

    def maps(step, c):
        heads = turn(step)
        keys, vals, queries, ratecol, raterow = [], [], [], [], []
        for h, b in many:
            kr = two_keys(k, b, heads[h]).astype(F32)
            inv = inv_norm(kr)
            kinv[heads[h], b] = inv
            keys.append(split(kr * inv))
            put(knp, (heads[h], b), keys[-1])
            vals.append(two_keys(v, b, heads[h]))
            qr = q[tokens(b), columns(heads[h])].astype(F32)
            inv = inv_norm(qr)
            qinv[heads[h], b] = inv
            queries.append(split(qr * inv))
            put(qnp, (heads[h], b), queries[-1])
            r = rate[heads[h], b : b + 1, :]
            raterow.append(r)
            ratecol.append(jnp.sum(jnp.where(eye, r, 0.0), axis=1, keepdims=True))
        both = [nt(stacked(keys[i], queries[i]), keys[i]) for i in range(count)]
        lower = [jnp.where(strict, ratecol[i] * both[i][:DIM], 0.0) for i in range(count)]
        scores = [split(jnp.where(reads, both[i][DIM:], 0.0)) for i in range(count)]
        first = level(1)
        inverse = [one - jnp.where(first, lower[i], 0.0) for i in range(count)]
        lower = [split(x) for x in lower]
        s = 2
        while s < DIM:
            mask = level(s)
            halves = [split(x) for x in inverse]
            inner = [split(nn(masked(lower[i], mask), halves[i])) for i in range(count)]
            inverse = [inverse[i] - nn(halves[i], inner[i]) for i in range(count)]
            s *= 2
        scaled = [split(inverse[i] * raterow[i]) for i in range(count)]
        zero = jnp.zeros((DIM, DIM), BF16)
        pack = [beside(keys[i], (vals[i], zero)) for i in range(count)]
        solved = [nn(scaled[i], pack[i]) for i in range(count)]
        solved_p = [split(x) for x in solved]
        move = [tn(solved_p[i], keys[i]) for i in range(count)]
        trans = [one - move[i][:DIM] for i in range(count)]
        offs = [move[i][DIM:] for i in range(count)]
        trans_p = [split(x) for x in trans]
        offs_p = [split(x) for x in offs]
        for i, (h, b) in enumerate(many):
            put(wp, (heads[h], b), tuple(x[:, :DIM] for x in solved_p[i]))
            u[heads[h], b] = solved[i][:, DIM:]
            put(xbp, (heads[h], b), scaled[i])
            put(scp, (heads[h], b), scores[i])
            put(tp, (heads[h], b), trans_p[i])
        for h in range(GROUP):
            a, b = 2 * h, 2 * h + 1
            through = nn(stacked(trans_p[a], offs_p[a]), trans_p[b])
            m_dev[heads[h], 0] = through[:DIM]
            m_dev[heads[h], 1] = through[DIM:] + offs[b]
            o_blk[heads[h]] = offs[a]

        @pl.when(step == 0)
        def _():
            pl.semaphore_wait(barrier, chips + ways - 1)

        for h in heads:
            swap(h).start()

        @pl.when(step > 0)
        def _():
            chip_maps(step - 1)

        return c

    for copy in fetch[:3]:
        copy.wait()
    lax.fori_loop(0, steps, maps, 0)
    chip_maps(steps - 1)
    m_all[chip] = m_out[chip]

    def deferred(step, c):
        query_side(step)
        return c

    lax.fori_loop(0, steps // 2, deferred, 0)

    def hand_over(i, c):
        p = lax.rem(chip - i + chips, chips)

        @pl.when(p != chip)
        def _():
            to(m_out.at[0], m_all.at[p], st.at[p], rt.at[p], there(p)).wait_recv()

        t_all[p, core] = m_all[p, :HALF]
        to(t_all.at[p, core], t_all.at[p, core], sf.at[p], rf.at[p], sibling).start()
        return c

    lax.fori_loop(0, chips, hand_over, 0)
    lax.fori_loop(steps // 2, steps, deferred, 0)

    def handed(i, c):
        p = lax.rem(chip - i + chips, chips)
        to(t_all.at[p, core], t_all.at[p, 1 - core], sf.at[p], rf.at[p], sibling).wait_recv()
        return c

    lax.fori_loop(0, chips, handed, 0)

    groups = chips // RUN
    bases = [g * RUN for g in range(groups)]

    def transit(p):
        return split(t_all[p].reshape(DIM, DIM))

    trans = [transit(p) for p in bases]
    offs = [m_all[p, HALF:] for p in bases]
    for g, p in enumerate(bases):
        put(runs, (p,), trans[g])
        local[p] = offs[g]
    trans = [stacked(trans[g], split(offs[g])) for g in range(groups)]
    for j in range(1, RUN):
        new = [nn(trans[g], transit(p + j)) for g, p in enumerate(bases)]
        for g, p in enumerate(bases):
            offs[g] = new[g][DIM:] + m_all[p + j, HALF:]
            local[p + j] = offs[g]
            trans[g] = split(jnp.concatenate([new[g][:DIM], offs[g]], axis=0))
            put(runs, (p + j,), tuple(x[:DIM] for x in trans[g]))

    def tell_state(p, now):
        s_all[p] = now

        @pl.when(p != chip)
        def _():
            to(s_all.at[p], state.at[core, chip], ss.at[p], rs.at[chip], there(p)).start()

    def walk(g, now):
        base = g * RUN
        tell_state(base, now)
        halves = split(now)
        new = [nn(halves, get(runs, base + j)) + local[base + j] for j in range(RUN)]
        for j in range(RUN - 1):
            tell_state(base + j + 1, new[j])
        return new[RUN - 1]

    lax.fori_loop(0, groups, walk, jnp.zeros((quarter, DIM), F32))
    state[core, chip] = s_all[chip]

    last = [transit(p + RUN - 1) for p in bases]
    for g, p in enumerate(bases):
        put(runs, (p + RUN - 2,), last[g])
    for j in range(RUN - 2, 0, -1):
        last = [split(nn(transit(p + j), last[g])) for g, p in enumerate(bases)]
        for g, p in enumerate(bases):
            put(runs, (p + j - 1,), last[g])

    def arrive(ref, sent, send, recv, hand_send, hand_recv):
        def one_head(h, c):
            for e in range(2):
                x = 2 * h + e

                @pl.when(x != chip)
                def _():
                    to(sent.at[x], ref.at[core, x], send.at[x], recv.at[x], there(x)).wait_recv()

            at = pl.ds(2 * h, 2)
            to(ref.at[core, at], ref.at[core, at], hand_send.at[h], hand_recv.at[h], sibling).start()
            return c

        lax.fori_loop(0, HEADS, one_head, 0)

    def handed_head(ref, h, hand_send, hand_recv):
        at = pl.ds(2 * h, 2)
        return to(ref.at[core, at], ref.at[1 - core, at], hand_send.at[h], hand_recv.at[h], sibling)

    def whole(ref, h):
        return jnp.concatenate([ref[c, pl.ds(2 * h, 2)].reshape(HALF, DIM) for c in range(2)], axis=0)

    arrive(state, s_all, ss, rs, shs, rhs)

    def swap_source(h):
        return to(src_two.at[h, 1 - core], src_got.at[h], sy.at[h], ry.at[h], sibling)

    def next_source(h):
        return to(src_own.at[h], src_next.at[h], so.at[h], ro.at[h], sibling)

    def chip_source(h):
        swap_source(h).wait_recv()
        both = src_two[h, core] + src_got[h]
        for e in range(2):
            x = 2 * h + e
            source[x, :quarter] = both[e * quarter : (e + 1) * quarter]
            source[x, quarter:] = both[HALF:]

            @pl.when(x != chip)
            def _():
                to(source.at[x], got.at[chip], sx.at[x], rx.at[chip], there(x)).start()

    def middle(step, c):
        heads = [step * GROUP + h for h in range(GROUP)]
        for h in heads:
            handed_head(state, h, shs, rhs).wait_recv()
        qd = [get(q_grp, h) for h in heads]
        outs = [nt(qd[i], split(whole(state, h))) + y_dev[h] for i, h in enumerate(heads)]
        for i, h in enumerate(heads):
            out = outs[i]
            cot = cotan[:, columns(h)].astype(F32)
            scale = lax.rsqrt(jnp.mean(out * out, axis=1, keepdims=True) + EPS_OUT)
            normed = out * scale
            scaled = cot * gain[h]
            grad = scale * (scaled - normed * jnp.mean(normed * scaled, axis=1, keepdims=True))
            halves = split(grad)
            put(dop, (h,), halves)
            src = tn(halves, qd[i])
            gains = jnp.broadcast_to(jnp.sum(cot * normed, axis=0, keepdims=True), (8, DIM))
            for j in range(2):
                src_two[h, j, :HALF] = src[j * HALF : (j + 1) * HALF]
                src_two[h, j, HALF:] = gains
            swap_source(h).start()

        @pl.when(step > 0)
        def _():
            for h in heads:
                chip_source(h - GROUP)

        return c

    fetch[3].wait()
    lax.fori_loop(0, steps, middle, 0)

    for h in range(HEADS - GROUP, HEADS):
        chip_source(h)
    got[chip] = source[chip]

    @pl.when(core == 1)
    def _():
        def own(step, c):
            for h in [step * GROUP + h for h in range(GROUP)]:
                src_own[h] = tn(get(dop, h), get(q_dev, h))
                next_source(h).start()
            return c

        lax.fori_loop(0, steps, own, 0)

    def by_states(step, c):
        heads = [step * GROUP + h for h in range(GROUP)]
        states, do = [], []
        for h in heads:
            begin = whole(state, h)
            moved = nn(split(begin), split(m_sib[h, 0])) + m_sib[h, 1]
            s0 = split(jnp.where(core == 0, begin, moved))
            s1 = split(nn(s0, get(tp, h, 0)) + o_blk[h])
            do0, do1 = get(dop, h, slice(0, HALF)), get(dop, h, slice(HALF, DIM))
            states += [s0, s1]
            do += [do0, do1]
            src1[h] = tn(do1, get(qep, h))
        update = [split(u[heads[h], b] - nt(get(wp, heads[h], b), states[i])) for i, (h, b) in enumerate(many)]
        d_scores = [split(jnp.where(reads, nt(do[i], update[i]), 0.0)) for i in range(count)]
        for i, (h, b) in enumerate(many):
            at = (heads[h], b)
            put(sp, at, states[i])
            put(upd, at, update[i])
            hold[at] = tn(get(zp, *at), do[i])
            qn = get(qnp, *at)
            part[at] = tn(d_scores[i], qn)
            grad = nn_sum((do[i], states[i]), (d_scores[i], get(knp, *at)))
            unit = joined(qn)
            grad = qinv[at] * (grad - unit * jnp.sum(unit * grad, axis=1, keepdims=True))
            gq_out[tokens(b), columns(heads[h])] = grad.astype(BF16)
        return c

    lax.fori_loop(0, steps, by_states, 0)
    queries_out = pltpu.make_async_copy(gq_out, gq_far, stored.at[0])
    queries_out.start()

    def source_here(i, gains):
        p = chips - 1 - i

        @pl.when(p != chip)
        def _():
            to(source.at[0], got.at[p], sx.at[p], rx.at[p], there(p)).wait_recv()

        return gains + got[p, quarter:]

    gains = lax.fori_loop(0, chips, source_here, jnp.zeros((8, DIM), F32))
    g_all[dp] = gains
    for i in range(1, ways):
        other = lax.rem(dp + i, ways)
        to(g_all.at[dp], g_all.at[dp], sd.at[other], rd.at[dp], {"dp": other}).start()

    now = [got[p + RUN - 1, :quarter] for p in bases]
    for g, p in enumerate(bases):
        local[p + RUN - 1] = now[g]
    for j in range(RUN - 1, 0, -1):
        new = [nt(split(now[g]), transit(p + j - 1)) for g, p in enumerate(bases)]
        now = [new[g] + got[p + j - 1, :quarter] for g, p in enumerate(bases)]
        for g, p in enumerate(bases):
            local[p + j - 1] = now[g]

    def tell_adjoint(p, now):
        a_all[p] = now

        @pl.when(p != chip)
        def _():
            to(a_all.at[p], adjoint.at[core, chip], sa.at[p], ra.at[chip], there(p)).start()

    def walk_back(i, now):
        base = (groups - 1 - i) * RUN
        tell_adjoint(base + RUN - 1, now)
        halves = split(now)
        new = [nt(halves, get(runs, base + j)) for j in range(RUN)]
        for j in range(RUN - 2, -1, -1):
            tell_adjoint(base + j, new[j] + local[base + j + 1])
        return new[RUN - 1] + local[base]

    lax.fori_loop(0, groups, walk_back, jnp.zeros((quarter, DIM), F32))
    adjoint[core, chip] = a_all[chip]

    @pl.when(core == 0)
    def _():
        def came(h, c):
            next_source(h).wait_recv()
            return c

        lax.fori_loop(0, HEADS, came, 0)

    arrive(adjoint, a_all, sa, ra, sha, rha)

    for i in range(1, ways):
        other = lax.rem(dp + i, ways)
        to(g_all.at[other], g_all.at[other], sd.at[other], rd.at[other], {"dp": other}).wait()

    @pl.when(lax.rem(chip, 2) == 0)
    def _():
        summed = g_all[0]
        for i in range(1, ways):
            summed = summed + g_all[i]
        total[mine] = summed

        def give(i, c):
            x = lax.rem(chip + i, chips)
            to(total.at[mine], total.at[mine], sg.at[x], rg.at[mine], there(x)).start()
            return c

        lax.fori_loop(1, chips, give, 0)

    def stores(step):
        cols = pl.ds(pl.multiple_of(step * GROUP * DIM, GROUP * DIM), GROUP * DIM)
        pairs = ((gk_out, gk_far), (gv_out, gv_far))
        return [
            pltpu.make_async_copy(src.at[:, :, cols], dst.at[:, :, cols], stored.at[1 + 2 * step + i])
            for i, (src, dst) in enumerate(pairs)
        ]

    def final(step, c):
        heads = [step * GROUP + h for h in range(GROUP)]
        for h in heads:
            handed_head(adjoint, h, sha, rha).wait_recv()
        adjoints = []
        for h in heads:
            end = whole(adjoint, h)
            moved = nt(split(end), split(m_sib[h, 0])) + src_next[h]
            a1 = split(jnp.where(core == 0, moved, end))
            adjoints += [split(nt(a1, get(tp, h, 1)) + src1[h]), a1]
        places_of = [(heads[h], b) for h, b in many]
        target = [hold[at] + nt(get(gp, *at), adjoints[i]) for i, at in enumerate(places_of)]
        less = [split(-x) for x in target]
        update = [get(upd, *at) for at in places_of]
        d_gram = [jnp.where(strict, nt(less[i], update[i]), 0.0) for i in range(count)]
        d_gram = [split(x + x.T) for x in d_gram]
        for i, (h, b) in enumerate(many):
            at = places_of[i]
            kn = get(knp, *at)
            grad = part[at] + nn_sum((less[i], get(sp, *at)), (d_gram[i], kn), (update[i], adjoints[i]))
            unit = joined(kn)
            grad = kinv[at] * (grad - unit * jnp.sum(unit * grad, axis=1, keepdims=True))
            gk_out[tokens(b), :, columns(heads[h])] = grad.astype(BF16).reshape(HALF, 2, DIM)
            gv_out[tokens(b), :, columns(heads[h])] = target[i].astype(BF16).reshape(HALF, 2, DIM)
        for copy in stores(step):
            copy.start()
        return c

    lax.fori_loop(0, steps, final, 0)
    queries_out.wait()
    for step in range(steps):
        for copy in stores(step):
            copy.wait()

    @pl.when(lax.rem(chip, 2) == 0)
    def _():
        def gone(i, c):
            x = lax.rem(chip + i, chips)
            to(total.at[mine], total.at[mine], sg.at[x], rg.at[mine], there(x)).wait_send()
            return c

        lax.fori_loop(1, chips, gone, 0)

    def finish(i, c):
        x = lax.rem(chip + i, chips)
        to(m_out.at[x], m_all.at[x], st.at[x], rt.at[x], there(x)).wait_send()
        to(s_all.at[x], state.at[core, x], ss.at[x], rs.at[x], there(x)).wait_send()
        to(source.at[x], got.at[x], sx.at[x], rx.at[x], there(x)).wait_send()
        to(a_all.at[x], adjoint.at[core, x], sa.at[x], ra.at[x], there(x)).wait_send()
        return c

    lax.fori_loop(1, chips, finish, 0)

    def finish_hand(p, c):
        to(t_all.at[p, core], t_all.at[p, core], sf.at[p], rf.at[p], sibling).wait_send()
        return c

    lax.fori_loop(0, chips, finish_hand, 0)

    def finish_heads(h, c):
        swap(h).wait_send()
        handed_head(state, h, shs, rhs).wait_send()
        handed_head(adjoint, h, sha, rha).wait_send()
        swap_source(h).wait_send()

        @pl.when(core == 1)
        def _():
            next_source(h).wait_send()

        @pl.when(2 * h != chip)
        def _():
            to(total.at[h], total.at[h], sg.at[h], rg.at[h], there(2 * h)).wait_recv()

        return c

    lax.fori_loop(0, HEADS, finish_heads, 0)


def shape(*dims, dtype=F32):
    return jax.ShapeDtypeStruct(dims, dtype)


def layer(q, k, v, rate, cotan, gain, n, ways):
    def full(*dims):
        return pltpu.VMEM(dims, F32)

    def pair(*dims):
        return pltpu.VMEM((2, *dims), BF16)

    def dma(size):
        return pltpu.SemaphoreType.DMA((size,))

    chips = n // 2
    square = (HEADS, DIM, DIM)
    blocks = (HEADS, 2, DIM, DIM)
    thin = (HEADS, 2, HALF, DIM)
    quarter = (chips, DIM // 4, DIM)
    spread = (2, *quarter)
    noted = (DIM // 4 + 8, DIM)
    wide = HEADS * DIM
    flat, deep = pltpu.VMEM((DIM, wide), BF16), pltpu.VMEM((DIM, 2, wide), BF16)
    scratch = [
        flat, deep, deep, flat, flat, deep, deep,
        full(*blocks), full(*blocks), pair(*square), pair(*square), full(*square),
        pair(*blocks), pair(*thin), full(HEADS, 2, DIM, 1), full(HEADS, 2, HALF, 1),
        pair(*blocks), full(*blocks), pair(*blocks), pair(*thin), pair(*blocks), full(*square), pair(HEADS, HALF, DIM),
        pair(*blocks), pair(*thin),
        full(chips, 96, DIM), full(chips, 96, DIM), full(chips, 2, HALF, DIM), pair(chips, DIM, DIM), full(*quarter), full(*quarter),
        full(*spread), pair(*square), full(HEADS, 2, HALF + 8, DIM), full(HEADS, HALF + 8, DIM), full(*square), full(*square),
        full(chips, *noted), full(chips, *noted), full(*quarter), full(*spread), full(ways, 8, DIM),
        pair(*blocks), pair(*blocks), full(*blocks), full(*blocks), full(*square),
    ]
    counts = [HEADS, chips, chips, chips, HEADS, HEADS, HEADS, chips, chips, HEADS, ways]
    sems = [dma(size) for size in counts for _ in range(2)] + [dma(chips), dma(HEADS), dma(4), dma(1 + 2 * HEADS // GROUP)]
    return pl.pallas_call(
        functools.partial(layer_kernel, n, ways),
        in_specs=[FAR, FAR, FAR, VMEM, FAR, VMEM],
        out_specs=[FAR, FAR, FAR, VMEM],
        out_shape=[
            shape(DIM, wide, dtype=BF16),
            shape(DIM, 2, wide, dtype=BF16),
            shape(DIM, 2, wide, dtype=BF16),
            shape(HEADS, 8, DIM),
        ],
        scratch_shapes=scratch + sems,
        compiler_params=pltpu.CompilerParams(collective_id=0, has_side_effects=True, vmem_limit_bytes=LIMIT),
    )(q, k, v, rate, cotan, gain)


def on_device(queries, keys, values, betas, grad_out, gain):
    n = lax.axis_size("outer") * lax.axis_size("inner")
    ways = lax.axis_size("dp")
    rate = betas[0].transpose(0, 2, 1).reshape(HEADS, 2, DIM)
    gq, gk, gv, total = layer(queries[0], keys[0], values[0], rate, grad_out[0], gain.reshape(HEADS, 1, DIM), n, ways)
    gain_grad = total[:, 0, :].reshape(HEADS * DIM) * (1.0 / math.sqrt(DIM * n * ways))
    return gq[None], gk[None], gv[None], gain_grad


def solution(mesh):
    seq = ("outer", "inner")
    return jax.shard_map(
        on_device,
        mesh=mesh,
        in_specs=(
            P("dp", seq, None),
            P("dp", seq, None, None),
            P("dp", seq, None, None),
            P("dp", None, None, seq),
            P("dp", seq, None),
            P(),
        ),
        out_specs=(P("dp", seq, None), P("dp", seq, None, None), P("dp", seq, None, None), P()),
        check_vma=False,
    )
```

```python
import functools
import math

import jax
import jax.numpy as jnp
from jax import lax
from jax.experimental import pallas as pl
from jax.experimental.pallas import tpu as pltpu
from jax.sharding import PartitionSpec as P

HEADS = 8
DIM = 128
HALF = 64
GROUP = 4
RUN = 4
EPS_KEY = 1e-06
EPS_OUT = 1e-05
F32 = jnp.float32
BF16 = jnp.bfloat16
MESH = pl.DeviceIdType.MESH
VMEM = pl.BlockSpec(memory_space=pltpu.VMEM)
LIMIT = 48 * 1024 * 1024


def split(x):
    high = x.astype(BF16)
    return high, (x - high.astype(F32)).astype(BF16)


def raw_dot(left, right, dims):
    return lax.dot_general(left, right, (dims, ((), ())), preferred_element_type=F32)


def folded(wide):
    half = wide.shape[1] // 2
    return wide[:, :half] + wide[:, half:]


def nn(a, b):
    lhs = jnp.concatenate(a, axis=1)
    rhs = jnp.concatenate(b, axis=1)
    return folded(raw_dot(lhs, jnp.concatenate([rhs, rhs], axis=0), ((1,), (0,))))


def nt(a, b):
    lhs = jnp.concatenate(a, axis=1)
    rhs = jnp.concatenate(b, axis=0)
    return folded(raw_dot(lhs, jnp.concatenate([rhs, rhs], axis=1), ((1,), (1,))))


def tn(a, b):
    lhs = jnp.concatenate(a, axis=0)
    rhs = jnp.concatenate(b, axis=1)
    return folded(raw_dot(lhs, jnp.concatenate([rhs, rhs], axis=0), ((0,), (0,))))


def nn_sum(*terms):
    lhs = jnp.concatenate([x for a, _ in terms for x in a], axis=1)
    rhs = []
    for _, b in terms:
        rhs += [jnp.concatenate(b, axis=1)] * 2
    return folded(raw_dot(lhs, jnp.concatenate(rhs, axis=0), ((1,), (0,))))


def stacked(*pairs):
    return tuple(jnp.concatenate(part, axis=0) for part in zip(*pairs))


def beside(*pairs):
    return tuple(jnp.concatenate(part, axis=1) for part in zip(*pairs))


def inv_norm(x):
    return lax.rsqrt(jnp.sum(x * x, axis=1, keepdims=True) + EPS_KEY)


def places():
    row = lax.broadcasted_iota(jnp.int32, (DIM, DIM), 0)
    return row, lax.broadcasted_iota(jnp.int32, (DIM, DIM), 1)


def read_mask(col):
    token = lax.broadcasted_iota(jnp.int32, (HALF, DIM), 0)
    return (col[:HALF] >> 1) <= token


def put(ref, at, pair):
    ref[(0, *at)] = pair[0]
    ref[(1, *at)] = pair[1]


def get(ref, *at):
    return ref[(0, *at)], ref[(1, *at)]


def joined(pair):
    return pair[0].astype(F32) + pair[1].astype(F32)


def columns(head):
    return pl.ds(pl.multiple_of(head * DIM, DIM), DIM)


def tokens(block):
    return slice(block * HALF, (block + 1) * HALF)


def two_keys(ref, block, head):
    return ref[tokens(block), :, columns(head)].reshape(DIM, DIM)


def to(src, dst, send, recv, target):
    return pltpu.make_async_remote_copy(
        src_ref=src, dst_ref=dst, send_sem=send, recv_sem=recv, device_id=target, device_id_type=MESH
    )


def home(h):
    return 2 * h + lax.rem(lax.div(h, 2), 2)


def layer_kernel(
    n, ways,
    q, k, v, rate, cotan, gain,
    gq_out, gk_out, gv_out, total,
    m_dev, m_sib, q_dev, q_grp, y_dev, knp, qnp, kinv, qinv, wp, u, gp, zp, tp, o_blk, qep, xbp, scp,
    m_out, m_all, t_all, runs, local, s_all, state, dop, src_two, src_got, src_own, src_next, source, got, a_all, adjoint, g_all,
    sp, upd, part, hold, src1,
    sw, rw, st, rt, sf, rf, ss, rs, shs, rhs, sy, ry, so, ro, sx, rx, sa, ra, sha, rha, sd, rd, sg, rg,
):
    core = lax.axis_index("inner")
    chip = lax.axis_index("outer")
    chips = n // 2
    mine = lax.div(chip, 2)
    owner = home(mine) == chip
    dp = lax.axis_index("dp")
    sibling = {"inner": 1 - core}
    steps = HEADS // GROUP

    def there(x):
        return {"outer": x}

    barrier = pltpu.get_barrier_semaphore()

    def tell(i, c):
        pl.semaphore_signal(barrier, inc=1, device_id=there(lax.rem(chip + i, chips)), device_id_type=MESH)
        return c

    lax.fori_loop(1, chips, tell, 0)
    pl.semaphore_signal(barrier, inc=1, device_id=sibling, device_id_type=MESH)
    for i in range(1, ways):
        pl.semaphore_signal(barrier, inc=1, device_id={"dp": lax.rem(dp + i, ways)}, device_id_type=MESH)

    row, col = places()
    eye = row == col
    strict = col < row
    reads = read_mask(col)
    many = [(h, b) for h in range(GROUP) for b in range(2)]
    count = len(many)
    one = jnp.where(eye, 1.0, 0.0)

    def level(s):
        shift = s.bit_length() - 1
        rb, cb = row >> shift, col >> shift
        return ((rb >> 1) == (cb >> 1)) & ((rb & 1) == 1) & ((cb & 1) == 0)

    def masked(pair, mask):
        return tuple(jnp.where(mask, x.astype(F32), 0.0).astype(BF16) for x in pair)

    def turn(step):
        first = lax.rem(step + chip, steps) * GROUP
        return [first + h for h in range(GROUP)]

    def swap(h):
        return to(m_dev.at[h], m_sib.at[h], sw.at[h], rw.at[h], sibling)

    def chip_maps(step):
        heads = turn(step)
        half = pl.ds(pl.multiple_of(core * HALF, HALF), HALF)
        lead = core == 0
        for h in heads:
            swap(h).wait_recv()
        rows, later, offs = [], [], []
        for h in heads:
            begin = [jnp.where(lead, m_dev[h, j, half], m_sib[h, j, half]) for j in range(2)]
            rows.append(split(jnp.concatenate(begin, axis=0)))
            later.append(split(jnp.where(lead, m_sib[h, 0], m_dev[h, 0])))
            offs.append(jnp.where(lead, m_sib[h, 1, half], m_dev[h, 1, half]))
        made = [nn(rows[i], later[i]) for i in range(GROUP)]
        for i, h in enumerate(heads):
            m_out[h, :HALF] = made[i][:HALF]
            m_out[h, HALF:] = made[i][HALF:] + offs[i]

            @pl.when(home(h) != chip)
            def _():
                to(m_out.at[h], m_all.at[chip], st.at[h], rt.at[chip], there(home(h))).start()

    def query_side(step):
        heads = [step * GROUP + h for h in range(GROUP)]
        zero = jnp.zeros((DIM, DIM), BF16)
        scaled = [get(xbp, heads[h], b) for h, b in many]
        keys = [get(knp, heads[h], b) for h, b in many]
        pack = [beside(keys[i], (two_keys(v, b, heads[h]), zero)) for i, (h, b) in enumerate(many)]
        z = [split(nn(get(scp, heads[h], b), scaled[i])) for i, (h, b) in enumerate(many)]
        zr = [nn(z[i], pack[i]) for i in range(count)]
        qe = [joined(get(qnp, heads[h], b)) - zr[i][:, :DIM] for i, (h, b) in enumerate(many)]
        for i, (h, b) in enumerate(many):
            put(gp, (heads[h], b), split(tn(scaled[i], keys[i])))
            put(zp, (heads[h], b), z[i])
        for h in range(GROUP):
            a, b = 2 * h, 2 * h + 1
            later = split(qe[b])
            back = nt(later, stacked(get(tp, heads[h], 0), split(o_blk[heads[h]])))
            for ref in (q_dev, q_grp):
                put(ref, (heads[h], slice(0, HALF)), split(qe[a]))
                put(ref, (heads[h], slice(HALF, DIM)), split(back[:, :DIM]))
            y_dev[heads[h], :HALF] = zr[a][:, DIM:]
            y_dev[heads[h], HALF:] = zr[b][:, DIM:] + back[:, DIM:]
            put(qep, (heads[h],), later)

        @pl.when(core == 1)
        def _():
            before = [stacked(split(m_sib[h, 0]), split(m_sib[h, 1])) for h in heads]
            back = [nt(get(q_dev, h), before[i]) for i, h in enumerate(heads)]
            for i, h in enumerate(heads):
                put(q_grp, (h,), split(back[i][:, :DIM]))
                y_dev[h] = y_dev[h] + back[i][:, DIM:]

    def maps(step, c):
        heads = turn(step)
        keys, vals, queries, ratecol, raterow = [], [], [], [], []
        for h, b in many:
            kr = two_keys(k, b, heads[h]).astype(F32)
            inv = inv_norm(kr)
            kinv[heads[h], b] = inv
            keys.append(split(kr * inv))
            put(knp, (heads[h], b), keys[-1])
            vals.append(two_keys(v, b, heads[h]))
            qr = q[tokens(b), columns(heads[h])].astype(F32)
            inv = inv_norm(qr)
            qinv[heads[h], b] = inv
            queries.append(split(qr * inv))
            put(qnp, (heads[h], b), queries[-1])
            r = rate[heads[h], b : b + 1, :]
            raterow.append(r)
            ratecol.append(jnp.sum(jnp.where(eye, r, 0.0), axis=1, keepdims=True))
        both = [nt(stacked(keys[i], queries[i]), keys[i]) for i in range(count)]
        lower = [jnp.where(strict, ratecol[i] * both[i][:DIM], 0.0) for i in range(count)]
        scores = [split(jnp.where(reads, both[i][DIM:], 0.0)) for i in range(count)]
        first = level(1)
        inverse = [one - jnp.where(first, lower[i], 0.0) for i in range(count)]
        lower = [split(x) for x in lower]
        s = 2
        while s < DIM:
            mask = level(s)
            halves = [split(x) for x in inverse]
            inner = [split(nn(masked(lower[i], mask), halves[i])) for i in range(count)]
            inverse = [inverse[i] - nn(halves[i], inner[i]) for i in range(count)]
            s *= 2
        scaled = [split(inverse[i] * raterow[i]) for i in range(count)]
        zero = jnp.zeros((DIM, DIM), BF16)
        pack = [beside(keys[i], (vals[i], zero)) for i in range(count)]
        solved = [nn(scaled[i], pack[i]) for i in range(count)]
        solved_p = [split(x) for x in solved]
        move = [tn(solved_p[i], keys[i]) for i in range(count)]
        trans = [one - move[i][:DIM] for i in range(count)]
        offs = [move[i][DIM:] for i in range(count)]
        trans_p = [split(x) for x in trans]
        offs_p = [split(x) for x in offs]
        for i, (h, b) in enumerate(many):
            put(wp, (heads[h], b), tuple(x[:, :DIM] for x in solved_p[i]))
            u[heads[h], b] = solved[i][:, DIM:]
            put(xbp, (heads[h], b), scaled[i])
            put(scp, (heads[h], b), scores[i])
            put(tp, (heads[h], b), trans_p[i])
        for h in range(GROUP):
            a, b = 2 * h, 2 * h + 1
            through = nn(stacked(trans_p[a], offs_p[a]), trans_p[b])
            m_dev[heads[h], 0] = through[:DIM]
            m_dev[heads[h], 1] = through[DIM:] + offs[b]
            o_blk[heads[h]] = offs[a]

        @pl.when(step == 0)
        def _():
            pl.semaphore_wait(barrier, chips + ways - 1)

        for h in heads:
            swap(h).start()

        @pl.when(step > 0)
        def _():
            chip_maps(step - 1)

        return c

    lax.fori_loop(0, steps, maps, 0)
    chip_maps(steps - 1)
    m_all[chip] = m_out[mine]

    def deferred(step, c):
        query_side(step)
        return c

    lax.fori_loop(0, steps // 2, deferred, 0)

    def hand_over(i, c):
        p = lax.rem(chip - i + chips, chips)

        @pl.when(p != chip)
        def _():
            to(m_out.at[0], m_all.at[p], st.at[0], rt.at[p], there(p)).wait_recv()

        t_all[p, core] = m_all[p, :HALF]
        to(t_all.at[p, core], t_all.at[p, core], sf.at[p], rf.at[p], sibling).start()
        return c

    @pl.when(owner)
    def _():
        lax.fori_loop(0, chips, hand_over, 0)

    lax.fori_loop(steps // 2, steps, deferred, 0)

    def handed(i, c):
        p = lax.rem(chip - i + chips, chips)
        to(t_all.at[p, core], t_all.at[p, 1 - core], sf.at[p], rf.at[p], sibling).wait_recv()
        return c


    groups = chips // RUN
    bases = [g * RUN for g in range(groups)]

    def transit(p):
        return split(t_all[p].reshape(DIM, DIM))

    @pl.when(owner)
    def _():
        lax.fori_loop(0, chips, handed, 0)
        trans = [transit(p) for p in bases]
        offs = [m_all[p, HALF:] for p in bases]
        for g, p in enumerate(bases):
            put(runs, (p,), trans[g])
            local[p] = offs[g]
        trans = [stacked(trans[g], split(offs[g])) for g in range(groups)]
        for j in range(1, RUN):
            new = [nn(trans[g], transit(p + j)) for g, p in enumerate(bases)]
            for g, p in enumerate(bases):
                offs[g] = new[g][DIM:] + m_all[p + j, HALF:]
                local[p + j] = offs[g]
                trans[g] = split(jnp.concatenate([new[g][:DIM], offs[g]], axis=0))
                put(runs, (p + j,), tuple(x[:DIM] for x in trans[g]))

        def tell_state(p, now):
            s_all[p] = now

            @pl.when(p != chip)
            def _():
                to(s_all.at[p], state.at[core, mine], ss.at[p], rs.at[mine], there(p)).start()

        def walk(g, now):
            base = g * RUN
            tell_state(base, now)
            halves = split(now)
            new = [nn(halves, get(runs, base + j)) + local[base + j] for j in range(RUN)]
            for j in range(RUN - 1):
                tell_state(base + j + 1, new[j])
            return new[RUN - 1]

        lax.fori_loop(0, groups, walk, jnp.zeros((HALF, DIM), F32))
        state[core, mine] = s_all[chip]

        last = [transit(p + RUN - 1) for p in bases]
        for g, p in enumerate(bases):
            put(runs, (p + RUN - 2,), last[g])
        for j in range(RUN - 2, 0, -1):
            last = [split(nn(transit(p + j), last[g])) for g, p in enumerate(bases)]
            for g, p in enumerate(bases):
                put(runs, (p + j - 1,), last[g])

    def arrive(ref, sent, send, recv, hand_send, hand_recv):
        def one_head(h, c):
            @pl.when(home(h) != chip)
            def _():
                to(sent.at[0], ref.at[core, h], send.at[0], recv.at[h], there(home(h))).wait_recv()

            to(ref.at[core, h], ref.at[core, h], hand_send.at[h], hand_recv.at[h], sibling).start()
            return c

        lax.fori_loop(0, HEADS, one_head, 0)

    def handed_head(ref, h, hand_send, hand_recv):
        return to(ref.at[core, h], ref.at[1 - core, h], hand_send.at[h], hand_recv.at[h], sibling)

    def whole(ref, h):
        return jnp.concatenate([ref[c, h] for c in range(2)], axis=0)

    arrive(state, s_all, ss, rs, shs, rhs)

    def swap_source(h):
        return to(src_two.at[h, 1 - core], src_got.at[h], sy.at[h], ry.at[h], sibling)

    def next_source(h):
        return to(src_own.at[h], src_next.at[h], so.at[h], ro.at[h], sibling)

    def chip_source(h):
        swap_source(h).wait_recv()
        source[h] = src_two[h, core] + src_got[h]

        @pl.when(home(h) != chip)
        def _():
            to(source.at[h], got.at[chip], sx.at[h], rx.at[chip], there(home(h))).start()

    def middle(step, c):
        heads = [step * GROUP + h for h in range(GROUP)]
        for h in heads:
            handed_head(state, h, shs, rhs).wait_recv()
        qd = [get(q_grp, h) for h in heads]
        outs = [nt(qd[i], split(whole(state, h))) + y_dev[h] for i, h in enumerate(heads)]
        for i, h in enumerate(heads):
            out = outs[i]
            cot = cotan[:, columns(h)].astype(F32)
            scale = lax.rsqrt(jnp.mean(out * out, axis=1, keepdims=True) + EPS_OUT)
            normed = out * scale
            scaled = cot * gain[h]
            grad = scale * (scaled - normed * jnp.mean(normed * scaled, axis=1, keepdims=True))
            halves = split(grad)
            put(dop, (h,), halves)
            src = tn(halves, qd[i])
            gains = jnp.broadcast_to(jnp.sum(cot * normed, axis=0, keepdims=True), (8, DIM))
            for j in range(2):
                src_two[h, j, :HALF] = src[j * HALF : (j + 1) * HALF]
                src_two[h, j, HALF:] = gains
            swap_source(h).start()

        @pl.when(step > 0)
        def _():
            for h in heads:
                chip_source(h - GROUP)

        return c

    lax.fori_loop(0, steps, middle, 0)

    for h in range(HEADS - GROUP, HEADS):
        chip_source(h)
    got[chip] = source[mine]

    @pl.when(core == 1)
    def _():
        def own(step, c):
            for h in [step * GROUP + h for h in range(GROUP)]:
                src_own[h] = tn(get(dop, h), get(q_dev, h))
                next_source(h).start()
            return c

        lax.fori_loop(0, steps, own, 0)

    def by_states(step, c):
        heads = [step * GROUP + h for h in range(GROUP)]
        states, do = [], []
        for h in heads:
            begin = whole(state, h)
            moved = nn(split(begin), split(m_sib[h, 0])) + m_sib[h, 1]
            s0 = split(jnp.where(core == 0, begin, moved))
            s1 = split(nn(s0, get(tp, h, 0)) + o_blk[h])
            do0, do1 = get(dop, h, slice(0, HALF)), get(dop, h, slice(HALF, DIM))
            states += [s0, s1]
            do += [do0, do1]
            src1[h] = tn(do1, get(qep, h))
        update = [split(u[heads[h], b] - nt(get(wp, heads[h], b), states[i])) for i, (h, b) in enumerate(many)]
        d_scores = [split(jnp.where(reads, nt(do[i], update[i]), 0.0)) for i in range(count)]
        for i, (h, b) in enumerate(many):
            at = (heads[h], b)
            put(sp, at, states[i])
            put(upd, at, update[i])
            hold[at] = tn(get(zp, *at), do[i])
            qn = get(qnp, *at)
            part[at] = tn(d_scores[i], qn)
            grad = nn_sum((do[i], states[i]), (d_scores[i], get(knp, *at)))
            unit = joined(qn)
            grad = qinv[at] * (grad - unit * jnp.sum(unit * grad, axis=1, keepdims=True))
            gq_out[tokens(b), columns(heads[h])] = grad.astype(BF16)
        return c

    lax.fori_loop(0, steps, by_states, 0)

    @pl.when(owner)
    def _():
        def source_here(i, gains):
            p = chips - 1 - i

            @pl.when(p != chip)
            def _():
                to(source.at[0], got.at[p], sx.at[0], rx.at[p], there(p)).wait_recv()

            return gains + got[p, HALF:]

        gains = lax.fori_loop(0, chips, source_here, jnp.zeros((8, DIM), F32))
        g_all[dp] = gains
        for i in range(1, ways):
            other = lax.rem(dp + i, ways)
            to(g_all.at[dp], g_all.at[dp], sd.at[other], rd.at[dp], {"dp": other}).start()

        now = [got[p + RUN - 1, :HALF] for p in bases]
        for g, p in enumerate(bases):
            local[p + RUN - 1] = now[g]
        for j in range(RUN - 1, 0, -1):
            new = [nt(split(now[g]), transit(p + j - 1)) for g, p in enumerate(bases)]
            now = [new[g] + got[p + j - 1, :HALF] for g, p in enumerate(bases)]
            for g, p in enumerate(bases):
                local[p + j - 1] = now[g]

        def tell_adjoint(p, now):
            a_all[p] = now

            @pl.when(p != chip)
            def _():
                to(a_all.at[p], adjoint.at[core, mine], sa.at[p], ra.at[mine], there(p)).start()

        def walk_back(i, now):
            base = (groups - 1 - i) * RUN
            tell_adjoint(base + RUN - 1, now)
            halves = split(now)
            new = [nt(halves, get(runs, base + j)) for j in range(RUN)]
            for j in range(RUN - 2, -1, -1):
                tell_adjoint(base + j, new[j] + local[base + j + 1])
            return new[RUN - 1] + local[base]

        lax.fori_loop(0, groups, walk_back, jnp.zeros((HALF, DIM), F32))
        adjoint[core, mine] = a_all[chip]

    @pl.when(core == 0)
    def _():
        def came(h, c):
            next_source(h).wait_recv()
            return c

        lax.fori_loop(0, HEADS, came, 0)

    arrive(adjoint, a_all, sa, ra, sha, rha)

    @pl.when(owner)
    def _():
        for i in range(1, ways):
            other = lax.rem(dp + i, ways)
            to(g_all.at[other], g_all.at[other], sd.at[other], rd.at[other], {"dp": other}).wait()

        summed = g_all[0]
        for i in range(1, ways):
            summed = summed + g_all[i]
        total[mine] = summed

        def give(i, c):
            x = lax.rem(chip + i, chips)
            to(total.at[mine], total.at[mine], sg.at[x], rg.at[mine], there(x)).start()
            return c

        lax.fori_loop(1, chips, give, 0)

    def final(step, c):
        heads = [step * GROUP + h for h in range(GROUP)]
        for h in heads:
            handed_head(adjoint, h, sha, rha).wait_recv()
        adjoints = []
        for h in heads:
            end = whole(adjoint, h)
            moved = nt(split(end), split(m_sib[h, 0])) + src_next[h]
            a1 = split(jnp.where(core == 0, moved, end))
            adjoints += [split(nt(a1, get(tp, h, 1)) + src1[h]), a1]
        places_of = [(heads[h], b) for h, b in many]
        target = [hold[at] + nt(get(gp, *at), adjoints[i]) for i, at in enumerate(places_of)]
        less = [split(-x) for x in target]
        update = [get(upd, *at) for at in places_of]
        d_gram = [jnp.where(strict, nt(less[i], update[i]), 0.0) for i in range(count)]
        d_gram = [split(x + x.T) for x in d_gram]
        for i, (h, b) in enumerate(many):
            at = places_of[i]
            kn = get(knp, *at)
            grad = part[at] + nn_sum((less[i], get(sp, *at)), (d_gram[i], kn), (update[i], adjoints[i]))
            unit = joined(kn)
            grad = kinv[at] * (grad - unit * jnp.sum(unit * grad, axis=1, keepdims=True))
            gk_out[tokens(b), :, columns(heads[h])] = grad.astype(BF16).reshape(HALF, 2, DIM)
            gv_out[tokens(b), :, columns(heads[h])] = target[i].astype(BF16).reshape(HALF, 2, DIM)
        return c

    lax.fori_loop(0, steps, final, 0)

    @pl.when(owner)
    def _():
        def finish(i, c):
            x = lax.rem(chip + i, chips)
            to(total.at[mine], total.at[mine], sg.at[x], rg.at[mine], there(x)).wait_send()
            to(s_all.at[x], state.at[core, mine], ss.at[x], rs.at[mine], there(x)).wait_send()
            to(a_all.at[x], adjoint.at[core, mine], sa.at[x], ra.at[mine], there(x)).wait_send()
            return c

        lax.fori_loop(1, chips, finish, 0)

        def finish_hand(p, c):
            to(t_all.at[p, core], t_all.at[p, core], sf.at[p], rf.at[p], sibling).wait_send()
            return c

        lax.fori_loop(0, chips, finish_hand, 0)

    def finish_heads(h, c):
        swap(h).wait_send()
        handed_head(state, h, shs, rhs).wait_send()
        handed_head(adjoint, h, sha, rha).wait_send()
        swap_source(h).wait_send()

        @pl.when(core == 1)
        def _():
            next_source(h).wait_send()

        @pl.when(home(h) != chip)
        def _():
            to(m_out.at[h], m_all.at[chip], st.at[h], rt.at[chip], there(home(h))).wait_send()
            to(source.at[h], got.at[chip], sx.at[h], rx.at[chip], there(home(h))).wait_send()
            to(total.at[h], total.at[h], sg.at[h], rg.at[h], there(home(h))).wait_recv()

        return c

    lax.fori_loop(0, HEADS, finish_heads, 0)


def shape(*dims, dtype=F32):
    return jax.ShapeDtypeStruct(dims, dtype)


def layer(q, k, v, rate, cotan, gain, n, ways):
    def full(*dims):
        return pltpu.VMEM(dims, F32)

    def pair(*dims):
        return pltpu.VMEM((2, *dims), BF16)

    def dma(size):
        return pltpu.SemaphoreType.DMA((size,))

    chips = n // 2
    square = (HEADS, DIM, DIM)
    blocks = (HEADS, 2, DIM, DIM)
    thin = (HEADS, 2, HALF, DIM)
    rows = (chips, HALF, DIM)
    spread = (2, HEADS, HALF, DIM)
    noted = (HALF + 8, DIM)
    scratch = [
        full(*blocks), full(*blocks), pair(*square), pair(*square), full(*square),
        pair(*blocks), pair(*thin), full(HEADS, 2, DIM, 1), full(HEADS, 2, HALF, 1),
        pair(*blocks), full(*blocks), pair(*blocks), pair(*thin), pair(*blocks), full(*square), pair(HEADS, HALF, DIM),
        pair(*blocks), pair(*thin),
        full(*square), full(chips, DIM, DIM), full(chips, 2, HALF, DIM), pair(chips, DIM, DIM), full(*rows), full(*rows),
        full(*spread), pair(*square), full(HEADS, 2, HALF + 8, DIM), full(HEADS, HALF + 8, DIM), full(*square), full(*square),
        full(HEADS, *noted), full(chips, *noted), full(*rows), full(*spread), full(ways, 8, DIM),
        pair(*blocks), pair(*blocks), full(*blocks), full(*blocks), full(*square),
    ]
    counts = [HEADS, chips, chips, chips, HEADS, HEADS, HEADS, chips, chips, HEADS, ways]
    sems = [dma(size) for size in counts for _ in range(2)] + [dma(chips), dma(HEADS)]
    wide = HEADS * DIM
    return pl.pallas_call(
        functools.partial(layer_kernel, n, ways),
        in_specs=[VMEM] * 6,
        out_specs=[VMEM] * 4,
        out_shape=[
            shape(DIM, wide, dtype=BF16),
            shape(DIM, 2, wide, dtype=BF16),
            shape(DIM, 2, wide, dtype=BF16),
            shape(HEADS, 8, DIM),
        ],
        scratch_shapes=scratch + sems,
        compiler_params=pltpu.CompilerParams(collective_id=0, has_side_effects=True, vmem_limit_bytes=LIMIT),
    )(q, k, v, rate, cotan, gain)


def on_device(queries, keys, values, betas, grad_out, gain):
    n = lax.axis_size("outer") * lax.axis_size("inner")
    ways = lax.axis_size("dp")
    rate = betas[0].transpose(0, 2, 1).reshape(HEADS, 2, DIM)
    gq, gk, gv, total = layer(queries[0], keys[0], values[0], rate, grad_out[0], gain.reshape(HEADS, 1, DIM), n, ways)
    gain_grad = total[:, 0, :].reshape(HEADS * DIM) * (1.0 / math.sqrt(DIM * n * ways))
    return gq[None], gk[None], gv[None], gain_grad


def solution(mesh):
    seq = ("outer", "inner")
    return jax.shard_map(
        on_device,
        mesh=mesh,
        in_specs=(
            P("dp", seq, None),
            P("dp", seq, None, None),
            P("dp", seq, None, None),
            P("dp", None, None, seq),
            P("dp", seq, None),
            P(),
        ),
        out_specs=(P("dp", seq, None), P("dp", seq, None, None), P("dp", seq, None, None), P()),
        check_vma=False,
    )
```

```python
import functools
import math

import jax
import jax.numpy as jnp
from jax import lax
from jax.experimental import pallas as pl
from jax.experimental.pallas import tpu as pltpu
from jax.sharding import PartitionSpec as P

HEADS = 8
DIM = 128
HALF = 64
GROUP = 4
RUN = 4
EPS_KEY = 1e-06
EPS_OUT = 1e-05
F32 = jnp.float32
BF16 = jnp.bfloat16
MESH = pl.DeviceIdType.MESH
VMEM = pl.BlockSpec(memory_space=pltpu.VMEM)
FAR = pl.BlockSpec(memory_space=pltpu.HBM)
LIMIT = 52 * 1024 * 1024


def split(x):
    high = x.astype(BF16)
    return high, (x - high.astype(F32)).astype(BF16)


def raw_dot(left, right, dims):
    return lax.dot_general(left, right, (dims, ((), ())), preferred_element_type=F32)


def folded(wide):
    half = wide.shape[1] // 2
    return wide[:, :half] + wide[:, half:]


def nn(a, b):
    lhs = jnp.concatenate(a, axis=1)
    rhs = jnp.concatenate(b, axis=1)
    return folded(raw_dot(lhs, jnp.concatenate([rhs, rhs], axis=0), ((1,), (0,))))


def nt(a, b):
    lhs = jnp.concatenate(a, axis=1)
    rhs = jnp.concatenate(b, axis=0)
    return folded(raw_dot(lhs, jnp.concatenate([rhs, rhs], axis=1), ((1,), (1,))))


def tn(a, b):
    lhs = jnp.concatenate(a, axis=0)
    rhs = jnp.concatenate(b, axis=1)
    return folded(raw_dot(lhs, jnp.concatenate([rhs, rhs], axis=0), ((0,), (0,))))


def nn_sum(*terms):
    lhs = jnp.concatenate([x for a, _ in terms for x in a], axis=1)
    rhs = []
    for _, b in terms:
        rhs += [jnp.concatenate(b, axis=1)] * 2
    return folded(raw_dot(lhs, jnp.concatenate(rhs, axis=0), ((1,), (0,))))


def stacked(*pairs):
    return tuple(jnp.concatenate(part, axis=0) for part in zip(*pairs))


def beside(*pairs):
    return tuple(jnp.concatenate(part, axis=1) for part in zip(*pairs))


def inv_norm(x):
    return lax.rsqrt(jnp.sum(x * x, axis=1, keepdims=True) + EPS_KEY)


def places():
    row = lax.broadcasted_iota(jnp.int32, (DIM, DIM), 0)
    return row, lax.broadcasted_iota(jnp.int32, (DIM, DIM), 1)


def read_mask(col):
    token = lax.broadcasted_iota(jnp.int32, (HALF, DIM), 0)
    return (col[:HALF] >> 1) <= token


def put(ref, at, pair):
    ref[(0, *at)] = pair[0]
    ref[(1, *at)] = pair[1]


def get(ref, *at):
    return ref[(0, *at)], ref[(1, *at)]


def joined(pair):
    return pair[0].astype(F32) + pair[1].astype(F32)


def columns(head):
    return pl.ds(pl.multiple_of(head * DIM, DIM), DIM)


def tokens(block):
    return slice(block * HALF, (block + 1) * HALF)


def two_keys(ref, block, head):
    return ref[tokens(block), :, columns(head)].reshape(DIM, DIM)


def to(src, dst, send, recv, target):
    return pltpu.make_async_remote_copy(
        src_ref=src, dst_ref=dst, send_sem=send, recv_sem=recv, device_id=target, device_id_type=MESH
    )


def layer_kernel(
    n, ways,
    q, k_far, v_far, rate, cotan, gain,
    gq_out, gk_out, gv_out, total,
    k, v,
    m_dev, m_sib, q_dev, q_grp, y_dev, knp, qnp, kinv, qinv, wp, u, gp, zp, tp, o_blk, qep, xbp, scp,
    m_out, m_all, t_all, runs, local, s_all, state, dop, src_two, src_got, src_own, src_next, source, got, a_all, adjoint, g_all,
    sp, upd, part, hold, src1,
    sw, rw, st, rt, sf, rf, ss, rs, shs, rhs, sy, ry, so, ro, sx, rx, sa, ra, sha, rha, sd, rd, sg, rg, fetched,
):
    core = lax.axis_index("inner")
    chip = lax.axis_index("outer")
    chips = n // 2
    mine = lax.div(chip, 2)
    dp = lax.axis_index("dp")
    sibling = {"inner": 1 - core}
    steps = HEADS // GROUP
    quarter = DIM // 4

    def there(x):
        return {"outer": x}

    far = ((k_far, k), (v_far, v))
    fetch = [pltpu.make_async_copy(src, dst, fetched.at[i]) for i, (src, dst) in enumerate(far)]
    for copy in fetch:
        copy.start()
    barrier = pltpu.get_barrier_semaphore()

    def tell(i, c):
        pl.semaphore_signal(barrier, inc=1, device_id=there(lax.rem(chip + i, chips)), device_id_type=MESH)
        return c

    lax.fori_loop(1, chips, tell, 0)
    pl.semaphore_signal(barrier, inc=1, device_id=sibling, device_id_type=MESH)
    for i in range(1, ways):
        pl.semaphore_signal(barrier, inc=1, device_id={"dp": lax.rem(dp + i, ways)}, device_id_type=MESH)

    row, col = places()
    eye = row == col
    strict = col < row
    reads = read_mask(col)
    many = [(h, b) for h in range(GROUP) for b in range(2)]
    count = len(many)
    one = jnp.where(eye, 1.0, 0.0)

    def level(s):
        shift = s.bit_length() - 1
        rb, cb = row >> shift, col >> shift
        return ((rb >> 1) == (cb >> 1)) & ((rb & 1) == 1) & ((cb & 1) == 0)

    def masked(pair, mask):
        return tuple(jnp.where(mask, x.astype(F32), 0.0).astype(BF16) for x in pair)

    def turn(step):
        first = lax.rem(step + chip, steps) * GROUP
        return [first + h for h in range(GROUP)]

    def swap(h):
        return to(m_dev.at[h], m_sib.at[h], sw.at[h], rw.at[h], sibling)

    def chip_maps(step):
        heads = turn(step)
        half = pl.ds(pl.multiple_of(core * HALF, HALF), HALF)
        lead = core == 0
        for h in heads:
            swap(h).wait_recv()
        rows, later, offs = [], [], []
        for h in heads:
            begin = [jnp.where(lead, m_dev[h, j, half], m_sib[h, j, half]) for j in range(2)]
            rows.append(split(jnp.concatenate(begin, axis=0)))
            later.append(split(jnp.where(lead, m_sib[h, 0], m_dev[h, 0])))
            offs.append(jnp.where(lead, m_sib[h, 1, half], m_dev[h, 1, half]))
        made = [nn(rows[i], later[i]) for i in range(GROUP)]
        for i, h in enumerate(heads):
            off = made[i][HALF:] + offs[i]
            for e in range(2):
                x = 2 * h + e
                m_out[x, :HALF] = made[i][:HALF]
                m_out[x, HALF:] = off[e * quarter : (e + 1) * quarter]

                @pl.when(x != chip)
                def _():
                    to(m_out.at[x], m_all.at[chip], st.at[x], rt.at[chip], there(x)).start()

    def query_side(step):
        heads = [step * GROUP + h for h in range(GROUP)]
        zero = jnp.zeros((DIM, DIM), BF16)
        scaled = [get(xbp, heads[h], b) for h, b in many]
        keys = [get(knp, heads[h], b) for h, b in many]
        pack = [beside(keys[i], (two_keys(v, b, heads[h]), zero)) for i, (h, b) in enumerate(many)]
        z = [split(nn(get(scp, heads[h], b), scaled[i])) for i, (h, b) in enumerate(many)]
        zr = [nn(z[i], pack[i]) for i in range(count)]
        qe = [joined(get(qnp, heads[h], b)) - zr[i][:, :DIM] for i, (h, b) in enumerate(many)]
        for i, (h, b) in enumerate(many):
            put(gp, (heads[h], b), split(tn(scaled[i], keys[i])))
            put(zp, (heads[h], b), z[i])
        for h in range(GROUP):
            a, b = 2 * h, 2 * h + 1
            later = split(qe[b])
            back = nt(later, stacked(get(tp, heads[h], 0), split(o_blk[heads[h]])))
            for ref in (q_dev, q_grp):
                put(ref, (heads[h], slice(0, HALF)), split(qe[a]))
                put(ref, (heads[h], slice(HALF, DIM)), split(back[:, :DIM]))
            y_dev[heads[h], :HALF] = zr[a][:, DIM:]
            y_dev[heads[h], HALF:] = zr[b][:, DIM:] + back[:, DIM:]
            put(qep, (heads[h],), later)

        @pl.when(core == 1)
        def _():
            before = [stacked(split(m_sib[h, 0]), split(m_sib[h, 1])) for h in heads]
            back = [nt(get(q_dev, h), before[i]) for i, h in enumerate(heads)]
            for i, h in enumerate(heads):
                put(q_grp, (h,), split(back[i][:, :DIM]))
                y_dev[h] = y_dev[h] + back[i][:, DIM:]

    def maps(step, c):
        heads = turn(step)
        keys, vals, queries, ratecol, raterow = [], [], [], [], []
        for h, b in many:
            kr = two_keys(k, b, heads[h]).astype(F32)
            inv = inv_norm(kr)
            kinv[heads[h], b] = inv
            keys.append(split(kr * inv))
            put(knp, (heads[h], b), keys[-1])
            vals.append(two_keys(v, b, heads[h]))
            qr = q[tokens(b), columns(heads[h])].astype(F32)
            inv = inv_norm(qr)
            qinv[heads[h], b] = inv
            queries.append(split(qr * inv))
            put(qnp, (heads[h], b), queries[-1])
            r = rate[heads[h], b : b + 1, :]
            raterow.append(r)
            ratecol.append(jnp.sum(jnp.where(eye, r, 0.0), axis=1, keepdims=True))
        both = [nt(stacked(keys[i], queries[i]), keys[i]) for i in range(count)]
        lower = [jnp.where(strict, ratecol[i] * both[i][:DIM], 0.0) for i in range(count)]
        scores = [split(jnp.where(reads, both[i][DIM:], 0.0)) for i in range(count)]
        first = level(1)
        inverse = [one - jnp.where(first, lower[i], 0.0) for i in range(count)]
        lower = [split(x) for x in lower]
        s = 2
        while s < DIM:
            mask = level(s)
            halves = [split(x) for x in inverse]
            inner = [split(nn(masked(lower[i], mask), halves[i])) for i in range(count)]
            inverse = [inverse[i] - nn(halves[i], inner[i]) for i in range(count)]
            s *= 2
        scaled = [split(inverse[i] * raterow[i]) for i in range(count)]
        zero = jnp.zeros((DIM, DIM), BF16)
        pack = [beside(keys[i], (vals[i], zero)) for i in range(count)]
        solved = [nn(scaled[i], pack[i]) for i in range(count)]
        solved_p = [split(x) for x in solved]
        move = [tn(solved_p[i], keys[i]) for i in range(count)]
        trans = [one - move[i][:DIM] for i in range(count)]
        offs = [move[i][DIM:] for i in range(count)]
        trans_p = [split(x) for x in trans]
        offs_p = [split(x) for x in offs]
        for i, (h, b) in enumerate(many):
            put(wp, (heads[h], b), tuple(x[:, :DIM] for x in solved_p[i]))
            u[heads[h], b] = solved[i][:, DIM:]
            put(xbp, (heads[h], b), scaled[i])
            put(scp, (heads[h], b), scores[i])
            put(tp, (heads[h], b), trans_p[i])
        for h in range(GROUP):
            a, b = 2 * h, 2 * h + 1
            through = nn(stacked(trans_p[a], offs_p[a]), trans_p[b])
            m_dev[heads[h], 0] = through[:DIM]
            m_dev[heads[h], 1] = through[DIM:] + offs[b]
            o_blk[heads[h]] = offs[a]

        @pl.when(step == 0)
        def _():
            pl.semaphore_wait(barrier, chips + ways - 1)

        for h in heads:
            swap(h).start()

        @pl.when(step > 0)
        def _():
            chip_maps(step - 1)

        return c

    for copy in fetch:
        copy.wait()
    lax.fori_loop(0, steps, maps, 0)
    chip_maps(steps - 1)
    m_all[chip] = m_out[chip]

    def deferred(step, c):
        query_side(step)
        return c

    lax.fori_loop(0, steps // 2, deferred, 0)

    def hand_over(i, c):
        p = lax.rem(chip - i + chips, chips)

        @pl.when(p != chip)
        def _():
            to(m_out.at[0], m_all.at[p], st.at[p], rt.at[p], there(p)).wait_recv()

        t_all[p, core] = m_all[p, :HALF]
        to(t_all.at[p, core], t_all.at[p, core], sf.at[p], rf.at[p], sibling).start()
        return c

    lax.fori_loop(0, chips, hand_over, 0)
    lax.fori_loop(steps // 2, steps, deferred, 0)

    def handed(i, c):
        p = lax.rem(chip - i + chips, chips)
        to(t_all.at[p, core], t_all.at[p, 1 - core], sf.at[p], rf.at[p], sibling).wait_recv()
        return c

    lax.fori_loop(0, chips, handed, 0)

    groups = chips // RUN
    bases = [g * RUN for g in range(groups)]

    def transit(p):
        return split(t_all[p].reshape(DIM, DIM))

    trans = [transit(p) for p in bases]
    offs = [m_all[p, HALF:] for p in bases]
    for g, p in enumerate(bases):
        put(runs, (p,), trans[g])
        local[p] = offs[g]
    trans = [stacked(trans[g], split(offs[g])) for g in range(groups)]
    for j in range(1, RUN):
        new = [nn(trans[g], transit(p + j)) for g, p in enumerate(bases)]
        for g, p in enumerate(bases):
            offs[g] = new[g][DIM:] + m_all[p + j, HALF:]
            local[p + j] = offs[g]
            trans[g] = split(jnp.concatenate([new[g][:DIM], offs[g]], axis=0))
            put(runs, (p + j,), tuple(x[:DIM] for x in trans[g]))

    def tell_state(p, now):
        s_all[p] = now

        @pl.when(p != chip)
        def _():
            to(s_all.at[p], state.at[core, chip], ss.at[p], rs.at[chip], there(p)).start()

    def walk(g, now):
        base = g * RUN
        tell_state(base, now)
        halves = split(now)
        new = [nn(halves, get(runs, base + j)) + local[base + j] for j in range(RUN)]
        for j in range(RUN - 1):
            tell_state(base + j + 1, new[j])
        return new[RUN - 1]

    lax.fori_loop(0, groups, walk, jnp.zeros((quarter, DIM), F32))
    state[core, chip] = s_all[chip]

    last = [transit(p + RUN - 1) for p in bases]
    for g, p in enumerate(bases):
        put(runs, (p + RUN - 2,), last[g])
    for j in range(RUN - 2, 0, -1):
        last = [split(nn(transit(p + j), last[g])) for g, p in enumerate(bases)]
        for g, p in enumerate(bases):
            put(runs, (p + j - 1,), last[g])

    def arrive(ref, sent, send, recv, hand_send, hand_recv):
        def one_head(h, c):
            for e in range(2):
                x = 2 * h + e

                @pl.when(x != chip)
                def _():
                    to(sent.at[x], ref.at[core, x], send.at[x], recv.at[x], there(x)).wait_recv()

            at = pl.ds(2 * h, 2)
            to(ref.at[core, at], ref.at[core, at], hand_send.at[h], hand_recv.at[h], sibling).start()
            return c

        lax.fori_loop(0, HEADS, one_head, 0)

    def handed_head(ref, h, hand_send, hand_recv):
        at = pl.ds(2 * h, 2)
        return to(ref.at[core, at], ref.at[1 - core, at], hand_send.at[h], hand_recv.at[h], sibling)

    def whole(ref, h):
        return jnp.concatenate([ref[c, pl.ds(2 * h, 2)].reshape(HALF, DIM) for c in range(2)], axis=0)

    arrive(state, s_all, ss, rs, shs, rhs)

    def swap_source(h):
        return to(src_two.at[h, 1 - core], src_got.at[h], sy.at[h], ry.at[h], sibling)

    def next_source(h):
        return to(src_own.at[h], src_next.at[h], so.at[h], ro.at[h], sibling)

    def chip_source(h):
        swap_source(h).wait_recv()
        both = src_two[h, core] + src_got[h]
        for e in range(2):
            x = 2 * h + e
            source[x, :quarter] = both[e * quarter : (e + 1) * quarter]
            source[x, quarter:] = both[HALF:]

            @pl.when(x != chip)
            def _():
                to(source.at[x], got.at[chip], sx.at[x], rx.at[chip], there(x)).start()

    def middle(step, c):
        heads = [step * GROUP + h for h in range(GROUP)]
        for h in heads:
            handed_head(state, h, shs, rhs).wait_recv()
        qd = [get(q_grp, h) for h in heads]
        outs = [nt(qd[i], split(whole(state, h))) + y_dev[h] for i, h in enumerate(heads)]
        for i, h in enumerate(heads):
            out = outs[i]
            cot = cotan[:, columns(h)].astype(F32)
            scale = lax.rsqrt(jnp.mean(out * out, axis=1, keepdims=True) + EPS_OUT)
            normed = out * scale
            scaled = cot * gain[h]
            grad = scale * (scaled - normed * jnp.mean(normed * scaled, axis=1, keepdims=True))
            halves = split(grad)
            put(dop, (h,), halves)
            src = tn(halves, qd[i])
            gains = jnp.broadcast_to(jnp.sum(cot * normed, axis=0, keepdims=True), (8, DIM))
            for j in range(2):
                src_two[h, j, :HALF] = src[j * HALF : (j + 1) * HALF]
                src_two[h, j, HALF:] = gains
            swap_source(h).start()

        @pl.when(step > 0)
        def _():
            for h in heads:
                chip_source(h - GROUP)

        return c

    lax.fori_loop(0, steps, middle, 0)

    for h in range(HEADS - GROUP, HEADS):
        chip_source(h)
    got[chip] = source[chip]

    @pl.when(core == 1)
    def _():
        def own(step, c):
            for h in [step * GROUP + h for h in range(GROUP)]:
                src_own[h] = tn(get(dop, h), get(q_dev, h))
                next_source(h).start()
            return c

        lax.fori_loop(0, steps, own, 0)

    def by_states(step, c):
        heads = [step * GROUP + h for h in range(GROUP)]
        states, do = [], []
        for h in heads:
            begin = whole(state, h)
            moved = nn(split(begin), split(m_sib[h, 0])) + m_sib[h, 1]
            s0 = split(jnp.where(core == 0, begin, moved))
            s1 = split(nn(s0, get(tp, h, 0)) + o_blk[h])
            do0, do1 = get(dop, h, slice(0, HALF)), get(dop, h, slice(HALF, DIM))
            states += [s0, s1]
            do += [do0, do1]
            src1[h] = tn(do1, get(qep, h))
        update = [split(u[heads[h], b] - nt(get(wp, heads[h], b), states[i])) for i, (h, b) in enumerate(many)]
        d_scores = [split(jnp.where(reads, nt(do[i], update[i]), 0.0)) for i in range(count)]
        for i, (h, b) in enumerate(many):
            at = (heads[h], b)
            put(sp, at, states[i])
            put(upd, at, update[i])
            hold[at] = tn(get(zp, *at), do[i])
            qn = get(qnp, *at)
            part[at] = tn(d_scores[i], qn)
            grad = nn_sum((do[i], states[i]), (d_scores[i], get(knp, *at)))
            unit = joined(qn)
            grad = qinv[at] * (grad - unit * jnp.sum(unit * grad, axis=1, keepdims=True))
            gq_out[tokens(b), columns(heads[h])] = grad.astype(BF16)
        return c

    lax.fori_loop(0, steps, by_states, 0)

    def source_here(i, gains):
        p = chips - 1 - i

        @pl.when(p != chip)
        def _():
            to(source.at[0], got.at[p], sx.at[p], rx.at[p], there(p)).wait_recv()

        return gains + got[p, quarter:]

    gains = lax.fori_loop(0, chips, source_here, jnp.zeros((8, DIM), F32))
    g_all[dp] = gains
    for i in range(1, ways):
        other = lax.rem(dp + i, ways)
        to(g_all.at[dp], g_all.at[dp], sd.at[other], rd.at[dp], {"dp": other}).start()

    now = [got[p + RUN - 1, :quarter] for p in bases]
    for g, p in enumerate(bases):
        local[p + RUN - 1] = now[g]
    for j in range(RUN - 1, 0, -1):
        new = [nt(split(now[g]), transit(p + j - 1)) for g, p in enumerate(bases)]
        now = [new[g] + got[p + j - 1, :quarter] for g, p in enumerate(bases)]
        for g, p in enumerate(bases):
            local[p + j - 1] = now[g]

    def tell_adjoint(p, now):
        a_all[p] = now

        @pl.when(p != chip)
        def _():
            to(a_all.at[p], adjoint.at[core, chip], sa.at[p], ra.at[chip], there(p)).start()

    def walk_back(i, now):
        base = (groups - 1 - i) * RUN
        tell_adjoint(base + RUN - 1, now)
        halves = split(now)
        new = [nt(halves, get(runs, base + j)) for j in range(RUN)]
        for j in range(RUN - 2, -1, -1):
            tell_adjoint(base + j, new[j] + local[base + j + 1])
        return new[RUN - 1] + local[base]

    lax.fori_loop(0, groups, walk_back, jnp.zeros((quarter, DIM), F32))
    adjoint[core, chip] = a_all[chip]

    @pl.when(core == 0)
    def _():
        def came(h, c):
            next_source(h).wait_recv()
            return c

        lax.fori_loop(0, HEADS, came, 0)

    arrive(adjoint, a_all, sa, ra, sha, rha)

    for i in range(1, ways):
        other = lax.rem(dp + i, ways)
        to(g_all.at[other], g_all.at[other], sd.at[other], rd.at[other], {"dp": other}).wait()

    @pl.when(lax.rem(chip, 2) == 0)
    def _():
        summed = g_all[0]
        for i in range(1, ways):
            summed = summed + g_all[i]
        total[mine] = summed

        def give(i, c):
            x = lax.rem(chip + i, chips)
            to(total.at[mine], total.at[mine], sg.at[x], rg.at[mine], there(x)).start()
            return c

        lax.fori_loop(1, chips, give, 0)

    def final(step, c):
        heads = [step * GROUP + h for h in range(GROUP)]
        for h in heads:
            handed_head(adjoint, h, sha, rha).wait_recv()
        adjoints = []
        for h in heads:
            end = whole(adjoint, h)
            moved = nt(split(end), split(m_sib[h, 0])) + src_next[h]
            a1 = split(jnp.where(core == 0, moved, end))
            adjoints += [split(nt(a1, get(tp, h, 1)) + src1[h]), a1]
        places_of = [(heads[h], b) for h, b in many]
        target = [hold[at] + nt(get(gp, *at), adjoints[i]) for i, at in enumerate(places_of)]
        less = [split(-x) for x in target]
        update = [get(upd, *at) for at in places_of]
        d_gram = [jnp.where(strict, nt(less[i], update[i]), 0.0) for i in range(count)]
        d_gram = [split(x + x.T) for x in d_gram]
        for i, (h, b) in enumerate(many):
            at = places_of[i]
            kn = get(knp, *at)
            grad = part[at] + nn_sum((less[i], get(sp, *at)), (d_gram[i], kn), (update[i], adjoints[i]))
            unit = joined(kn)
            grad = kinv[at] * (grad - unit * jnp.sum(unit * grad, axis=1, keepdims=True))
            gk_out[tokens(b), :, columns(heads[h])] = grad.astype(BF16).reshape(HALF, 2, DIM)
            gv_out[tokens(b), :, columns(heads[h])] = target[i].astype(BF16).reshape(HALF, 2, DIM)
        return c

    lax.fori_loop(0, steps, final, 0)

    @pl.when(lax.rem(chip, 2) == 0)
    def _():
        def gone(i, c):
            x = lax.rem(chip + i, chips)
            to(total.at[mine], total.at[mine], sg.at[x], rg.at[mine], there(x)).wait_send()
            return c

        lax.fori_loop(1, chips, gone, 0)

    def finish(i, c):
        x = lax.rem(chip + i, chips)
        to(m_out.at[x], m_all.at[x], st.at[x], rt.at[x], there(x)).wait_send()
        to(s_all.at[x], state.at[core, x], ss.at[x], rs.at[x], there(x)).wait_send()
        to(source.at[x], got.at[x], sx.at[x], rx.at[x], there(x)).wait_send()
        to(a_all.at[x], adjoint.at[core, x], sa.at[x], ra.at[x], there(x)).wait_send()
        return c

    lax.fori_loop(1, chips, finish, 0)

    def finish_hand(p, c):
        to(t_all.at[p, core], t_all.at[p, core], sf.at[p], rf.at[p], sibling).wait_send()
        return c

    lax.fori_loop(0, chips, finish_hand, 0)

    def finish_heads(h, c):
        swap(h).wait_send()
        handed_head(state, h, shs, rhs).wait_send()
        handed_head(adjoint, h, sha, rha).wait_send()
        swap_source(h).wait_send()

        @pl.when(core == 1)
        def _():
            next_source(h).wait_send()

        @pl.when(2 * h != chip)
        def _():
            to(total.at[h], total.at[h], sg.at[h], rg.at[h], there(2 * h)).wait_recv()

        return c

    lax.fori_loop(0, HEADS, finish_heads, 0)


def shape(*dims, dtype=F32):
    return jax.ShapeDtypeStruct(dims, dtype)


def layer(q, k, v, rate, cotan, gain, n, ways):
    def full(*dims):
        return pltpu.VMEM(dims, F32)

    def pair(*dims):
        return pltpu.VMEM((2, *dims), BF16)

    def dma(size):
        return pltpu.SemaphoreType.DMA((size,))

    chips = n // 2
    square = (HEADS, DIM, DIM)
    blocks = (HEADS, 2, DIM, DIM)
    thin = (HEADS, 2, HALF, DIM)
    quarter = (chips, DIM // 4, DIM)
    spread = (2, *quarter)
    noted = (DIM // 4 + 8, DIM)
    wide = HEADS * DIM
    deep = pltpu.VMEM((DIM, 2, wide), BF16)
    scratch = [
        deep, deep,
        full(*blocks), full(*blocks), pair(*square), pair(*square), full(*square),
        pair(*blocks), pair(*thin), full(HEADS, 2, DIM, 1), full(HEADS, 2, HALF, 1),
        pair(*blocks), full(*blocks), pair(*blocks), pair(*thin), pair(*blocks), full(*square), pair(HEADS, HALF, DIM),
        pair(*blocks), pair(*thin),
        full(chips, 96, DIM), full(chips, 96, DIM), full(chips, 2, HALF, DIM), pair(chips, DIM, DIM), full(*quarter), full(*quarter),
        full(*spread), pair(*square), full(HEADS, 2, HALF + 8, DIM), full(HEADS, HALF + 8, DIM), full(*square), full(*square),
        full(chips, *noted), full(chips, *noted), full(*quarter), full(*spread), full(ways, 8, DIM),
        pair(*blocks), pair(*blocks), full(*blocks), full(*blocks), full(*square),
    ]
    counts = [HEADS, chips, chips, chips, HEADS, HEADS, HEADS, chips, chips, HEADS, ways]
    sems = [dma(size) for size in counts for _ in range(2)] + [dma(chips), dma(HEADS), dma(2)]
    return pl.pallas_call(
        functools.partial(layer_kernel, n, ways),
        in_specs=[VMEM, FAR, FAR, VMEM, VMEM, VMEM],
        out_specs=[VMEM] * 4,
        out_shape=[
            shape(DIM, wide, dtype=BF16),
            shape(DIM, 2, wide, dtype=BF16),
            shape(DIM, 2, wide, dtype=BF16),
            shape(HEADS, 8, DIM),
        ],
        scratch_shapes=scratch + sems,
        compiler_params=pltpu.CompilerParams(collective_id=0, has_side_effects=True, vmem_limit_bytes=LIMIT),
    )(q, k, v, rate, cotan, gain)


def on_device(queries, keys, values, betas, grad_out, gain):
    n = lax.axis_size("outer") * lax.axis_size("inner")
    ways = lax.axis_size("dp")
    rate = betas[0].transpose(0, 2, 1).reshape(HEADS, 2, DIM)
    gq, gk, gv, total = layer(queries[0], keys[0], values[0], rate, grad_out[0], gain.reshape(HEADS, 1, DIM), n, ways)
    gain_grad = total[:, 0, :].reshape(HEADS * DIM) * (1.0 / math.sqrt(DIM * n * ways))
    return gq[None], gk[None], gv[None], gain_grad


def solution(mesh):
    seq = ("outer", "inner")
    return jax.shard_map(
        on_device,
        mesh=mesh,
        in_specs=(
            P("dp", seq, None),
            P("dp", seq, None, None),
            P("dp", seq, None, None),
            P("dp", None, None, seq),
            P("dp", seq, None),
            P(),
        ),
        out_specs=(P("dp", seq, None), P("dp", seq, None, None), P("dp", seq, None, None), P()),
        check_vma=False,
    )
```
